32 devices in a mesh: row: 8 (over y, x, core), col: 4 (over z).
Axes of the slice: x: 2, y: 2, z: 4, core: 2. Of those that a mesh axis runs over, the one named last changes fastest.
Arguments:
- features: bfloat16 [4096, 256], P(('row', 'col')), may hold values from -6 to 6
- degree: int32 [4096], P(('row', 'col')), may hold values from 1 to 128, as said below
- weight: bfloat16 [256, 256], replicated, may hold values from -0.375 to 0.375
- bias_vector: float32 [256], replicated, may hold values from -3 to 3
- cotangent: bfloat16 [4096, 256], P(('row', 'col')), may hold values from -6 to 6
- block_pos: int32 [8, 4, 16], P('row', 'col'), may hold values from 0 to 31
- edge_pos: int32 [8, 4, 16, 512], P('row', 'col'), may hold values from 0 to 16383
- block_count: int32 [8, 4], P('row', 'col'), may hold values from 2 to 16, as said below
Outputs:
- output: bfloat16 [4096, 256], P(('row', 'col'))
- grad_x: bfloat16 [4096, 256], P(('row', 'col'))
- grad_w: float32 [256, 256], replicated
- grad_b: float32 [256], replicated
The draws below stay inside these ranges and needn't reach their ends.
Inputs may be any that keep to these rules, and one draw needn't show every extreme that they name: `degree`: powers of two up to 64 times 1 or 2; some node has 128. `block_count`: slots from this number on are ignored; some device has 16 live slots.
All inputs are finite; a program needn't handle non-finite values.
Results may differ from the reference program's by a relative error of at most 0.008.
Values may be sent and summed in bfloat16 or wider, within the bound.
No kernel may reach another device: no remote copies, remote signals or barrier semaphores. Data moves between devices by JAX's collectives and lax.ppermute only.
A program may use at most 64 MiB of HBM per device.

```python
import jax
import jax.numpy as jnp
from jax import lax

F = 256
BLOCK = 128
ROWS_DEV = 128
BMAX = 16
EB = 512
NODES = 4096
RB = 4
CBK = 8
N_ROW = 8
N_COL = 4


def draw_degree(key, part):
    key_a, key_b, key_c = jax.random.split(key, 3)
    powers = jax.random.randint(key_a, (NODES,), 0, 7)
    factor = jax.random.randint(key_b, (NODES,), 1, 3)
    values = jnp.left_shift(jnp.ones((NODES,), jnp.int32), powers.astype(jnp.int32)) * factor.astype(jnp.int32)
    chosen = jax.random.randint(key_c, (), 0, NODES)
    return values.at[chosen].set(128).astype(jnp.int32)


def draw_block_count(key, part):
    key_a, key_b = jax.random.split(key)
    counts = jax.random.randint(key_a, (N_ROW * N_COL,), BMAX // 8, BMAX // 2 + 1)
    chosen = jax.random.randint(key_b, (), 0, N_ROW * N_COL)
    counts = counts.at[chosen].set(BMAX)
    return counts.reshape(N_ROW, N_COL).astype(jnp.int32)


def touch_ends(entries, key, low, largest):
    spot = [jax.random.randint(jax.random.fold_in(key, axis), (), 0, length) for axis, length in enumerate(entries.shape)]
    main_axis = entries.shape.index(max(entries.shape))
    neighbour = spot[:main_axis] + [(spot[main_axis] + 1) % entries.shape[main_axis]] + spot[main_axis + 1:]
    return entries.at[tuple(spot)].set(low).at[tuple(neighbour)].set(largest)


def block_levels(own_key, dims, shards, smallest, high):
    def one(dim, blocks):
        draws = jax.random.uniform(jax.random.fold_in(jax.random.fold_in(own_key, 6), dim), (blocks,), jnp.float32, smallest / len(shards), high / len(shards))
        return jnp.repeat(jnp.exp(draws), dims[dim] // blocks).reshape((-1,) + (1,) * (len(dims) - dim - 1))

    gain = one(*shards[0])
    for cut in shards[1:]:
        gain = gain * one(*cut)
    return gain


def normal_values(key, dims, spread, limit, shards=(), held_as=jnp.bfloat16):
    result = jax.random.normal(key, dims, jnp.float32) * spread
    if len(shards) > 0:
        result = block_levels(key, dims, shards, -0.22, 0.18) * result
    return jnp.clip(result, min=-limit, max=limit).astype(held_as)


def setup_inputs(seed: int = 0) -> dict:
    key_of = jax.random.split(jax.random.key(seed), 9)
    features = normal_values(key_of[0], (NODES, F), 1.0, 6.0, ((0, 32),))
    degree = draw_degree(jax.random.fold_in(key_of[8], 71), 0)
    weight = normal_values(key_of[2], (F, F), F ** -0.5, 0.375)
    bias_vector = normal_values(key_of[3], (F,), 0.5, 3.0, (), jnp.float32)
    cotangent = normal_values(key_of[4], (NODES, F), 1.0, 6.0, ((0, 32),))
    block_pos = touch_ends(jax.random.randint(key_of[5], (N_ROW, N_COL, BMAX), 0, RB * CBK), jax.random.fold_in(key_of[5], 1), 0, (RB * CBK) - 1).astype(jnp.int32)
    edge_pos = touch_ends(jax.random.randint(key_of[6], (N_ROW, N_COL, BMAX, EB), 0, BLOCK * BLOCK), jax.random.fold_in(key_of[6], 1), 0, (BLOCK * BLOCK) - 1).astype(jnp.int32)
    block_count = draw_block_count(jax.random.fold_in(key_of[8], 71), 0)
    return dict(features=features, degree=degree, weight=weight, bias_vector=bias_vector, cotangent=cotangent, block_pos=block_pos, edge_pos=edge_pos, block_count=block_count)


def build_blocks(positions, edge_list, live_count, row_blocks, col_blocks):
    flat_index = (jnp.arange(BMAX, dtype=jnp.int32)[:, None] * (BLOCK * BLOCK) + edge_list).reshape(-1)
    blocks = jnp.zeros((BMAX * BLOCK * BLOCK,), jnp.float32).at[flat_index].add(1.0)
    blocks = blocks.reshape(BMAX, BLOCK, BLOCK).astype(jnp.bfloat16)
    live_slots = jnp.arange(BMAX, dtype=jnp.int32) < live_count
    row_sel = positions // col_blocks
    col_sel = positions % col_blocks
    onehot_row = ((jnp.arange(row_blocks, dtype=jnp.int32)[:, None] == row_sel[None, :]) & live_slots[None, :]).astype(jnp.float32)
    onehot_col = ((jnp.arange(col_blocks, dtype=jnp.int32)[:, None] == col_sel[None, :]) & live_slots[None, :]).astype(jnp.float32)
    return (blocks, row_sel, col_sel, onehot_row, onehot_col)

def reference(features, degree, weight, bias_vector, cotangent, block_pos, edge_pos, block_count):
    inv_root = 1.0 / jnp.sqrt(degree.astype(jnp.float32))
    scaled = (features.astype(jnp.float32) * inv_root[:, None]).astype(jnp.bfloat16)
    by_owner = scaled.reshape(N_ROW, N_COL, ROWS_DEV, F)
    devices = jnp.arange(N_ROW * N_COL, dtype=jnp.int32)

    def forward_step(totals, device):
        row_index = device // N_COL
        col_index = device % N_COL
        blocks, row_sel, col_sel, onehot_row, onehot_col = build_blocks(block_pos[row_index, col_index], edge_pos[row_index, col_index], block_count[row_index, col_index], RB, CBK)
        gathered = by_owner[:, col_index].reshape(CBK, BLOCK, F)
        picked = gathered[col_sel]
        products = jnp.einsum('bmk,bkf->bmf', blocks.astype(jnp.float32), picked.astype(jnp.float32))
        partial_rows = jnp.einsum('rb,bmf->rmf', onehot_row, products, precision=lax.Precision.HIGHEST)
        totals = totals.at[row_index].add(partial_rows.reshape(RB * BLOCK, F))
        return (totals, None)
    start_rows = jnp.zeros((N_ROW, RB * BLOCK, F), jnp.float32)
    row_sums, _ = lax.scan(forward_step, start_rows, devices)
    agg = (row_sums.reshape(NODES, F) * inv_root[:, None]).astype(jnp.bfloat16)
    preact = jnp.dot(agg, weight, preferred_element_type=jnp.float32) + bias_vector
    output = jax.nn.silu(preact).astype(jnp.bfloat16)
    sig = jax.nn.sigmoid(preact)
    grad_pre = (cotangent.astype(jnp.float32) * sig * (1.0 + preact * (1.0 - sig))).astype(jnp.bfloat16)
    norm_scale = 1.0 / jnp.sqrt(jnp.float32(NODES))
    grad_w = jnp.dot(agg.T, grad_pre, preferred_element_type=jnp.float32) * norm_scale
    grad_b = lax.optimization_barrier(jnp.sum(grad_pre.astype(jnp.float32), axis=0)) * norm_scale
    grad_hidden = (jnp.dot(grad_pre, weight.T, preferred_element_type=jnp.float32) * inv_root[:, None]).astype(jnp.bfloat16)
    hidden_rows = grad_hidden.reshape(N_ROW, RB * BLOCK, F)

    def backward_step(totals, device):
        row_index = device // N_COL
        col_index = device % N_COL
        blocks, row_sel, col_sel, onehot_row, onehot_col = build_blocks(block_pos[row_index, col_index], edge_pos[row_index, col_index], block_count[row_index, col_index], RB, CBK)
        picked = hidden_rows[row_index].reshape(RB, BLOCK, F)[row_sel]
        products = jnp.einsum('bmk,bmf->bkf', blocks.astype(jnp.float32), picked.astype(jnp.float32))
        partial_cols = jnp.einsum('cb,bkf->ckf', onehot_col, products, precision=lax.Precision.HIGHEST)
        totals = totals.at[col_index].add(partial_cols.reshape(CBK * BLOCK, F))
        return (totals, None)
    start_cols = jnp.zeros((N_COL, CBK * BLOCK, F), jnp.float32)
    col_sums, _ = lax.scan(backward_step, start_cols, devices)
    col_sums = col_sums.reshape(N_COL, N_ROW, ROWS_DEV, F).transpose(1, 0, 2, 3).reshape(NODES, F)
    grad_x = (col_sums * inv_root[:, None]).astype(jnp.bfloat16)
    return (output, grad_x, grad_w, grad_b)
```

```python
import functools

import jax
import jax.numpy as jnp
from jax import lax
from jax.experimental import pallas as pl
from jax.experimental.pallas import tpu as pltpu
from jax.sharding import PartitionSpec as P

BLOCK = 128
CORES = 2
EXTRA = 16
VMEM = pl.BlockSpec(memory_space=pltpu.VMEM)
SMEM = pl.BlockSpec(memory_space=pltpu.SMEM)
NT = (((1,), (1,)), ((), ()))
TN = (((0,), (0,)), ((), ()))
BF16 = jnp.bfloat16
F32 = jnp.float32


def is_power(n):
    return n & (n - 1) == 0


def target(n, i, k):
    return i ^ k if is_power(n) else (i + k) % n


def offset_to(n, me, other):
    return me ^ other if is_power(n) else lax.rem(other - me + n, n)


def offset_from(n, me, other):
    return me ^ other if is_power(n) else lax.rem(me - other + n, n)


def to_core(x, rows):
    return lax.ppermute(x, "row", [(i, i ^ 1) for i in range(rows)])


def to_chip(x, rows, k):
    chips = rows // CORES
    pairs = [
        (a * CORES + b, target(chips, a, k) * CORES + b)
        for a in range(chips)
        for b in range(CORES)
    ]
    return lax.ppermute(x, "row", pairs)


def to_col(x, cols, k):
    return lax.ppermute(x, "col", [(i, target(cols, i, k)) for i in range(cols)])


def spread_inv(degree_ref, width):
    inv = lax.rsqrt(degree_ref[...].astype(F32))
    owned = inv.shape[1]
    tall = jnp.broadcast_to(inv, (BLOCK, owned)).T
    return jnp.concatenate([tall] * (width // BLOCK), axis=1)


def scale_kernel(features_ref, degree_ref, out_ref):
    inv = spread_inv(degree_ref, features_ref.shape[1])
    out_ref[...] = (features_ref[...].astype(F32) * inv).astype(BF16)


def for_live(count_ref, slots, body):
    count = count_ref[0, 0]

    def step(i, carry):
        body(i)
        return carry

    lax.fori_loop(0, count, step, 0)


def build_kernel(count_ref, edge_ref, blocks_ref):
    slots, edges = edge_ref.shape[2], edge_ref.shape[3]
    node = lax.broadcasted_iota(jnp.int32, (BLOCK, edges), 0)

    def build(s):
        edge = edge_ref[0, 0, pl.ds(s, 1), :]
        row_hot = jnp.where(node == edge // BLOCK, 1.0, 0.0).astype(BF16)
        col_hot = jnp.where(node == edge % BLOCK, 1.0, 0.0).astype(BF16)
        counts = lax.dot_general(row_hot, col_hot, NT, preferred_element_type=F32)
        blocks_ref[s] = counts.astype(BF16)

    for_live(count_ref, slots, build)


def forward_kernel(rows, cols, pos_ref, count_ref, blocks_ref, *refs):
    near = refs[: 2 * (rows // CORES)]
    own_ref, *send = refs[len(near) : len(near) + cols]
    gathered, acc = refs[len(near) + cols :]
    chips = rows // CORES
    row, col = lax.axis_index("row"), lax.axis_index("col")
    for n, ref in enumerate(near):
        gathered[n] = ref[...]
    acc[...] = jnp.zeros_like(acc)

    def add(s):
        p = pos_ref[0, 0, s]
        u, v = p // rows, lax.rem(p, rows)
        k = offset_from(chips, row // CORES, v // CORES)
        src = (lax.rem(v, CORES) ^ lax.rem(row, CORES)) * chips + k
        dst = offset_to(cols, col, u)
        acc[dst] += jnp.dot(blocks_ref[s], gathered[src], preferred_element_type=F32)

    for_live(count_ref, blocks_ref.shape[0], add)
    own_ref[...] = acc[0]
    for k, ref in enumerate(send, 1):
        ref[...] = acc[k].astype(BF16)


def pack_bias(total, rows):
    head = total.astype(BF16)
    tail = (total - head.astype(F32)).astype(BF16)
    index = lax.broadcasted_iota(jnp.int32, (rows, total.shape[1]), 0)
    both = jnp.where(index == 0, head.astype(F32), jnp.where(index == 1, tail.astype(F32), 0.0))
    return both.astype(BF16)


def add_bias(packed):
    return jnp.sum(packed.astype(F32), axis=0, keepdims=True)


def pointwise_kernel(cols, weight_ref, bias_ref, cot_ref, degree_ref, *refs):
    own_ref, *parts = refs[:cols]
    out_ref, hidden_ref, keep_ref, bias_keep_ref, send_ref = refs[cols:]
    width = out_ref.shape[1]
    half = width // CORES
    core = lax.rem(lax.axis_index("row"), CORES)
    inv = spread_inv(degree_ref, width)
    total = own_ref[...]
    for ref in parts:
        total = total + ref[...].astype(F32)
    agg = (total * inv).astype(BF16)
    weight = weight_ref[...]
    preact = jnp.dot(agg, weight, preferred_element_type=F32) + bias_ref[...]
    sig = jax.nn.sigmoid(preact)
    out_ref[...] = (preact * sig).astype(BF16)
    grad_pre = (cot_ref[...].astype(F32) * sig * (1.0 + preact * (1.0 - sig))).astype(BF16)
    hidden = lax.dot_general(grad_pre, weight, NT, preferred_element_type=F32)
    hidden_ref[...] = (hidden * inv).astype(BF16)
    term = lax.dot_general(agg, grad_pre, TN, preferred_element_type=F32)
    low, high = term[:half], term[half:]
    first = core == 0
    keep_ref[...] = jnp.where(first, low, high)
    send_ref[:half] = jnp.where(first, high, low).astype(BF16)
    bias_sum = jnp.sum(grad_pre.astype(F32), axis=0, keepdims=True)
    bias_keep_ref[...] = bias_sum
    send_ref[half:] = pack_bias(bias_sum, EXTRA)


def pair_sum_kernel(keep_ref, bias_keep_ref, got_ref, out_ref):
    half = keep_ref.shape[0]
    out_ref[:half] = (keep_ref[...] + got_ref[:half].astype(F32)).astype(BF16)
    out_ref[half:] = pack_bias(bias_keep_ref[...] + add_bias(got_ref[half:]), EXTRA)


def add_kernel(half, a_ref, b_ref, out_ref):
    out_ref[:half] = (a_ref[:half].astype(F32) + b_ref[:half].astype(F32)).astype(BF16)
    out_ref[half:] = pack_bias(add_bias(a_ref[half:]) + add_bias(b_ref[half:]), EXTRA)


def backward_kernel(rows, cols, pos_ref, count_ref, blocks_ref, *refs):
    hidden_parts = refs[:cols]
    keep_ref, send_ref, hidden, acc = refs[cols:]
    chips = rows // CORES
    row, col = lax.axis_index("row"), lax.axis_index("col")
    for n, ref in enumerate(hidden_parts):
        hidden[n] = ref[...]
    acc[...] = jnp.zeros_like(acc)

    def add(s):
        p = pos_ref[0, 0, s]
        u, v = p // rows, lax.rem(p, rows)
        src = offset_from(cols, col, u)
        k = offset_to(chips, row // CORES, v // CORES)
        dst = (lax.rem(v, CORES) ^ lax.rem(row, CORES)) * chips + k
        acc[dst] += lax.dot_general(blocks_ref[s], hidden[src], TN, preferred_element_type=F32)

    for_live(count_ref, blocks_ref.shape[0], add)
    keep_ref[...] = acc[:chips]
    send_ref[...] = acc[chips:].astype(BF16)


def merge_kernel(keep_ref, got_ref, grads_ref, own_ref, *send):
    own_ref[...] = keep_ref[0] + got_ref[0].astype(F32)
    for k, ref in enumerate(send, 1):
        ref[:BLOCK] = (keep_ref[k] + got_ref[k].astype(F32)).astype(BF16)
        ref[BLOCK:] = grads_ref[...]


def finish_kernel(chips, norm, degree_ref, own_ref, grads_ref, *refs):
    parts = refs[: chips - 1]
    grad_x_ref, half_ref, grad_b_ref = refs[chips - 1 :]
    half = half_ref.shape[0]
    total = own_ref[...]
    grads = grads_ref[:half].astype(F32)
    bias = add_bias(grads_ref[half:])
    for ref in parts:
        total = total + ref[:BLOCK].astype(F32)
        grads = grads + ref[BLOCK : BLOCK + half].astype(F32)
        bias = bias + add_bias(ref[BLOCK + half :])
    grad_x_ref[...] = (total * spread_inv(degree_ref, total.shape[1])).astype(BF16)
    half_ref[...] = grads * norm
    grad_b_ref[...] = bias * norm


def join_kernel(mine_ref, got_ref, out_ref):
    half = mine_ref.shape[0]
    first = lax.rem(lax.axis_index("row"), CORES) == 0
    out_ref[:half] = jnp.where(first, mine_ref[...], got_ref[...])
    out_ref[half:] = jnp.where(first, got_ref[...], mine_ref[...])


def call(kernel, specs, outs, scratch=(), flops=1_000_000):
    shapes = [jax.ShapeDtypeStruct(shape, dtype) for shape, dtype in outs]
    single = len(shapes) == 1
    return pl.pallas_call(
        kernel,
        out_shape=shapes[0] if single else tuple(shapes),
        in_specs=specs,
        out_specs=VMEM if single else tuple(VMEM for _ in shapes),
        scratch_shapes=[pltpu.VMEM(shape, dtype) for shape, dtype in scratch],
        compiler_params=pltpu.CompilerParams(vmem_limit_bytes=40 * 1024 * 1024),
        cost_estimate=pl.CostEstimate(flops=flops, bytes_accessed=1_000_000, transcendentals=0),
    )


def per_device(features, degree, weight, bias_vector, cotangent, block_pos, edge_pos, block_count):
    owned, width = features.shape
    rows, cols = lax.axis_size("row"), lax.axis_size("col")
    chips = rows // CORES
    slots = block_pos.shape[2]
    half = width // CORES
    piece = (owned, width)
    grads_shape = (half + EXTRA, width)
    degree = degree.reshape(1, owned)
    bias_vector = bias_vector.reshape(1, width)

    scaled = call(scale_kernel, [VMEM, VMEM], [(piece, BF16)])(features, degree)
    near = [scaled] + [to_chip(scaled, rows, k) for k in range(1, chips)]
    blocks = call(
        build_kernel, [SMEM, VMEM], [((slots, BLOCK, BLOCK), BF16)], flops=2_000_000_000
    )(block_count, edge_pos)
    near = near + [to_core(x, rows) for x in near]

    own, *send = call(
        functools.partial(forward_kernel, rows, cols),
        [SMEM, SMEM, VMEM] + [VMEM] * len(near),
        [(piece, F32)] + [(piece, BF16)] * (cols - 1),
        [((rows,) + piece, BF16), ((cols,) + piece, F32)],
    )(block_pos, block_count, blocks, *near)
    parts = [to_col(x, cols, k) for k, x in enumerate(send, 1)]

    output, hidden, keep, bias_keep, half_send = call(
        functools.partial(pointwise_kernel, cols),
        [VMEM] * (4 + cols),
        [(piece, BF16), (piece, BF16), ((half, width), F32), ((1, width), F32), (grads_shape, BF16)],
    )(weight, bias_vector, cotangent, degree, own, *parts)
    hidden_parts = [hidden] + [to_col(hidden, cols, k) for k in range(1, cols)]

    grads = call(pair_sum_kernel, [VMEM] * 3, [(grads_shape, BF16)])(
        keep, bias_keep, to_core(half_send, rows)
    )
    step = 1
    while step < cols:
        grads = call(functools.partial(add_kernel, half), [VMEM] * 2, [(grads_shape, BF16)])(
            grads, to_col(grads, cols, step)
        )
        step *= 2

    col_keep, col_send = call(
        functools.partial(backward_kernel, rows, cols),
        [SMEM, SMEM, VMEM] + [VMEM] * cols,
        [((chips,) + piece, F32), ((chips,) + piece, BF16)],
        [((cols,) + piece, BF16), ((rows,) + piece, F32)],
    )(block_pos, block_count, blocks, *hidden_parts)
    own_x, *send_x = call(
        merge_kernel,
        [VMEM] * 3,
        [(piece, F32)] + [((owned + half + EXTRA, width), BF16)] * (chips - 1),
    )(col_keep, to_core(col_send, rows), grads)
    parts_x = [to_chip(x, rows, k) for k, x in enumerate(send_x, 1)]

    norm = float((owned * rows * cols) ** -0.5)
    grad_x, mine, grad_b = call(
        functools.partial(finish_kernel, chips, norm),
        [VMEM] * (2 + chips),
        [(piece, BF16), ((half, width), F32), ((1, width), F32)],
    )(degree, own_x, grads, *parts_x)
    grad_w = call(join_kernel, [VMEM] * 2, [((width, width), F32)])(mine, to_core(mine, rows))
    return (output, grad_x, grad_w, grad_b.reshape(width))


def solution(mesh):
    placed = (
        P(("row", "col"), None),
        P(("row", "col")),
        P(),
        P(),
        P(("row", "col"), None),
        P("row", "col", None),
        P("row", "col", None, None),
        P("row", "col"),
    )
    return jax.shard_map(
        per_device,
        mesh=mesh,
        in_specs=placed,
        out_specs=(P(("row", "col"), None), P(("row", "col"), None), P(), P()),
        check_vma=False,
    )
```

```python
import functools

import jax
import jax.numpy as jnp
from jax import lax
from jax.experimental import pallas as pl
from jax.experimental.pallas import tpu as pltpu
from jax.sharding import PartitionSpec as P

BLOCK = 128
CORES = 2
EXTRA = 16
LONG = 4_000_000_000
VMEM = pl.BlockSpec(memory_space=pltpu.VMEM)
SMEM = pl.BlockSpec(memory_space=pltpu.SMEM)
NT = (((1,), (1,)), ((), ()))
TN = (((0,), (0,)), ((), ()))
BF16 = jnp.bfloat16
F32 = jnp.float32


def is_power(n):
    return n & (n - 1) == 0


def target(n, i, k):
    return i ^ k if is_power(n) else (i + k) % n


def offset_to(n, me, other):
    return me ^ other if is_power(n) else lax.rem(other - me + n, n)


def offset_from(n, me, other):
    return me ^ other if is_power(n) else lax.rem(me - other + n, n)


def to_core(x, rows):
    return lax.ppermute(x, "row", [(i, i ^ 1) for i in range(rows)])


def to_chip(x, rows, k):
    chips = rows // CORES
    pairs = [
        (a * CORES + b, target(chips, a, k) * CORES + b)
        for a in range(chips)
        for b in range(CORES)
    ]
    return lax.ppermute(x, "row", pairs)


def to_col(x, cols, k):
    return lax.ppermute(x, "col", [(i, target(cols, i, k)) for i in range(cols)])


def spread_inv(degree_ref, width):
    inv = lax.rsqrt(degree_ref[...].astype(F32))
    owned = inv.shape[1]
    tall = jnp.broadcast_to(inv, (BLOCK, owned)).T
    return jnp.concatenate([tall] * (width // BLOCK), axis=1)


def scale_kernel(features_hbm, degree_hbm, out_ref, features_ref, degree_ref, sems):
    copies = [
        pltpu.make_async_copy(degree_hbm, degree_ref, sems.at[0]),
        pltpu.make_async_copy(features_hbm, features_ref, sems.at[1]),
    ]
    for copy in copies:
        copy.start()
    copies[0].wait()
    inv = spread_inv(degree_ref, features_ref.shape[1])
    copies[1].wait()
    out_ref[...] = (features_ref[...].astype(F32) * inv).astype(BF16)


def for_live(count_ref, slots, body):
    count = count_ref[0, 0]

    def step(i, carry):
        body(i)
        return carry

    lax.fori_loop(0, count, step, 0)


def build_kernel(count_ref, edge_ref, bias_ref, blocks_ref, bias_out_ref):
    bias_out_ref[...] = bias_ref[...]
    slots, edges = edge_ref.shape[2], edge_ref.shape[3]
    node = lax.broadcasted_iota(jnp.int32, (BLOCK, edges), 0)

    def build(s):
        edge = edge_ref[0, 0, pl.ds(s, 1), :]
        row_hot = jnp.where(node == edge // BLOCK, 1.0, 0.0).astype(BF16)
        col_hot = jnp.where(node == edge % BLOCK, 1.0, 0.0).astype(BF16)
        counts = lax.dot_general(row_hot, col_hot, NT, preferred_element_type=F32)
        blocks_ref[s] = counts.astype(BF16)

    for_live(count_ref, slots, build)


def forward_kernel(rows, cols, pos_ref, count_ref, blocks_ref, *refs):
    near = refs[: 2 * (rows // CORES)]
    own_ref, *send = refs[len(near) : len(near) + cols]
    gathered, acc = refs[len(near) + cols :]
    chips = rows // CORES
    row, col = lax.axis_index("row"), lax.axis_index("col")
    for n, ref in enumerate(near):
        gathered[n] = ref[...]
    acc[...] = jnp.zeros_like(acc)

    def add(s):
        p = pos_ref[0, 0, s]
        u, v = p // rows, lax.rem(p, rows)
        k = offset_from(chips, row // CORES, v // CORES)
        src = (lax.rem(v, CORES) ^ lax.rem(row, CORES)) * chips + k
        dst = offset_to(cols, col, u)
        acc[dst] += jnp.dot(blocks_ref[s], gathered[src], preferred_element_type=F32)

    for_live(count_ref, blocks_ref.shape[0], add)
    own_ref[...] = acc[0]
    for k, ref in enumerate(send, 1):
        ref[...] = acc[k].astype(BF16)


def pack_bias(total, rows):
    head = total.astype(BF16)
    tail = (total - head.astype(F32)).astype(BF16)
    index = lax.broadcasted_iota(jnp.int32, (rows, total.shape[1]), 0)
    both = jnp.where(index == 0, head.astype(F32), jnp.where(index == 1, tail.astype(F32), 0.0))
    return both.astype(BF16)


def add_bias(packed):
    return jnp.sum(packed.astype(F32), axis=0, keepdims=True)


def pointwise_kernel(cols, weight_ref, bias_ref, cot_ref, degree_ref, *refs):
    own_ref, *parts = refs[:cols]
    out_ref, hidden_ref, keep_ref, bias_keep_ref, send_ref = refs[cols:]
    width = out_ref.shape[1]
    half = width // CORES
    core = lax.rem(lax.axis_index("row"), CORES)
    inv = spread_inv(degree_ref, width)
    total = own_ref[...]
    for ref in parts:
        total = total + ref[...].astype(F32)
    agg = (total * inv).astype(BF16)
    weight = weight_ref[...]
    preact = jnp.dot(agg, weight, preferred_element_type=F32) + bias_ref[...]
    sig = jax.nn.sigmoid(preact)
    out_ref[...] = (preact * sig).astype(BF16)
    grad_pre = (cot_ref[...].astype(F32) * sig * (1.0 + preact * (1.0 - sig))).astype(BF16)
    hidden = lax.dot_general(grad_pre, weight, NT, preferred_element_type=F32)
    hidden_ref[...] = (hidden * inv).astype(BF16)
    term = lax.dot_general(agg, grad_pre, TN, preferred_element_type=F32)
    low, high = term[:half], term[half:]
    first = core == 0
    keep_ref[...] = jnp.where(first, low, high)
    send_ref[:half] = jnp.where(first, high, low).astype(BF16)
    bias_sum = jnp.sum(grad_pre.astype(F32), axis=0, keepdims=True)
    bias_keep_ref[...] = bias_sum
    send_ref[half:] = pack_bias(bias_sum, EXTRA)


def pair_sum_kernel(keep_ref, bias_keep_ref, got_ref, hidden_ref, out_ref):
    owned, half = hidden_ref.shape[0], keep_ref.shape[0]
    out_ref[:owned] = hidden_ref[...]
    out_ref[owned : owned + half] = (keep_ref[...] + got_ref[:half].astype(F32)).astype(BF16)
    out_ref[owned + half :] = pack_bias(bias_keep_ref[...] + add_bias(got_ref[half:]), EXTRA)


def add_grads(half, a, b):
    total = (a[:half].astype(F32) + b[:half].astype(F32)).astype(BF16)
    return total, pack_bias(add_bias(a[half:]) + add_bias(b[half:]), EXTRA)


def add_kernel(half, a_ref, b_ref, out_ref):
    rows = half + EXTRA
    a, b = (ref[ref.shape[0] - rows :] for ref in (a_ref, b_ref))
    out_ref[:half], out_ref[half:] = add_grads(half, a, b)


def backward_kernel(rows, cols, pos_ref, count_ref, blocks_ref, *refs):
    hidden_parts = refs[:cols]
    keep_ref, send_ref, hidden, acc = refs[cols:]
    chips = rows // CORES
    row, col = lax.axis_index("row"), lax.axis_index("col")
    for n, ref in enumerate(hidden_parts):
        hidden[n] = ref[:BLOCK]
    acc[...] = jnp.zeros_like(acc)

    def add(s):
        p = pos_ref[0, 0, s]
        u, v = p // rows, lax.rem(p, rows)
        src = offset_from(cols, col, u)
        k = offset_to(chips, row // CORES, v // CORES)
        dst = (lax.rem(v, CORES) ^ lax.rem(row, CORES)) * chips + k
        acc[dst] += lax.dot_general(blocks_ref[s], hidden[src], TN, preferred_element_type=F32)

    for_live(count_ref, blocks_ref.shape[0], add)
    keep_ref[...] = acc[:chips]
    send_ref[...] = acc[chips:].astype(BF16)


def merge_kernel(keep_ref, got_ref, a_ref, b_ref, own_ref, grads_ref, *send):
    own_ref[...] = keep_ref[0] + got_ref[0].astype(F32)
    half = grads_ref.shape[0] - EXTRA
    total, bias = add_grads(half, a_ref[...], b_ref[...])
    grads_ref[:half] = total
    grads_ref[half:] = bias
    for k, ref in enumerate(send, 1):
        ref[:BLOCK] = (keep_ref[k] + got_ref[k].astype(F32)).astype(BF16)
        ref[BLOCK : BLOCK + half] = total
        ref[BLOCK + half :] = bias


def finish_grads_kernel(norm, grads_ref, *refs):
    *parts, half_ref, grad_b_ref = refs
    half = half_ref.shape[0]
    grads = grads_ref[:half].astype(F32)
    bias = add_bias(grads_ref[half:])
    for ref in parts:
        grads = grads + ref[BLOCK : BLOCK + half].astype(F32)
        bias = bias + add_bias(ref[BLOCK + half :])
    half_ref[...] = grads * norm
    grad_b_ref[...] = bias * norm


def finish_kernel(degree_ref, own_ref, *refs):
    *parts, grad_x_ref = refs
    total = own_ref[...]
    for ref in parts:
        total = total + ref[:BLOCK].astype(F32)
    grad_x_ref[...] = (total * spread_inv(degree_ref, total.shape[1])).astype(BF16)


def join_kernel(mine_ref, got_ref, out_ref):
    half = mine_ref.shape[0]
    first = lax.rem(lax.axis_index("row"), CORES) == 0
    out_ref[:half] = jnp.where(first, mine_ref[...], got_ref[...])
    out_ref[half:] = jnp.where(first, got_ref[...], mine_ref[...])


def call(kernel, specs, outs, scratch=(), flops=1_000_000):
    shapes = [jax.ShapeDtypeStruct(shape, dtype) for shape, dtype in outs]
    single = len(shapes) == 1
    return pl.pallas_call(
        kernel,
        out_shape=shapes[0] if single else tuple(shapes),
        in_specs=specs,
        out_specs=VMEM if single else tuple(VMEM for _ in shapes),
        scratch_shapes=[pltpu.VMEM(*s) if isinstance(s, tuple) else s for s in scratch],
        compiler_params=pltpu.CompilerParams(vmem_limit_bytes=40 * 1024 * 1024),
        cost_estimate=pl.CostEstimate(flops=flops, bytes_accessed=1_000_000, transcendentals=0),
    )


def per_device(features, degree, weight, bias_vector, cotangent, block_pos, edge_pos, block_count):
    owned, width = features.shape
    rows, cols = lax.axis_size("row"), lax.axis_size("col")
    chips = rows // CORES
    slots = block_pos.shape[2]
    half = width // CORES
    piece = (owned, width)
    grads_shape = (half + EXTRA, width)
    degree = degree.reshape(1, owned)
    bias_vector = bias_vector.reshape(1, width)

    scaled = call(
        scale_kernel,
        [pl.BlockSpec(memory_space=pltpu.HBM)] * 2,
        [(piece, BF16)],
        [(piece, BF16), ((1, owned), jnp.int32), pltpu.SemaphoreType.DMA((2,))],
    )(features, degree)
    near = [scaled] + [to_chip(scaled, rows, k) for k in range(1, chips)]
    blocks, bias_vector = call(
        build_kernel,
        [SMEM, VMEM, VMEM],
        [((slots, BLOCK, BLOCK), BF16), ((1, width), F32)],
        flops=LONG,
    )(block_count, edge_pos, bias_vector)
    blocks, *got = lax.optimization_barrier((blocks, *near[1:]))
    near = [scaled, *got]
    near = near + [to_core(x, rows) for x in near]

    own, *send = call(
        functools.partial(forward_kernel, rows, cols),
        [SMEM, SMEM, VMEM] + [VMEM] * len(near),
        [(piece, F32)] + [(piece, BF16)] * (cols - 1),
        [((rows,) + piece, BF16), ((cols,) + piece, F32)],
    )(block_pos, block_count, blocks, *near)
    order = list(range(2, cols)) + [1]
    parts = [to_col(send[k - 1], cols, k) for k in order]

    output, hidden, keep, bias_keep, half_send = call(
        functools.partial(pointwise_kernel, cols),
        [VMEM] * (4 + cols),
        [(piece, BF16), (piece, BF16), ((half, width), F32), ((1, width), F32), (grads_shape, BF16)],
    )(weight, bias_vector, cotangent, degree, own, *parts)

    half_got = to_core(half_send, rows)
    far = [to_col(hidden, cols, k) for k in range(2, cols)]
    message = call(
        pair_sum_kernel, [VMEM] * 4, [((owned + half + EXTRA, width), BF16)], flops=LONG
    )(keep, bias_keep, half_got, hidden)
    next_to = to_col(message, cols, 1)
    grads, other = message, next_to
    add = call(functools.partial(add_kernel, half), [VMEM] * 2, [(grads_shape, BF16)])
    step = 2
    while step < cols:
        grads = add(grads, other)
        other = to_col(grads, cols, step)
        step *= 2

    grads, next_to = lax.optimization_barrier((grads, next_to))
    col_keep, col_send = call(
        functools.partial(backward_kernel, rows, cols),
        [SMEM, SMEM, VMEM] + [VMEM] * cols,
        [((chips,) + piece, F32), ((chips,) + piece, BF16)],
        [((cols,) + piece, BF16), ((rows,) + piece, F32)],
        flops=LONG,
    )(block_pos, block_count, blocks, hidden, next_to, *far)
    own_x, grads, *send_x = call(
        merge_kernel,
        [VMEM] * 4,
        [(piece, F32), (grads_shape, BF16)]
        + [((owned + half + EXTRA, width), BF16)] * (chips - 1),
    )(col_keep, to_core(col_send, rows), grads, other)
    parts_x = [to_chip(x, rows, k) for k, x in enumerate(send_x, 1)]

    norm = float((owned * rows * cols) ** -0.5)
    mine, grad_b = call(
        functools.partial(finish_grads_kernel, norm),
        [VMEM] * chips,
        [((half, width), F32), ((1, width), F32)],
    )(grads, *parts_x)
    theirs = to_core(mine, rows)
    grad_x = call(finish_kernel, [VMEM] * (1 + chips), [(piece, BF16)])(degree, own_x, *parts_x)
    grad_w = call(join_kernel, [VMEM] * 2, [((width, width), F32)])(mine, theirs)
    return (output, grad_x, grad_w, grad_b.reshape(width))


def solution(mesh):
    placed = (
        P(("row", "col"), None),
        P(("row", "col")),
        P(),
        P(),
        P(("row", "col"), None),
        P("row", "col", None),
        P("row", "col", None, None),
        P("row", "col"),
    )
    return jax.shard_map(
        per_device,
        mesh=mesh,
        in_specs=placed,
        out_specs=(P(("row", "col"), None), P(("row", "col"), None), P(), P()),
        check_vma=False,
    )
```

```python
import functools

import jax
import jax.numpy as jnp
from jax import lax
from jax.experimental import pallas as pl
from jax.experimental.pallas import tpu as pltpu
from jax.sharding import PartitionSpec as P

BLOCK = 128
CORES = 2
EXTRA = 16
LONG = 4_000_000_000
VMEM = pl.BlockSpec(memory_space=pltpu.VMEM)
SMEM = pl.BlockSpec(memory_space=pltpu.SMEM)
NT = (((1,), (1,)), ((), ()))
TN = (((0,), (0,)), ((), ()))
BF16 = jnp.bfloat16
F32 = jnp.float32


def is_power(n):
    return n & (n - 1) == 0


def target(n, i, k):
    return i ^ k if is_power(n) else (i + k) % n


def offset_to(n, me, other):
    return me ^ other if is_power(n) else lax.rem(other - me + n, n)


def offset_from(n, me, other):
    return me ^ other if is_power(n) else lax.rem(me - other + n, n)


def to_core(x, rows):
    return lax.ppermute(x, "row", [(i, i ^ 1) for i in range(rows)])


def to_chip(x, rows, k):
    chips = rows // CORES
    pairs = [
        (a * CORES + b, target(chips, a, k) * CORES + b)
        for a in range(chips)
        for b in range(CORES)
    ]
    return lax.ppermute(x, "row", pairs)


def to_col(x, cols, k):
    return lax.ppermute(x, "col", [(i, target(cols, i, k)) for i in range(cols)])


def spread_inv(degree_ref, width):
    inv = lax.rsqrt(degree_ref[...].astype(F32))
    owned = inv.shape[1]
    tall = jnp.broadcast_to(inv, (BLOCK, owned)).T
    return jnp.concatenate([tall] * (width // BLOCK), axis=1)


def scale_kernel(features_hbm, degree_hbm, out_ref, features_ref, degree_ref, sems):
    copies = [
        pltpu.make_async_copy(degree_hbm, degree_ref, sems.at[0]),
        pltpu.make_async_copy(features_hbm, features_ref, sems.at[1]),
    ]
    for copy in copies:
        copy.start()
    copies[0].wait()
    inv = spread_inv(degree_ref, features_ref.shape[1])
    copies[1].wait()
    out_ref[...] = (features_ref[...].astype(F32) * inv).astype(BF16)


def for_live(count_ref, slots, body):
    count = count_ref[0, 0]

    def step(i, carry):
        body(i)
        return carry

    lax.fori_loop(0, count, step, 0)


def build_kernel(count_ref, edge_ref, blocks_ref):
    slots, edges = edge_ref.shape[2], edge_ref.shape[3]
    node = lax.broadcasted_iota(jnp.int32, (BLOCK, edges), 0)

    def build(s):
        edge = edge_ref[0, 0, pl.ds(s, 1), :]
        row_hot = jnp.where(node == edge // BLOCK, 1.0, 0.0).astype(BF16)
        col_hot = jnp.where(node == edge % BLOCK, 1.0, 0.0).astype(BF16)
        counts = lax.dot_general(row_hot, col_hot, NT, preferred_element_type=F32)
        blocks_ref[s] = counts.astype(BF16)

    for_live(count_ref, slots, build)


def forward_kernel(rows, cols, pos_ref, count_ref, bias_ref, blocks_ref, *refs):
    near = refs[: 2 * (rows // CORES)]
    bias_out_ref, own_ref, *send, gathered, acc = refs[len(near) :]
    bias_out_ref[...] = bias_ref[...]
    chips = rows // CORES
    row, col = lax.axis_index("row"), lax.axis_index("col")
    for n, ref in enumerate(near):
        gathered[n] = ref[...]
    acc[...] = jnp.zeros_like(acc)

    def add(s):
        p = pos_ref[0, 0, s]
        u, v = p // rows, lax.rem(p, rows)
        k = offset_from(chips, row // CORES, v // CORES)
        src = (lax.rem(v, CORES) ^ lax.rem(row, CORES)) * chips + k
        dst = offset_to(cols, col, u)
        acc[dst] += jnp.dot(blocks_ref[s], gathered[src], preferred_element_type=F32)

    for_live(count_ref, blocks_ref.shape[0], add)
    own_ref[...] = acc[0]
    for k, ref in enumerate(send, 1):
        ref[...] = acc[k].astype(BF16)


def pack_bias(total, rows):
    head = total.astype(BF16)
    tail = (total - head.astype(F32)).astype(BF16)
    index = lax.broadcasted_iota(jnp.int32, (rows, total.shape[1]), 0)
    both = jnp.where(index == 0, head.astype(F32), jnp.where(index == 1, tail.astype(F32), 0.0))
    return both.astype(BF16)


def add_bias(packed):
    return jnp.sum(packed.astype(F32), axis=0, keepdims=True)


def pointwise_kernel(cols, weight_ref, bias_ref, cot_ref, degree_ref, *refs):
    own_ref, *parts = refs[:cols]
    out_ref, hidden_ref, keep_ref, bias_keep_ref, send_ref = refs[cols:]
    width = out_ref.shape[1]
    half = width // CORES
    core = lax.rem(lax.axis_index("row"), CORES)
    inv = spread_inv(degree_ref, width)
    total = own_ref[...]
    for ref in parts:
        total = total + ref[...].astype(F32)
    agg = (total * inv).astype(BF16)
    weight = weight_ref[...]
    preact = jnp.dot(agg, weight, preferred_element_type=F32) + bias_ref[...]
    sig = jax.nn.sigmoid(preact)
    out_ref[...] = (preact * sig).astype(BF16)
    grad_pre = (cot_ref[...].astype(F32) * sig * (1.0 + preact * (1.0 - sig))).astype(BF16)
    hidden = lax.dot_general(grad_pre, weight, NT, preferred_element_type=F32)
    hidden_ref[...] = (hidden * inv).astype(BF16)
    term = lax.dot_general(agg, grad_pre, TN, preferred_element_type=F32)
    low, high = term[:half], term[half:]
    first = core == 0
    keep_ref[...] = jnp.where(first, low, high)
    send_ref[:half] = jnp.where(first, high, low).astype(BF16)
    bias_sum = jnp.sum(grad_pre.astype(F32), axis=0, keepdims=True)
    bias_keep_ref[...] = bias_sum
    send_ref[half:] = pack_bias(bias_sum, EXTRA)


def pair_sum_kernel(keep_ref, bias_keep_ref, got_ref, hidden_ref, out_ref):
    owned, half = hidden_ref.shape[0], keep_ref.shape[0]
    out_ref[:owned] = hidden_ref[...]
    out_ref[owned : owned + half] = (keep_ref[...] + got_ref[:half].astype(F32)).astype(BF16)
    out_ref[owned + half :] = pack_bias(bias_keep_ref[...] + add_bias(got_ref[half:]), EXTRA)


def add_grads(half, a, b):
    total = (a[:half].astype(F32) + b[:half].astype(F32)).astype(BF16)
    return total, pack_bias(add_bias(a[half:]) + add_bias(b[half:]), EXTRA)


def add_kernel(half, a_ref, b_ref, out_ref):
    rows = half + EXTRA
    a, b = (ref[ref.shape[0] - rows :] for ref in (a_ref, b_ref))
    out_ref[:half], out_ref[half:] = add_grads(half, a, b)


def backward_kernel(rows, cols, pos_ref, count_ref, blocks_ref, *refs):
    hidden_parts = refs[:cols]
    keep_ref, send_ref, hidden, acc = refs[cols:]
    chips = rows // CORES
    row, col = lax.axis_index("row"), lax.axis_index("col")
    for n, ref in enumerate(hidden_parts):
        hidden[n] = ref[:BLOCK]
    acc[...] = jnp.zeros_like(acc)

    def add(s):
        p = pos_ref[0, 0, s]
        u, v = p // rows, lax.rem(p, rows)
        src = offset_from(cols, col, u)
        k = offset_to(chips, row // CORES, v // CORES)
        dst = (lax.rem(v, CORES) ^ lax.rem(row, CORES)) * chips + k
        acc[dst] += lax.dot_general(blocks_ref[s], hidden[src], TN, preferred_element_type=F32)

    for_live(count_ref, blocks_ref.shape[0], add)
    keep_ref[...] = acc[:chips]
    send_ref[...] = acc[chips:].astype(BF16)


def merge_kernel(keep_ref, got_ref, a_ref, b_ref, own_ref, grads_ref, *send):
    own_ref[...] = keep_ref[0] + got_ref[0].astype(F32)
    half = grads_ref.shape[0] - EXTRA
    total, bias = add_grads(half, a_ref[...], b_ref[...])
    grads_ref[:half] = total
    grads_ref[half:] = bias
    for k, ref in enumerate(send, 1):
        ref[:BLOCK] = (keep_ref[k] + got_ref[k].astype(F32)).astype(BF16)
        ref[BLOCK : BLOCK + half] = total
        ref[BLOCK + half :] = bias


def finish_grads_kernel(norm, grads_ref, *refs):
    *parts, half_ref, grad_b_ref = refs
    half = half_ref.shape[0]
    grads = grads_ref[:half].astype(F32)
    bias = add_bias(grads_ref[half:])
    for ref in parts:
        grads = grads + ref[BLOCK : BLOCK + half].astype(F32)
        bias = bias + add_bias(ref[BLOCK + half :])
    half_ref[...] = grads * norm
    grad_b_ref[...] = bias * norm


def finish_kernel(degree_ref, own_ref, *refs):
    *parts, grad_x_ref = refs
    total = own_ref[...]
    for ref in parts:
        total = total + ref[:BLOCK].astype(F32)
    grad_x_ref[...] = (total * spread_inv(degree_ref, total.shape[1])).astype(BF16)


def join_kernel(mine_ref, got_ref, out_ref):
    half = mine_ref.shape[0]
    first = lax.rem(lax.axis_index("row"), CORES) == 0
    out_ref[:half] = jnp.where(first, mine_ref[...], got_ref[...])
    out_ref[half:] = jnp.where(first, got_ref[...], mine_ref[...])


def call(kernel, specs, outs, scratch=(), flops=1_000_000):
    shapes = [jax.ShapeDtypeStruct(shape, dtype) for shape, dtype in outs]
    single = len(shapes) == 1
    return pl.pallas_call(
        kernel,
        out_shape=shapes[0] if single else tuple(shapes),
        in_specs=specs,
        out_specs=VMEM if single else tuple(VMEM for _ in shapes),
        scratch_shapes=[pltpu.VMEM(*s) if isinstance(s, tuple) else s for s in scratch],
        compiler_params=pltpu.CompilerParams(vmem_limit_bytes=40 * 1024 * 1024),
        cost_estimate=pl.CostEstimate(flops=flops, bytes_accessed=1_000_000, transcendentals=0),
    )


def per_device(features, degree, weight, bias_vector, cotangent, block_pos, edge_pos, block_count):
    owned, width = features.shape
    rows, cols = lax.axis_size("row"), lax.axis_size("col")
    chips = rows // CORES
    slots = block_pos.shape[2]
    half = width // CORES
    piece = (owned, width)
    grads_shape = (half + EXTRA, width)
    degree = degree.reshape(1, owned)
    bias_vector = bias_vector.reshape(1, width)

    scaled = call(
        scale_kernel,
        [pl.BlockSpec(memory_space=pltpu.HBM)] * 2,
        [(piece, BF16)],
        [(piece, BF16), ((1, owned), jnp.int32), pltpu.SemaphoreType.DMA((2,))],
    )(features, degree)
    near = [scaled] + [to_chip(scaled, rows, k) for k in range(1, chips)]
    blocks = call(build_kernel, [SMEM, VMEM], [((slots, BLOCK, BLOCK), BF16)], flops=LONG)(
        block_count, edge_pos
    )
    blocks, *got = lax.optimization_barrier((blocks, *near[1:]))
    near = [scaled, *got]
    near = near + [to_core(x, rows) for x in near]

    bias_vector, own, *send = call(
        functools.partial(forward_kernel, rows, cols),
        [SMEM, SMEM, VMEM, VMEM] + [VMEM] * len(near),
        [((1, width), F32), (piece, F32)] + [(piece, BF16)] * (cols - 1),
        [((rows,) + piece, BF16), ((cols,) + piece, F32)],
    )(block_pos, block_count, bias_vector, blocks, *near)
    order = list(range(2, cols)) + [1]
    parts = [to_col(send[k - 1], cols, k) for k in order]

    output, hidden, keep, bias_keep, half_send = call(
        functools.partial(pointwise_kernel, cols),
        [VMEM] * (4 + cols),
        [(piece, BF16), (piece, BF16), ((half, width), F32), ((1, width), F32), (grads_shape, BF16)],
    )(weight, bias_vector, cotangent, degree, own, *parts)

    half_got = to_core(half_send, rows)
    far = [to_col(hidden, cols, k) for k in range(2, cols)]
    message = call(
        pair_sum_kernel, [VMEM] * 4, [((owned + half + EXTRA, width), BF16)], flops=LONG
    )(keep, bias_keep, half_got, hidden)
    next_to = to_col(message, cols, 1)
    grads, other = message, next_to
    add = call(functools.partial(add_kernel, half), [VMEM] * 2, [(grads_shape, BF16)])
    step = 2
    while step < cols:
        grads = add(grads, other)
        other = to_col(grads, cols, step)
        step *= 2

    col_keep, col_send = call(
        functools.partial(backward_kernel, rows, cols),
        [SMEM, SMEM, VMEM] + [VMEM] * cols,
        [((chips,) + piece, F32), ((chips,) + piece, BF16)],
        [((cols,) + piece, BF16), ((rows,) + piece, F32)],
        flops=LONG,
    )(block_pos, block_count, blocks, hidden, next_to, *far)
    col_send, other = lax.optimization_barrier((col_send, other))
    own_x, grads, *send_x = call(
        merge_kernel,
        [VMEM] * 4,
        [(piece, F32), (grads_shape, BF16)]
        + [((owned + half + EXTRA, width), BF16)] * (chips - 1),
    )(col_keep, to_core(col_send, rows), grads, other)
    parts_x = [to_chip(x, rows, k) for k, x in enumerate(send_x, 1)]

    norm = float((owned * rows * cols) ** -0.5)
    mine, grad_b = call(
        functools.partial(finish_grads_kernel, norm),
        [VMEM] * chips,
        [((half, width), F32), ((1, width), F32)],
    )(grads, *parts_x)
    theirs = to_core(mine, rows)
    grad_x = call(finish_kernel, [VMEM] * (1 + chips), [(piece, BF16)])(degree, own_x, *parts_x)
    grad_w = call(join_kernel, [VMEM] * 2, [((width, width), F32)])(mine, theirs)
    return (output, grad_x, grad_w, grad_b.reshape(width))


def solution(mesh):
    placed = (
        P(("row", "col"), None),
        P(("row", "col")),
        P(),
        P(),
        P(("row", "col"), None),
        P("row", "col", None),
        P("row", "col", None, None),
        P("row", "col"),
    )
    return jax.shard_map(
        per_device,
        mesh=mesh,
        in_specs=placed,
        out_specs=(P(("row", "col"), None), P(("row", "col"), None), P(), P()),
        check_vma=False,
    )
```

```python
import functools

import jax
import jax.numpy as jnp
from jax import lax
from jax.experimental import pallas as pl
from jax.experimental.pallas import tpu as pltpu
from jax.sharding import PartitionSpec as P

BLOCK = 128
CORES = 2
EXTRA = 16
LONG = 4_000_000_000
GROUP = 4
VMEM = pl.BlockSpec(memory_space=pltpu.VMEM)
SMEM = pl.BlockSpec(memory_space=pltpu.SMEM)
NT = (((1,), (1,)), ((), ()))
TN = (((0,), (0,)), ((), ()))
BF16 = jnp.bfloat16
F32 = jnp.float32


def is_power(n):
    return n & (n - 1) == 0


def target(n, i, k):
    return i ^ k if is_power(n) else (i + k) % n


def offset_to(n, me, other):
    return me ^ other if is_power(n) else lax.rem(other - me + n, n)


def offset_from(n, me, other):
    return me ^ other if is_power(n) else lax.rem(me - other + n, n)


def to_core(x, rows):
    return lax.ppermute(x, "row", [(i, i ^ 1) for i in range(rows)])


def to_chip(x, rows, k):
    chips = rows // CORES
    pairs = [
        (a * CORES + b, target(chips, a, k) * CORES + b)
        for a in range(chips)
        for b in range(CORES)
    ]
    return lax.ppermute(x, "row", pairs)


def to_col(x, cols, k):
    return lax.ppermute(x, "col", [(i, target(cols, i, k)) for i in range(cols)])


def spread_inv(degree_ref, width):
    inv = lax.rsqrt(degree_ref[...].astype(F32))
    owned = inv.shape[1]
    tall = jnp.broadcast_to(inv, (BLOCK, owned)).T
    return jnp.concatenate([tall] * (width // BLOCK), axis=1)


def scale_kernel(features_ref, degree_ref, out_ref, inv_ref):
    inv = spread_inv(degree_ref, features_ref.shape[1])
    inv_ref[...] = inv
    out_ref[...] = (features_ref[...].astype(F32) * inv).astype(BF16)


def for_live(count_ref, slots, body):
    count = count_ref[0, 0]
    group = GROUP if slots % GROUP == 0 else 1

    def step(i, carry):
        for j in range(group):
            slot = i * group + j
            body(slot, slot < count)
        return carry

    lax.fori_loop(0, (count + group - 1) // group, step, 0)


def build_kernel(count_ref, edge_ref, blocks_ref, turned_ref):
    slots, edges = edge_ref.shape[2], edge_ref.shape[3]
    node = lax.broadcasted_iota(jnp.int32, (BLOCK, edges), 0)

    def build(s, live):
        edge = edge_ref[0, 0, pl.ds(s, 1), :]
        row_hot = jnp.where(node == edge // BLOCK, 1.0, 0.0).astype(BF16)
        col_hot = jnp.where(node == edge % BLOCK, 1.0, 0.0).astype(BF16)
        counts = lax.dot_general(row_hot, col_hot, NT, preferred_element_type=F32)
        block = jnp.where(live, counts, 0.0).astype(BF16)
        blocks_ref[s] = block
        turned_ref[s] = block.T

    for_live(count_ref, slots, build)


def forward_kernel(rows, cols, pos_ref, count_ref, bias_ref, blocks_ref, *refs):
    near = refs[: 2 * (rows // CORES)]
    bias_out_ref, own_ref, *send, gathered, acc = refs[len(near) :]
    bias_out_ref[...] = bias_ref[...]
    chips = rows // CORES
    row, col = lax.axis_index("row"), lax.axis_index("col")
    for n, ref in enumerate(near):
        gathered[n] = ref[...]
    acc[...] = jnp.zeros_like(acc)

    def add(s, live):
        p = pos_ref[0, 0, s]
        u, v = p // rows, lax.rem(p, rows)
        k = offset_from(chips, row // CORES, v // CORES)
        src = (lax.rem(v, CORES) ^ lax.rem(row, CORES)) * chips + k
        dst = offset_to(cols, col, u)
        acc[dst] += jnp.dot(blocks_ref[s], gathered[src], preferred_element_type=F32)

    for_live(count_ref, blocks_ref.shape[0], add)
    own_ref[...] = acc[0]
    for k, ref in enumerate(send, 1):
        ref[...] = acc[k].astype(BF16)


def pack_bias(total, rows):
    head = total.astype(BF16)
    tail = (total - head.astype(F32)).astype(BF16)
    index = lax.broadcasted_iota(jnp.int32, (rows, total.shape[1]), 0)
    both = jnp.where(index == 0, head.astype(F32), jnp.where(index == 1, tail.astype(F32), 0.0))
    return both.astype(BF16)


def add_bias(packed):
    return jnp.sum(packed.astype(F32), axis=0, keepdims=True)


def pointwise_kernel(cols, weight_ref, bias_ref, cot_ref, inv_ref, *refs):
    own_ref, *parts = refs[:cols]
    out_ref, hidden_ref, keep_ref, bias_keep_ref, send_ref = refs[cols:]
    width = out_ref.shape[1]
    half = width // CORES
    core = lax.rem(lax.axis_index("row"), CORES)
    inv = inv_ref[...]
    total = own_ref[...]
    for ref in parts:
        total = total + ref[...].astype(F32)
    agg = (total * inv).astype(BF16)
    weight = weight_ref[...]
    preact = jnp.dot(agg, weight, preferred_element_type=F32) + bias_ref[...]
    sig = jax.nn.sigmoid(preact)
    out_ref[...] = (preact * sig).astype(BF16)
    grad_pre = (cot_ref[...].astype(F32) * sig * (1.0 + preact * (1.0 - sig))).astype(BF16)
    hidden = lax.dot_general(grad_pre, weight, NT, preferred_element_type=F32)
    hidden_ref[...] = (hidden * inv).astype(BF16)
    term = lax.dot_general(agg, grad_pre, TN, preferred_element_type=F32)
    low, high = term[:half], term[half:]
    first = core == 0
    keep_ref[...] = jnp.where(first, low, high)
    send_ref[:half] = jnp.where(first, high, low).astype(BF16)
    bias_sum = jnp.sum(grad_pre.astype(F32), axis=0, keepdims=True)
    bias_keep_ref[...] = bias_sum
    send_ref[half:] = pack_bias(bias_sum, EXTRA)


def pair_sum_kernel(keep_ref, bias_keep_ref, got_ref, hidden_ref, out_ref):
    owned, half = hidden_ref.shape[0], keep_ref.shape[0]
    out_ref[:owned] = hidden_ref[...]
    out_ref[owned : owned + half] = (keep_ref[...] + got_ref[:half].astype(F32)).astype(BF16)
    out_ref[owned + half :] = pack_bias(bias_keep_ref[...] + add_bias(got_ref[half:]), EXTRA)


def add_grads(half, a, b):
    total = (a[:half].astype(F32) + b[:half].astype(F32)).astype(BF16)
    return total, pack_bias(add_bias(a[half:]) + add_bias(b[half:]), EXTRA)


def add_kernel(half, a_ref, b_ref, out_ref):
    rows = half + EXTRA
    a, b = (ref[ref.shape[0] - rows :] for ref in (a_ref, b_ref))
    out_ref[:half], out_ref[half:] = add_grads(half, a, b)


def backward_kernel(rows, cols, pos_ref, count_ref, turned_ref, *refs):
    hidden_parts = refs[:cols]
    keep_ref, send_ref, hidden, acc = refs[cols:]
    chips = rows // CORES
    row, col = lax.axis_index("row"), lax.axis_index("col")
    for n, ref in enumerate(hidden_parts):
        hidden[n] = ref[:BLOCK]
    acc[...] = jnp.zeros_like(acc)

    def add(s, live):
        p = pos_ref[0, 0, s]
        u, v = p // rows, lax.rem(p, rows)
        src = offset_from(cols, col, u)
        k = offset_to(chips, row // CORES, v // CORES)
        dst = (lax.rem(v, CORES) ^ lax.rem(row, CORES)) * chips + k
        acc[dst] += jnp.dot(turned_ref[s], hidden[src], preferred_element_type=F32)

    for_live(count_ref, turned_ref.shape[0], add)
    keep_ref[...] = acc[:chips]
    send_ref[...] = acc[chips:].astype(BF16)


def merge_kernel(keep_ref, got_ref, a_ref, b_ref, own_ref, grads_ref, *send):
    own_ref[...] = keep_ref[0] + got_ref[0].astype(F32)
    half = grads_ref.shape[0] - EXTRA
    total, bias = add_grads(half, a_ref[...], b_ref[...])
    grads_ref[:half] = total
    grads_ref[half:] = bias
    for k, ref in enumerate(send, 1):
        ref[:BLOCK] = (keep_ref[k] + got_ref[k].astype(F32)).astype(BF16)
        ref[BLOCK : BLOCK + half] = total
        ref[BLOCK + half :] = bias


def sum_grads_kernel(grads_ref, *refs):
    *parts, half_ref, bias_ref = refs
    half = half_ref.shape[0]
    grads = grads_ref[:half].astype(F32)
    bias = add_bias(grads_ref[half:])
    for ref in parts:
        grads = grads + ref[BLOCK : BLOCK + half].astype(F32)
        bias = bias + add_bias(ref[BLOCK + half :])
    half_ref[...] = grads
    bias_ref[...] = bias


def finish_kernel(norm, out_ref, inv_ref, own_ref, mine_ref, theirs_ref, bias_ref, *refs):
    *parts, output_ref, grad_x_ref, grad_w_ref, grad_b_ref = refs
    output_ref[...] = out_ref[...]
    total = own_ref[...]
    for ref in parts:
        total = total + ref[:BLOCK].astype(F32)
    grad_x_ref[...] = (total * inv_ref[...]).astype(BF16)
    half = mine_ref.shape[0]
    first = lax.rem(lax.axis_index("row"), CORES) == 0
    mine, theirs = mine_ref[...] * norm, theirs_ref[...] * norm
    grad_w_ref[:half] = jnp.where(first, mine, theirs)
    grad_w_ref[half:] = jnp.where(first, theirs, mine)
    grad_b_ref[...] = bias_ref[...] * norm


def call(kernel, specs, outs, scratch=(), flops=1_000_000):
    shapes = [jax.ShapeDtypeStruct(shape, dtype) for shape, dtype in outs]
    single = len(shapes) == 1
    return pl.pallas_call(
        kernel,
        out_shape=shapes[0] if single else tuple(shapes),
        in_specs=specs,
        out_specs=VMEM if single else tuple(VMEM for _ in shapes),
        scratch_shapes=[pltpu.VMEM(*s) for s in scratch],
        compiler_params=pltpu.CompilerParams(vmem_limit_bytes=40 * 1024 * 1024),
        cost_estimate=pl.CostEstimate(flops=flops, bytes_accessed=1_000_000, transcendentals=0),
    )


def per_device(features, degree, weight, bias_vector, cotangent, block_pos, edge_pos, block_count):
    owned, width = features.shape
    rows, cols = lax.axis_size("row"), lax.axis_size("col")
    chips = rows // CORES
    slots = block_pos.shape[2]
    half = width // CORES
    piece = (owned, width)
    grads_shape = (half + EXTRA, width)
    degree = degree.reshape(1, owned)
    bias_vector = bias_vector.reshape(1, width)

    scaled, inv = call(scale_kernel, [VMEM, VMEM], [(piece, BF16), (piece, F32)])(features, degree)
    near = [scaled] + [to_chip(scaled, rows, k) for k in range(1, chips)]
    blocks, turned = call(
        build_kernel, [SMEM, VMEM], [((slots, BLOCK, BLOCK), BF16)] * 2, flops=LONG
    )(block_count, edge_pos)
    blocks, *got = lax.optimization_barrier((blocks, *near[1:]))
    near = [scaled, *got]
    near = near + [to_core(x, rows) for x in near]

    bias_vector, own, *send = call(
        functools.partial(forward_kernel, rows, cols),
        [SMEM, SMEM, VMEM, VMEM] + [VMEM] * len(near),
        [((1, width), F32), (piece, F32)] + [(piece, BF16)] * (cols - 1),
        [((rows,) + piece, BF16), ((cols,) + piece, F32)],
    )(block_pos, block_count, bias_vector, blocks, *near)
    order = list(range(2, cols)) + [1]
    parts = [to_col(send[k - 1], cols, k) for k in order]

    out_piece, hidden, keep, bias_keep, half_send = call(
        functools.partial(pointwise_kernel, cols),
        [VMEM] * (4 + cols),
        [(piece, BF16), (piece, BF16), ((half, width), F32), ((1, width), F32), (grads_shape, BF16)],
    )(weight, bias_vector, cotangent, inv, own, *parts)

    half_got = to_core(half_send, rows)
    far = [to_col(hidden, cols, k) for k in range(2, cols)]
    message = call(
        pair_sum_kernel, [VMEM] * 4, [((owned + half + EXTRA, width), BF16)], flops=LONG
    )(keep, bias_keep, half_got, hidden)
    next_to = to_col(message, cols, 1)
    grads, other = message, next_to
    add = call(functools.partial(add_kernel, half), [VMEM] * 2, [(grads_shape, BF16)])
    step = 2
    while step < cols:
        grads = add(grads, other)
        other = to_col(grads, cols, step)
        step *= 2

    col_keep, col_send = call(
        functools.partial(backward_kernel, rows, cols),
        [SMEM, SMEM, VMEM] + [VMEM] * cols,
        [((chips,) + piece, F32), ((chips,) + piece, BF16)],
        [((cols,) + piece, BF16), ((rows,) + piece, F32)],
        flops=LONG,
    )(block_pos, block_count, turned, hidden, next_to, *far)
    col_send, other = lax.optimization_barrier((col_send, other))
    own_x, grads, *send_x = call(
        merge_kernel,
        [VMEM] * 4,
        [(piece, F32), (grads_shape, BF16)]
        + [((owned + half + EXTRA, width), BF16)] * (chips - 1),
    )(col_keep, to_core(col_send, rows), grads, other)
    parts_x = [to_chip(x, rows, k) for k, x in enumerate(send_x, 1)]

    mine, bias_sum = call(
        sum_grads_kernel, [VMEM] * chips, [((half, width), F32), ((1, width), F32)]
    )(grads, *parts_x)
    theirs = to_core(mine, rows)
    norm = float((owned * rows * cols) ** -0.5)
    output, grad_x, grad_w, grad_b = call(
        functools.partial(finish_kernel, norm),
        [VMEM] * (5 + chips),
        [(piece, BF16), (piece, BF16), ((width, width), F32), ((1, width), F32)],
    )(out_piece, inv, own_x, mine, theirs, bias_sum, *parts_x)
    return (output, grad_x, grad_w, grad_b.reshape(width))


def solution(mesh):
    placed = (
        P(("row", "col"), None),
        P(("row", "col")),
        P(),
        P(),
        P(("row", "col"), None),
        P("row", "col", None),
        P("row", "col", None, None),
        P("row", "col"),
    )
    return jax.shard_map(
        per_device,
        mesh=mesh,
        in_specs=placed,
        out_specs=(P(("row", "col"), None), P(("row", "col"), None), P(), P()),
        check_vma=False,
    )
```

```python
import functools

import jax
import jax.numpy as jnp
from jax import lax
from jax.experimental import pallas as pl
from jax.experimental.pallas import tpu as pltpu
from jax.sharding import PartitionSpec as P

BLOCK = 128
CORES = 2
EXTRA = 16
LONG = 4_000_000_000
GROUP = 4
VMEM = pl.BlockSpec(memory_space=pltpu.VMEM)
SMEM = pl.BlockSpec(memory_space=pltpu.SMEM)
NT = (((1,), (1,)), ((), ()))
TN = (((0,), (0,)), ((), ()))
BF16 = jnp.bfloat16
F32 = jnp.float32


def is_power(n):
    return n & (n - 1) == 0


def target(n, i, k):
    return i ^ k if is_power(n) else (i + k) % n


def offset_to(n, me, other):
    return me ^ other if is_power(n) else lax.rem(other - me + n, n)


def offset_from(n, me, other):
    return me ^ other if is_power(n) else lax.rem(me - other + n, n)


def to_core(x, rows):
    return lax.ppermute(x, "row", [(i, i ^ 1) for i in range(rows)])


def to_chip(x, rows, k):
    chips = rows // CORES
    pairs = [
        (a * CORES + b, target(chips, a, k) * CORES + b)
        for a in range(chips)
        for b in range(CORES)
    ]
    return lax.ppermute(x, "row", pairs)


def to_col(x, cols, k):
    return lax.ppermute(x, "col", [(i, target(cols, i, k)) for i in range(cols)])


def spread_inv(degree_ref, width):
    inv = lax.rsqrt(degree_ref[...].astype(F32))
    owned = inv.shape[1]
    tall = jnp.broadcast_to(inv, (BLOCK, owned)).T
    return jnp.concatenate([tall] * (width // BLOCK), axis=1)


def scale_kernel(features_ref, degree_ref, out_ref, inv_ref):
    inv = spread_inv(degree_ref, features_ref.shape[1])
    inv_ref[...] = inv
    out_ref[...] = (features_ref[...].astype(F32) * inv).astype(BF16)


def for_live(count_ref, slots, body):
    count = count_ref[0, 0]
    group = GROUP if slots % GROUP == 0 else 1

    def step(i, carry):
        for j in range(group):
            slot = i * group + j
            body(slot, slot < count)
        return carry

    lax.fori_loop(0, (count + group - 1) // group, step, 0)


def build_kernel(count_ref, edge_ref, blocks_ref, turned_ref):
    slots, edges = edge_ref.shape[2], edge_ref.shape[3]
    node = lax.broadcasted_iota(jnp.int32, (BLOCK, edges), 0)

    def build(s, live):
        edge = edge_ref[0, 0, pl.ds(s, 1), :]
        row_hot = jnp.where(node == edge // BLOCK, 1.0, 0.0).astype(BF16)
        col_hot = jnp.where(node == edge % BLOCK, 1.0, 0.0).astype(BF16)
        counts = lax.dot_general(row_hot, col_hot, NT, preferred_element_type=F32)
        block = jnp.where(live, counts, 0.0).astype(BF16)
        blocks_ref[s] = block
        turned_ref[s] = block.T

    for_live(count_ref, slots, build)


def forward_kernel(rows, cols, pos_ref, count_ref, bias_ref, blocks_ref, *refs):
    near = refs[: 2 * (rows // CORES)]
    bias_out_ref, own_ref, *send, gathered, acc = refs[len(near) :]
    bias_out_ref[...] = bias_ref[...]
    chips = rows // CORES
    row, col = lax.axis_index("row"), lax.axis_index("col")
    for n, ref in enumerate(near):
        gathered[n] = ref[...]
    acc[...] = jnp.zeros_like(acc)

    def add(s, live):
        p = pos_ref[0, 0, s]
        u, v = p // rows, lax.rem(p, rows)
        k = offset_from(chips, row // CORES, v // CORES)
        src = (lax.rem(v, CORES) ^ lax.rem(row, CORES)) * chips + k
        dst = offset_to(cols, col, u)
        acc[dst] += jnp.dot(blocks_ref[s], gathered[src], preferred_element_type=F32)

    for_live(count_ref, blocks_ref.shape[0], add)
    own_ref[...] = acc[0]
    for k, ref in enumerate(send, 1):
        ref[...] = acc[k].astype(BF16)


def pack_bias(total, rows):
    head = total.astype(BF16)
    tail = (total - head.astype(F32)).astype(BF16)
    index = lax.broadcasted_iota(jnp.int32, (rows, total.shape[1]), 0)
    both = jnp.where(index == 0, head.astype(F32), jnp.where(index == 1, tail.astype(F32), 0.0))
    return both.astype(BF16)


def add_bias(packed):
    return jnp.sum(packed.astype(F32), axis=0, keepdims=True)


def pointwise_kernel(cols, weight_ref, bias_ref, cot_ref, inv_ref, *refs):
    own_ref, *parts = refs[:cols]
    out_ref, hidden_ref, keep_ref, bias_keep_ref, send_ref = refs[cols:]
    width = out_ref.shape[1]
    half = width // CORES
    core = lax.rem(lax.axis_index("row"), CORES)
    inv = inv_ref[...]
    total = own_ref[...]
    for ref in parts:
        total = total + ref[...].astype(F32)
    agg = (total * inv).astype(BF16)
    weight = weight_ref[...]
    preact = jnp.dot(agg, weight, preferred_element_type=F32) + bias_ref[...]
    sig = jax.nn.sigmoid(preact)
    out_ref[...] = (preact * sig).astype(BF16)
    grad_pre = (cot_ref[...].astype(F32) * sig * (1.0 + preact * (1.0 - sig))).astype(BF16)
    hidden = lax.dot_general(grad_pre, weight, NT, preferred_element_type=F32)
    hidden_ref[...] = (hidden * inv).astype(BF16)
    term = lax.dot_general(agg, grad_pre, TN, preferred_element_type=F32)
    low, high = term[:half], term[half:]
    first = core == 0
    keep_ref[...] = jnp.where(first, low, high)
    send_ref[:half] = jnp.where(first, high, low).astype(BF16)
    bias_sum = jnp.sum(grad_pre.astype(F32), axis=0, keepdims=True)
    bias_keep_ref[...] = bias_sum
    send_ref[half:] = pack_bias(bias_sum, EXTRA)


def pair_sum_kernel(keep_ref, bias_keep_ref, got_ref, hidden_ref, out_ref):
    owned, half = hidden_ref.shape[0], keep_ref.shape[0]
    out_ref[:owned] = hidden_ref[...]
    out_ref[owned : owned + half] = (keep_ref[...] + got_ref[:half].astype(F32)).astype(BF16)
    out_ref[owned + half :] = pack_bias(bias_keep_ref[...] + add_bias(got_ref[half:]), EXTRA)


def add_grads(half, a, b):
    total = (a[:half].astype(F32) + b[:half].astype(F32)).astype(BF16)
    return total, pack_bias(add_bias(a[half:]) + add_bias(b[half:]), EXTRA)


def add_kernel(half, a_ref, b_ref, out_ref):
    rows = half + EXTRA
    a, b = (ref[ref.shape[0] - rows :] for ref in (a_ref, b_ref))
    out_ref[:half], out_ref[half:] = add_grads(half, a, b)


def collect_kernel(*refs):
    *parts, out_ref = refs
    for n, ref in enumerate(parts):
        out_ref[n] = ref[...]


def backward_kernel(
    rows, cols, pos_ref, count_ref, turned_ref, own_ref, next_ref, far_ref, keep_ref, send_ref, hidden, acc
):
    chips = rows // CORES
    row, col = lax.axis_index("row"), lax.axis_index("col")
    hidden[0] = own_ref[...]
    hidden[1] = next_ref[:BLOCK]
    hidden[2:] = far_ref[...]
    acc[...] = jnp.zeros_like(acc)

    def add(s, live):
        p = pos_ref[0, 0, s]
        u, v = p // rows, lax.rem(p, rows)
        src = offset_from(cols, col, u)
        k = offset_to(chips, row // CORES, v // CORES)
        dst = (lax.rem(v, CORES) ^ lax.rem(row, CORES)) * chips + k
        acc[dst] += jnp.dot(turned_ref[s], hidden[src], preferred_element_type=F32)

    for_live(count_ref, turned_ref.shape[0], add)
    keep_ref[...] = acc[:chips]
    send_ref[...] = acc[chips:].astype(BF16)


def merge_kernel(keep_ref, got_ref, grads_ref, own_ref, *send):
    own_ref[...] = keep_ref[0] + got_ref[0].astype(F32)
    for k, ref in enumerate(send, 1):
        ref[:BLOCK] = (keep_ref[k] + got_ref[k].astype(F32)).astype(BF16)
        ref[BLOCK:] = grads_ref[...]


def sum_grads_kernel(grads_ref, *refs):
    *parts, half_ref, bias_ref = refs
    half = half_ref.shape[0]
    grads = grads_ref[:half].astype(F32)
    bias = add_bias(grads_ref[half:])
    for ref in parts:
        grads = grads + ref[BLOCK : BLOCK + half].astype(F32)
        bias = bias + add_bias(ref[BLOCK + half :])
    half_ref[...] = grads
    bias_ref[...] = bias


def finish_kernel(norm, out_ref, inv_ref, own_ref, mine_ref, theirs_ref, bias_ref, *refs):
    *parts, output_ref, grad_x_ref, grad_w_ref, grad_b_ref = refs
    output_ref[...] = out_ref[...]
    total = own_ref[...]
    for ref in parts:
        total = total + ref[:BLOCK].astype(F32)
    grad_x_ref[...] = (total * inv_ref[...]).astype(BF16)
    half = mine_ref.shape[0]
    first = lax.rem(lax.axis_index("row"), CORES) == 0
    mine, theirs = mine_ref[...] * norm, theirs_ref[...] * norm
    grad_w_ref[:half] = jnp.where(first, mine, theirs)
    grad_w_ref[half:] = jnp.where(first, theirs, mine)
    grad_b_ref[...] = bias_ref[...] * norm


def call(kernel, specs, outs, scratch=(), flops=1_000_000):
    shapes = [jax.ShapeDtypeStruct(shape, dtype) for shape, dtype in outs]
    single = len(shapes) == 1
    return pl.pallas_call(
        kernel,
        out_shape=shapes[0] if single else tuple(shapes),
        in_specs=specs,
        out_specs=VMEM if single else tuple(VMEM for _ in shapes),
        scratch_shapes=[pltpu.VMEM(*s) for s in scratch],
        compiler_params=pltpu.CompilerParams(vmem_limit_bytes=40 * 1024 * 1024),
        cost_estimate=pl.CostEstimate(flops=flops, bytes_accessed=1_000_000, transcendentals=0),
    )


def per_device(features, degree, weight, bias_vector, cotangent, block_pos, edge_pos, block_count):
    owned, width = features.shape
    rows, cols = lax.axis_size("row"), lax.axis_size("col")
    chips = rows // CORES
    slots = block_pos.shape[2]
    half = width // CORES
    piece = (owned, width)
    grads_shape = (half + EXTRA, width)
    degree = degree.reshape(1, owned)
    bias_vector = bias_vector.reshape(1, width)

    scaled, inv = call(scale_kernel, [VMEM, VMEM], [(piece, BF16), (piece, F32)])(features, degree)
    near = [scaled] + [to_chip(scaled, rows, k) for k in range(1, chips)]
    blocks, turned = call(
        build_kernel, [SMEM, VMEM], [((slots, BLOCK, BLOCK), BF16)] * 2, flops=LONG
    )(block_count, edge_pos)
    blocks, *got = lax.optimization_barrier((blocks, *near[1:]))
    near = [scaled, *got]
    near = near + [to_core(x, rows) for x in near]

    bias_vector, own, *send = call(
        functools.partial(forward_kernel, rows, cols),
        [SMEM, SMEM, VMEM, VMEM] + [VMEM] * len(near),
        [((1, width), F32), (piece, F32)] + [(piece, BF16)] * (cols - 1),
        [((rows,) + piece, BF16), ((cols,) + piece, F32)],
    )(block_pos, block_count, bias_vector, blocks, *near)
    order = list(range(2, cols)) + [1]
    parts = [to_col(send[k - 1], cols, k) for k in order]

    out_piece, hidden, keep, bias_keep, half_send = call(
        functools.partial(pointwise_kernel, cols),
        [VMEM] * (4 + cols),
        [(piece, BF16), (piece, BF16), ((half, width), F32), ((1, width), F32), (grads_shape, BF16)],
    )(weight, bias_vector, cotangent, inv, own, *parts)

    half_got = to_core(half_send, rows)
    far = [to_col(hidden, cols, k) for k in range(2, cols)]
    message = call(
        pair_sum_kernel, [VMEM] * 4, [((owned + half + EXTRA, width), BF16)], flops=LONG
    )(keep, bias_keep, half_got, hidden)
    next_to = to_col(message, cols, 1)
    far = call(collect_kernel, [VMEM] * len(far), [((cols - 2,) + piece, BF16)], flops=LONG)(*far)
    far, other = lax.optimization_barrier((far, next_to))
    next_to, grads = other, message
    add = call(functools.partial(add_kernel, half), [VMEM] * 2, [(grads_shape, BF16)], flops=LONG)
    step = 2
    while step < cols:
        grads = add(grads, other)
        other = to_col(grads, cols, step)
        step *= 2

    col_keep, col_send = call(
        functools.partial(backward_kernel, rows, cols),
        [SMEM, SMEM] + [VMEM] * 4,
        [((chips,) + piece, F32), ((chips,) + piece, BF16)],
        [((cols,) + piece, BF16), ((rows,) + piece, F32)],
        flops=LONG,
    )(block_pos, block_count, turned, hidden, next_to, far)
    grads = add(grads, other)
    own_x, *send_x = call(
        merge_kernel,
        [VMEM] * 3,
        [(piece, F32)] + [((owned + half + EXTRA, width), BF16)] * (chips - 1),
    )(col_keep, to_core(col_send, rows), grads)
    parts_x = [to_chip(send_x[k - 1], rows, k) for k in range(chips - 1, 0, -1)]

    mine, bias_sum = call(
        sum_grads_kernel, [VMEM] * chips, [((half, width), F32), ((1, width), F32)]
    )(grads, *parts_x)
    theirs = to_core(mine, rows)
    norm = float((owned * rows * cols) ** -0.5)
    output, grad_x, grad_w, grad_b = call(
        functools.partial(finish_kernel, norm),
        [VMEM] * (5 + chips),
        [(piece, BF16), (piece, BF16), ((width, width), F32), ((1, width), F32)],
    )(out_piece, inv, own_x, mine, theirs, bias_sum, *parts_x)
    return (output, grad_x, grad_w, grad_b.reshape(width))


def solution(mesh):
    placed = (
        P(("row", "col"), None),
        P(("row", "col")),
        P(),
        P(),
        P(("row", "col"), None),
        P("row", "col", None),
        P("row", "col", None, None),
        P("row", "col"),
    )
    return jax.shard_map(
        per_device,
        mesh=mesh,
        in_specs=placed,
        out_specs=(P(("row", "col"), None), P(("row", "col"), None), P(), P()),
        check_vma=False,
    )
```

```python
import functools

import jax
import jax.numpy as jnp
from jax import lax
from jax.experimental import pallas as pl
from jax.experimental.pallas import tpu as pltpu
from jax.sharding import PartitionSpec as P

BLOCK = 128
CORES = 2
EXTRA = 16
LONG = 4_000_000_000
GROUP = 4
VMEM = pl.BlockSpec(memory_space=pltpu.VMEM)
SMEM = pl.BlockSpec(memory_space=pltpu.SMEM)
NT = (((1,), (1,)), ((), ()))
TN = (((0,), (0,)), ((), ()))
BF16 = jnp.bfloat16
F32 = jnp.float32


def is_power(n):
    return n & (n - 1) == 0


def target(n, i, k):
    return i ^ k if is_power(n) else (i + k) % n


def offset_to(n, me, other):
    return me ^ other if is_power(n) else lax.rem(other - me + n, n)


def offset_from(n, me, other):
    return me ^ other if is_power(n) else lax.rem(me - other + n, n)


def to_core(x, rows):
    return lax.ppermute(x, "row", [(i, i ^ 1) for i in range(rows)])


def to_chip(x, rows, k):
    chips = rows // CORES
    pairs = [
        (a * CORES + b, target(chips, a, k) * CORES + b)
        for a in range(chips)
        for b in range(CORES)
    ]
    return lax.ppermute(x, "row", pairs)


def to_col(x, cols, k):
    return lax.ppermute(x, "col", [(i, target(cols, i, k)) for i in range(cols)])


def spread_inv(degree_ref, width):
    inv = lax.rsqrt(degree_ref[...].astype(F32))
    owned = inv.shape[1]
    tall = jnp.broadcast_to(inv, (BLOCK, owned)).T
    return jnp.concatenate([tall] * (width // BLOCK), axis=1)


def scale_kernel(features_ref, degree_ref, out_ref, inv_ref):
    inv = spread_inv(degree_ref, features_ref.shape[1])
    inv_ref[...] = inv
    out_ref[...] = (features_ref[...].astype(F32) * inv).astype(BF16)


def for_live(count_ref, slots, body):
    count = count_ref[0, 0]
    group = GROUP if slots % GROUP == 0 else 1

    def step(i, carry):
        for j in range(group):
            slot = i * group + j
            body(slot, slot < count)
        return carry

    lax.fori_loop(0, (count + group - 1) // group, step, 0)


def build_kernel(count_ref, edge_ref, bias_ref, blocks_ref, turned_ref, bias_out_ref):
    bias_out_ref[...] = bias_ref[...]
    slots, edges = edge_ref.shape[2], edge_ref.shape[3]
    node = lax.broadcasted_iota(jnp.int32, (BLOCK, edges), 0)

    def build(s, live):
        edge = edge_ref[0, 0, pl.ds(s, 1), :]
        row_hot = jnp.where(node == edge // BLOCK, 1.0, 0.0).astype(BF16)
        col_hot = jnp.where(node == edge % BLOCK, 1.0, 0.0).astype(BF16)
        counts = lax.dot_general(row_hot, col_hot, NT, preferred_element_type=F32)
        block = jnp.where(live, counts, 0.0).astype(BF16)
        blocks_ref[s] = block
        turned_ref[s] = block.T

    for_live(count_ref, slots, build)


def forward_kernel(rows, cols, pos_hold_ref, count_ref, blocks_ref, near_ref, next_ref, *refs):
    own_ref, *send, gathered, acc, pos_ref, sem = refs
    fetch = pltpu.make_async_copy(pos_hold_ref, pos_ref, sem)
    fetch.start()
    chips = rows // CORES
    row, col = lax.axis_index("row"), lax.axis_index("col")
    gathered[:chips] = near_ref[...]
    gathered[chips:] = next_ref[...]
    acc[...] = jnp.zeros_like(acc)
    fetch.wait()

    def add(s, live):
        p = pos_ref[0, 0, s]
        u, v = p // rows, lax.rem(p, rows)
        k = offset_from(chips, row // CORES, v // CORES)
        src = (lax.rem(v, CORES) ^ lax.rem(row, CORES)) * chips + k
        dst = offset_to(cols, col, u)
        acc[dst] += jnp.dot(blocks_ref[s], gathered[src], preferred_element_type=F32)

    for_live(count_ref, blocks_ref.shape[0], add)
    own_ref[...] = acc[0]
    for k, ref in enumerate(send, 1):
        ref[...] = acc[k].astype(BF16)


def pack_bias(total, rows):
    head = total.astype(BF16)
    tail = (total - head.astype(F32)).astype(BF16)
    index = lax.broadcasted_iota(jnp.int32, (rows, total.shape[1]), 0)
    both = jnp.where(index == 0, head.astype(F32), jnp.where(index == 1, tail.astype(F32), 0.0))
    return both.astype(BF16)


def add_bias(packed):
    return jnp.sum(packed.astype(F32), axis=0, keepdims=True)


def pointwise_kernel(cols, weight_ref, bias_ref, cot_ref, inv_ref, *refs):
    own_ref, *parts = refs[:cols]
    out_ref, hidden_ref, keep_ref, bias_keep_ref, send_ref = refs[cols:]
    width = out_ref.shape[1]
    half = width // CORES
    core = lax.rem(lax.axis_index("row"), CORES)
    inv = inv_ref[...]
    total = own_ref[...]
    for ref in parts:
        total = total + ref[...].astype(F32)
    agg = (total * inv).astype(BF16)
    weight = weight_ref[...]
    preact = jnp.dot(agg, weight, preferred_element_type=F32) + bias_ref[...]
    sig = jax.nn.sigmoid(preact)
    out_ref[...] = (preact * sig).astype(BF16)
    grad_pre = (cot_ref[...].astype(F32) * sig * (1.0 + preact * (1.0 - sig))).astype(BF16)
    hidden = lax.dot_general(grad_pre, weight, NT, preferred_element_type=F32)
    hidden_ref[...] = (hidden * inv).astype(BF16)
    term = lax.dot_general(agg, grad_pre, TN, preferred_element_type=F32)
    low, high = term[:half], term[half:]
    first = core == 0
    keep_ref[...] = jnp.where(first, low, high)
    send_ref[:half] = jnp.where(first, high, low).astype(BF16)
    bias_sum = jnp.sum(grad_pre.astype(F32), axis=0, keepdims=True)
    bias_keep_ref[...] = bias_sum
    send_ref[half:] = pack_bias(bias_sum, EXTRA)


def pair_sum_kernel(keep_ref, bias_keep_ref, got_ref, hidden_ref, out_ref):
    owned, half = hidden_ref.shape[0], keep_ref.shape[0]
    out_ref[:owned] = hidden_ref[...]
    out_ref[owned : owned + half] = (keep_ref[...] + got_ref[:half].astype(F32)).astype(BF16)
    out_ref[owned + half :] = pack_bias(bias_keep_ref[...] + add_bias(got_ref[half:]), EXTRA)


def add_grads(half, a, b):
    total = (a[:half].astype(F32) + b[:half].astype(F32)).astype(BF16)
    return total, pack_bias(add_bias(a[half:]) + add_bias(b[half:]), EXTRA)


def add_kernel(half, a_ref, b_ref, out_ref):
    rows = half + EXTRA
    a, b = (ref[ref.shape[0] - rows :] for ref in (a_ref, b_ref))
    out_ref[:half], out_ref[half:] = add_grads(half, a, b)


def collect_kernel(*refs):
    *parts, out_ref = refs
    for n, ref in enumerate(parts):
        out_ref[n] = ref[...]


def backward_kernel(rows, cols, pos_hold_ref, count_ref, turned_ref, *refs):
    own_ref, next_ref, far_ref, keep_ref, send_ref, hidden, acc, pos_ref, sem = refs
    fetch = pltpu.make_async_copy(pos_hold_ref, pos_ref, sem)
    fetch.start()
    chips = rows // CORES
    row, col = lax.axis_index("row"), lax.axis_index("col")
    hidden[0] = own_ref[...]
    hidden[1] = next_ref[:BLOCK]
    hidden[2:] = far_ref[...]
    acc[...] = jnp.zeros_like(acc)
    fetch.wait()

    def add(s, live):
        p = pos_ref[0, 0, s]
        u, v = p // rows, lax.rem(p, rows)
        src = offset_from(cols, col, u)
        k = offset_to(chips, row // CORES, v // CORES)
        dst = (lax.rem(v, CORES) ^ lax.rem(row, CORES)) * chips + k
        acc[dst] += jnp.dot(turned_ref[s], hidden[src], preferred_element_type=F32)

    for_live(count_ref, turned_ref.shape[0], add)
    keep_ref[...] = acc[:chips]
    send_ref[...] = acc[chips:].astype(BF16)


def merge_kernel(keep_ref, got_ref, grads_ref, own_ref, *send):
    own_ref[...] = keep_ref[0] + got_ref[0].astype(F32)
    for k, ref in enumerate(send, 1):
        ref[:BLOCK] = (keep_ref[k] + got_ref[k].astype(F32)).astype(BF16)
        ref[BLOCK:] = grads_ref[...]


def sum_grads_kernel(grads_ref, *refs):
    *parts, half_ref, bias_ref = refs
    half = half_ref.shape[0]
    grads = grads_ref[:half].astype(F32)
    bias = add_bias(grads_ref[half:])
    for ref in parts:
        grads = grads + ref[BLOCK : BLOCK + half].astype(F32)
        bias = bias + add_bias(ref[BLOCK + half :])
    half_ref[...] = grads
    bias_ref[...] = bias


def finish_kernel(norm, out_ref, inv_ref, own_ref, mine_ref, theirs_ref, bias_ref, *refs):
    *parts, output_ref, grad_x_ref, grad_w_ref, grad_b_ref = refs
    output_ref[...] = out_ref[...]
    total = own_ref[...]
    for ref in parts:
        total = total + ref[:BLOCK].astype(F32)
    grad_x_ref[...] = (total * inv_ref[...]).astype(BF16)
    half = mine_ref.shape[0]
    first = lax.rem(lax.axis_index("row"), CORES) == 0
    mine, theirs = mine_ref[...] * norm, theirs_ref[...] * norm
    grad_w_ref[:half] = jnp.where(first, mine, theirs)
    grad_w_ref[half:] = jnp.where(first, theirs, mine)
    grad_b_ref[...] = bias_ref[...] * norm


def call(kernel, specs, outs, scratch=(), flops=1_000_000):
    shapes = [jax.ShapeDtypeStruct(shape, dtype) for shape, dtype in outs]
    single = len(shapes) == 1
    return pl.pallas_call(
        kernel,
        out_shape=shapes[0] if single else tuple(shapes),
        in_specs=specs,
        out_specs=VMEM if single else tuple(VMEM for _ in shapes),
        scratch_shapes=scratch,
        compiler_params=pltpu.CompilerParams(vmem_limit_bytes=40 * 1024 * 1024),
        cost_estimate=pl.CostEstimate(flops=flops, bytes_accessed=1_000_000, transcendentals=0),
    )


def per_device(features, degree, weight, bias_vector, cotangent, block_pos, edge_pos, block_count):
    owned, width = features.shape
    rows, cols = lax.axis_size("row"), lax.axis_size("col")
    chips = rows // CORES
    slots = block_pos.shape[2]
    half = width // CORES
    piece = (owned, width)
    grads_shape = (half + EXTRA, width)
    degree = degree.reshape(1, owned)
    bias_vector = bias_vector.reshape(1, width)

    scaled, inv = call(scale_kernel, [VMEM, VMEM], [(piece, BF16), (piece, F32)])(features, degree)
    near = [to_chip(scaled, rows, k) for k in range(1, chips)]
    blocks, turned, bias_vector = call(
        build_kernel,
        [SMEM, VMEM, VMEM],
        [((slots, BLOCK, BLOCK), BF16)] * 2 + [((1, width), F32)],
        flops=LONG,
    )(block_count, edge_pos, bias_vector)
    blocks, *near = lax.optimization_barrier((blocks, *near))
    near = call(collect_kernel, [VMEM] * chips, [((chips,) + piece, BF16)])(scaled, *near)

    fetched = [pltpu.SMEM(block_pos.shape, jnp.int32), pltpu.SemaphoreType.DMA]
    own, *send = call(
        functools.partial(forward_kernel, rows, cols),
        [VMEM, SMEM, VMEM, VMEM, VMEM],
        [(piece, F32)] + [(piece, BF16)] * (cols - 1),
        [pltpu.VMEM((rows,) + piece, BF16), pltpu.VMEM((cols,) + piece, F32), *fetched],
    )(block_pos, block_count, blocks, near, to_core(near, rows))
    order = list(range(2, cols)) + [1]
    parts = [to_col(send[k - 1], cols, k) for k in order]

    out_piece, hidden, keep, bias_keep, half_send = call(
        functools.partial(pointwise_kernel, cols),
        [VMEM] * (4 + cols),
        [(piece, BF16), (piece, BF16), ((half, width), F32), ((1, width), F32), (grads_shape, BF16)],
    )(weight, bias_vector, cotangent, inv, own, *parts)

    half_got = to_core(half_send, rows)
    far = [to_col(hidden, cols, k) for k in range(2, cols)]
    message = call(
        pair_sum_kernel, [VMEM] * 4, [((owned + half + EXTRA, width), BF16)], flops=LONG
    )(keep, bias_keep, half_got, hidden)
    next_to = to_col(message, cols, 1)
    far = call(collect_kernel, [VMEM] * len(far), [((cols - 2,) + piece, BF16)], flops=LONG)(*far)
    far, other = lax.optimization_barrier((far, next_to))
    next_to, grads = other, message
    add = call(functools.partial(add_kernel, half), [VMEM] * 2, [(grads_shape, BF16)], flops=LONG)
    step = 2
    while step < cols:
        grads = add(grads, other)
        other = to_col(grads, cols, step)
        step *= 2

    col_keep, col_send = call(
        functools.partial(backward_kernel, rows, cols),
        [VMEM, SMEM] + [VMEM] * 4,
        [((chips,) + piece, F32), ((chips,) + piece, BF16)],
        [pltpu.VMEM((cols,) + piece, BF16), pltpu.VMEM((rows,) + piece, F32), *fetched],
        flops=LONG,
    )(block_pos, block_count, turned, hidden, next_to, far)
    grads = add(grads, other)
    own_x, *send_x = call(
        merge_kernel,
        [VMEM] * 3,
        [(piece, F32)] + [((owned + half + EXTRA, width), BF16)] * (chips - 1),
    )(col_keep, to_core(col_send, rows), grads)
    parts_x = [to_chip(send_x[k - 1], rows, k) for k in range(chips - 1, 0, -1)]

    mine, bias_sum = call(
        sum_grads_kernel, [VMEM] * chips, [((half, width), F32), ((1, width), F32)]
    )(grads, *parts_x)
    theirs = to_core(mine, rows)
    norm = float((owned * rows * cols) ** -0.5)
    output, grad_x, grad_w, grad_b = call(
        functools.partial(finish_kernel, norm),
        [VMEM] * (5 + chips),
        [(piece, BF16), (piece, BF16), ((width, width), F32), ((1, width), F32)],
    )(out_piece, inv, own_x, mine, theirs, bias_sum, *parts_x)
    return (output, grad_x, grad_w, grad_b.reshape(width))


def solution(mesh):
    placed = (
        P(("row", "col"), None),
        P(("row", "col")),
        P(),
        P(),
        P(("row", "col"), None),
        P("row", "col", None),
        P("row", "col", None, None),
        P("row", "col"),
    )
    return jax.shard_map(
        per_device,
        mesh=mesh,
        in_specs=placed,
        out_specs=(P(("row", "col"), None), P(("row", "col"), None), P(), P()),
        check_vma=False,
    )
```

```python
import functools

import jax
import jax.numpy as jnp
from jax import lax
from jax.experimental import pallas as pl
from jax.experimental.pallas import tpu as pltpu
from jax.sharding import PartitionSpec as P

BLOCK = 128
CORES = 2
EXTRA = 16
LONG = 4_000_000_000
GROUP = 4
VMEM = pl.BlockSpec(memory_space=pltpu.VMEM)
SMEM = pl.BlockSpec(memory_space=pltpu.SMEM)
NT = (((1,), (1,)), ((), ()))
TN = (((0,), (0,)), ((), ()))
BF16 = jnp.bfloat16
F32 = jnp.float32


def is_power(n):
    return n & (n - 1) == 0


def target(n, i, k):
    return i ^ k if is_power(n) else (i + k) % n


def offset_to(n, me, other):
    return me ^ other if is_power(n) else lax.rem(other - me + n, n)


def offset_from(n, me, other):
    return me ^ other if is_power(n) else lax.rem(me - other + n, n)


def to_core(x, rows):
    return lax.ppermute(x, "row", [(i, i ^ 1) for i in range(rows)])


def to_chip(x, rows, k):
    chips = rows // CORES
    pairs = [
        (a * CORES + b, target(chips, a, k) * CORES + b)
        for a in range(chips)
        for b in range(CORES)
    ]
    return lax.ppermute(x, "row", pairs)


def to_col(x, cols, k):
    return lax.ppermute(x, "col", [(i, target(cols, i, k)) for i in range(cols)])


def spread_inv(degree_ref, width):
    inv = lax.rsqrt(degree_ref[...].astype(F32))
    owned = inv.shape[1]
    tall = jnp.broadcast_to(inv, (BLOCK, owned)).T
    return jnp.concatenate([tall] * (width // BLOCK), axis=1)


def scale_kernel(features_ref, degree_ref, out_ref, inv_ref):
    inv = spread_inv(degree_ref, features_ref.shape[1])
    inv_ref[...] = inv
    out_ref[...] = (features_ref[...].astype(F32) * inv).astype(BF16)


def for_live(count_ref, slots, body):
    count = count_ref[0, 0]
    group = GROUP if slots % GROUP == 0 else 1

    def step(i, carry):
        for j in range(group):
            slot = i * group + j
            body(slot, slot < count)
        return carry

    lax.fori_loop(0, (count + group - 1) // group, step, 0)


def build_kernel(count_ref, edge_ref, bias_ref, blocks_ref, turned_ref, bias_out_ref):
    bias_out_ref[...] = bias_ref[...]
    slots, edges = edge_ref.shape[2], edge_ref.shape[3]
    node = lax.broadcasted_iota(jnp.int32, (BLOCK, edges), 0)

    def build(s, live):
        edge = edge_ref[0, 0, pl.ds(s, 1), :]
        row_hot = jnp.where(node == edge // BLOCK, 1.0, 0.0).astype(BF16)
        col_hot = jnp.where(node == edge % BLOCK, 1.0, 0.0).astype(BF16)
        counts = lax.dot_general(row_hot, col_hot, NT, preferred_element_type=F32)
        block = jnp.where(live, counts, 0.0).astype(BF16)
        blocks_ref[s] = block
        turned_ref[s] = block.T

    for_live(count_ref, slots, build)


def forward_kernel(rows, cols, pos_hold_ref, count_ref, blocks_ref, near_ref, next_ref, *refs):
    own_ref, *send, gathered, acc, pos_ref, sem = refs
    fetch = pltpu.make_async_copy(pos_hold_ref, pos_ref, sem)
    fetch.start()
    chips = rows // CORES
    row, col = lax.axis_index("row"), lax.axis_index("col")
    gathered[:chips] = near_ref[...]
    gathered[chips:] = next_ref[...]
    acc[...] = jnp.zeros_like(acc)
    fetch.wait()

    def add(s, live):
        p = pos_ref[0, 0, s]
        u, v = p // rows, lax.rem(p, rows)
        k = offset_from(chips, row // CORES, v // CORES)
        src = (lax.rem(v, CORES) ^ lax.rem(row, CORES)) * chips + k
        dst = offset_to(cols, col, u)
        acc[dst] += jnp.dot(blocks_ref[s], gathered[src], preferred_element_type=F32)

    for_live(count_ref, blocks_ref.shape[0], add)
    own_ref[...] = acc[0]
    for k, ref in enumerate(send, 1):
        ref[...] = acc[k].astype(BF16)


def pack_bias(total, rows):
    head = total.astype(BF16)
    tail = (total - head.astype(F32)).astype(BF16)
    index = lax.broadcasted_iota(jnp.int32, (rows, total.shape[1]), 0)
    both = jnp.where(index == 0, head.astype(F32), jnp.where(index == 1, tail.astype(F32), 0.0))
    return both.astype(BF16)


def add_bias(packed):
    return jnp.sum(packed.astype(F32), axis=0, keepdims=True)


def pointwise_kernel(cols, weight_ref, bias_ref, cot_ref, inv_ref, *refs):
    own_ref, *parts = refs[:cols]
    out_ref, message_ref = refs[cols:]
    owned = out_ref.shape[0]
    inv = inv_ref[...]
    total = own_ref[...]
    for ref in parts:
        total = total + ref[...].astype(F32)
    agg = (total * inv).astype(BF16)
    preact = jnp.dot(agg, weight_ref[...], preferred_element_type=F32) + bias_ref[...]
    sig = jax.nn.sigmoid(preact)
    out_ref[...] = (preact * sig).astype(BF16)
    grad_pre = (cot_ref[...].astype(F32) * sig * (1.0 + preact * (1.0 - sig))).astype(BF16).astype(F32)
    message_ref[:owned] = (grad_pre * inv).astype(BF16)
    message_ref[owned : 2 * owned] = total.astype(BF16)
    message_ref[2 * owned :] = pack_bias(jnp.sum(grad_pre, axis=0, keepdims=True), EXTRA)


def collect_kernel(*refs):
    *parts, out_ref = refs
    for n, ref in enumerate(parts):
        out_ref[n] = ref[...]


def backward_kernel(rows, cols, pos_hold_ref, count_ref, turned_ref, weight_ref, *refs):
    messages = refs[:cols]
    keep_ref, grads_keep_ref, bias_keep_ref, send_ref = refs[cols : cols + 4]
    rooted, sums, biases, hidden, acc, pos_ref, sem = refs[cols + 4 :]
    fetch = pltpu.make_async_copy(pos_hold_ref, pos_ref, sem)
    fetch.start()
    chips = rows // CORES
    row, col = lax.axis_index("row"), lax.axis_index("col")
    owned, width = rooted.shape[1:]
    for k, ref in enumerate(messages):
        owner = col ^ k if is_power(cols) else lax.rem(col - k + cols, cols)
        rooted[owner] = ref[:owned]
        sums[owner] = ref[owned : 2 * owned]
        biases[owner] = ref[2 * owned :]
    acc[...] = jnp.zeros_like(acc)
    for n in range(cols):
        hidden[n] = lax.dot_general(
            rooted[n], weight_ref[...], NT, preferred_element_type=F32
        ).astype(BF16)
    fetch.wait()

    def add(s, live):
        p = pos_ref[0, 0, s]
        u, v = p // rows, lax.rem(p, rows)
        k = offset_to(chips, row // CORES, v // CORES)
        dst = (lax.rem(v, CORES) ^ lax.rem(row, CORES)) * chips + k
        acc[dst] += jnp.dot(turned_ref[s], hidden[u], preferred_element_type=F32)

    for_live(count_ref, turned_ref.shape[0], add)
    keep_ref[...] = acc[:chips]
    for k in range(chips):
        send_ref[k * owned : (k + 1) * owned] = acc[chips + k].astype(BF16)

    term = lax.dot_general(
        sums[...].reshape(cols * owned, width),
        rooted[...].reshape(cols * owned, width),
        TN,
        preferred_element_type=F32,
    )
    half = width // CORES
    low, high = term[:half], term[half:]
    first = lax.rem(row, CORES) == 0
    grads_keep_ref[...] = jnp.where(first, low, high)
    base = chips * owned
    send_ref[base : base + half] = jnp.where(first, high, low).astype(BF16)
    bias = jnp.sum(biases[...].astype(F32), axis=(0, 1)).reshape(1, width)
    bias_keep_ref[...] = bias
    send_ref[base + half :] = pack_bias(bias, EXTRA)


def merge_kernel(keep_ref, grads_keep_ref, bias_keep_ref, got_ref, own_ref, grads_ref, *send):
    chips, owned = keep_ref.shape[:2]
    half = grads_keep_ref.shape[0]
    base = chips * owned
    grads = (grads_keep_ref[...] + got_ref[base : base + half].astype(F32)).astype(BF16)
    bias = pack_bias(bias_keep_ref[...] + add_bias(got_ref[base + half :]), EXTRA)
    grads_ref[:half] = grads
    grads_ref[half:] = bias
    own_ref[...] = keep_ref[0] + got_ref[:owned].astype(F32)
    for k, ref in enumerate(send, 1):
        part = got_ref[k * owned : (k + 1) * owned].astype(F32)
        ref[:owned] = (keep_ref[k] + part).astype(BF16)
        ref[owned : owned + half] = grads
        ref[owned + half :] = bias


def sum_grads_kernel(grads_ref, *refs):
    *parts, half_ref, bias_ref = refs
    half = half_ref.shape[0]
    grads = grads_ref[:half].astype(F32)
    bias = add_bias(grads_ref[half:])
    for ref in parts:
        grads = grads + ref[BLOCK : BLOCK + half].astype(F32)
        bias = bias + add_bias(ref[BLOCK + half :])
    half_ref[...] = grads
    bias_ref[...] = bias


def finish_kernel(norm, out_ref, inv_ref, own_ref, mine_ref, theirs_ref, bias_ref, *refs):
    *parts, output_ref, grad_x_ref, grad_w_ref, grad_b_ref = refs
    output_ref[...] = out_ref[...]
    total = own_ref[...]
    for ref in parts:
        total = total + ref[:BLOCK].astype(F32)
    grad_x_ref[...] = (total * inv_ref[...]).astype(BF16)
    half = mine_ref.shape[0]
    first = lax.rem(lax.axis_index("row"), CORES) == 0
    mine, theirs = mine_ref[...] * norm, theirs_ref[...] * norm
    grad_w_ref[:half] = jnp.where(first, mine, theirs)
    grad_w_ref[half:] = jnp.where(first, theirs, mine)
    grad_b_ref[...] = bias_ref[...] * norm


def call(kernel, specs, outs, scratch=(), flops=1_000_000):
    shapes = [jax.ShapeDtypeStruct(shape, dtype) for shape, dtype in outs]
    single = len(shapes) == 1
    return pl.pallas_call(
        kernel,
        out_shape=shapes[0] if single else tuple(shapes),
        in_specs=specs,
        out_specs=VMEM if single else tuple(VMEM for _ in shapes),
        scratch_shapes=scratch,
        compiler_params=pltpu.CompilerParams(vmem_limit_bytes=40 * 1024 * 1024),
        cost_estimate=pl.CostEstimate(flops=flops, bytes_accessed=1_000_000, transcendentals=0),
    )


def per_device(features, degree, weight, bias_vector, cotangent, block_pos, edge_pos, block_count):
    owned, width = features.shape
    rows, cols = lax.axis_size("row"), lax.axis_size("col")
    chips = rows // CORES
    slots = block_pos.shape[2]
    half = width // CORES
    piece = (owned, width)
    grads_shape = (half + EXTRA, width)
    degree = degree.reshape(1, owned)
    bias_vector = bias_vector.reshape(1, width)

    scaled, inv = call(scale_kernel, [VMEM, VMEM], [(piece, BF16), (piece, F32)])(features, degree)
    near = [to_chip(scaled, rows, k) for k in range(1, chips)]
    blocks, turned, bias_vector = call(
        build_kernel,
        [SMEM, VMEM, VMEM],
        [((slots, BLOCK, BLOCK), BF16)] * 2 + [((1, width), F32)],
        flops=LONG,
    )(block_count, edge_pos, bias_vector)
    blocks, *near = lax.optimization_barrier((blocks, *near))
    near = call(collect_kernel, [VMEM] * chips, [((chips,) + piece, BF16)])(scaled, *near)

    fetched = [pltpu.SMEM(block_pos.shape, jnp.int32), pltpu.SemaphoreType.DMA]
    own, *send = call(
        functools.partial(forward_kernel, rows, cols),
        [VMEM, SMEM, VMEM, VMEM, VMEM],
        [(piece, F32)] + [(piece, BF16)] * (cols - 1),
        [pltpu.VMEM((rows,) + piece, BF16), pltpu.VMEM((cols,) + piece, F32), *fetched],
    )(block_pos, block_count, blocks, near, to_core(near, rows))
    order = list(range(2, cols)) + [1]
    parts = [to_col(send[k - 1], cols, k) for k in order]

    out_piece, message = call(
        functools.partial(pointwise_kernel, cols),
        [VMEM] * (4 + cols),
        [(piece, BF16), ((2 * owned + EXTRA, width), BF16)],
    )(weight, bias_vector, cotangent, inv, own, *parts)
    messages = {k: to_col(message, cols, k) for k in order}

    col_keep, grads_keep, bias_keep, col_send = call(
        functools.partial(backward_kernel, rows, cols),
        [VMEM, SMEM, VMEM, VMEM] + [VMEM] * cols,
        [
            ((chips,) + piece, F32),
            ((half, width), F32),
            ((1, width), F32),
            ((chips * owned + half + EXTRA, width), BF16),
        ],
        [
            pltpu.VMEM((cols,) + piece, BF16),
            pltpu.VMEM((cols,) + piece, BF16),
            pltpu.VMEM((cols, EXTRA, width), BF16),
            pltpu.VMEM((cols,) + piece, BF16),
            pltpu.VMEM((rows,) + piece, F32),
            *fetched,
        ],
    )(block_pos, block_count, turned, weight, message, *(messages[k] for k in range(1, cols)))
    own_x, grads, *send_x = call(
        merge_kernel,
        [VMEM] * 4,
        [(piece, F32), (grads_shape, BF16)]
        + [((owned + half + EXTRA, width), BF16)] * (chips - 1),
    )(col_keep, grads_keep, bias_keep, to_core(col_send, rows))
    parts_x = [to_chip(send_x[k - 1], rows, k) for k in range(chips - 1, 0, -1)]

    mine, bias_sum = call(
        sum_grads_kernel, [VMEM] * chips, [((half, width), F32), ((1, width), F32)]
    )(grads, *parts_x)
    theirs = to_core(mine, rows)
    norm = float((owned * rows * cols) ** -0.5)
    output, grad_x, grad_w, grad_b = call(
        functools.partial(finish_kernel, norm),
        [VMEM] * (5 + chips),
        [(piece, BF16), (piece, BF16), ((width, width), F32), ((1, width), F32)],
    )(out_piece, inv, own_x, mine, theirs, bias_sum, *parts_x)
    return (output, grad_x, grad_w, grad_b.reshape(width))


def solution(mesh):
    placed = (
        P(("row", "col"), None),
        P(("row", "col")),
        P(),
        P(),
        P(("row", "col"), None),
        P("row", "col", None),
        P("row", "col", None, None),
        P("row", "col"),
    )
    return jax.shard_map(
        per_device,
        mesh=mesh,
        in_specs=placed,
        out_specs=(P(("row", "col"), None), P(("row", "col"), None), P(), P()),
        check_vma=False,
    )
```

```python
import functools

import jax
import jax.numpy as jnp
from jax import lax
from jax.experimental import pallas as pl
from jax.experimental.pallas import tpu as pltpu
from jax.sharding import PartitionSpec as P

BLOCK = 128
CORES = 2
EXTRA = 16
LONG = 4_000_000_000
GROUP = 4
VMEM = pl.BlockSpec(memory_space=pltpu.VMEM)
SMEM = pl.BlockSpec(memory_space=pltpu.SMEM)
NT = (((1,), (1,)), ((), ()))
TN = (((0,), (0,)), ((), ()))
BF16 = jnp.bfloat16
F32 = jnp.float32


def is_power(n):
    return n & (n - 1) == 0


def target(n, i, k):
    return i ^ k if is_power(n) else (i + k) % n


def offset_to(n, me, other):
    return me ^ other if is_power(n) else lax.rem(other - me + n, n)


def offset_from(n, me, other):
    return me ^ other if is_power(n) else lax.rem(me - other + n, n)


def to_core(x, rows):
    return lax.ppermute(x, "row", [(i, i ^ 1) for i in range(rows)])


def to_chip(x, rows, k):
    chips = rows // CORES
    pairs = [
        (a * CORES + b, target(chips, a, k) * CORES + b)
        for a in range(chips)
        for b in range(CORES)
    ]
    return lax.ppermute(x, "row", pairs)


def to_col(x, cols, k):
    return lax.ppermute(x, "col", [(i, target(cols, i, k)) for i in range(cols)])


def spread_inv(degree_ref, width):
    inv = lax.rsqrt(degree_ref[...].astype(F32))
    owned = inv.shape[1]
    tall = jnp.broadcast_to(inv, (BLOCK, owned)).T
    return jnp.concatenate([tall] * (width // BLOCK), axis=1)


def scale_kernel(features_ref, degree_ref, out_ref, inv_ref):
    inv = spread_inv(degree_ref, features_ref.shape[1])
    inv_ref[...] = inv
    out_ref[...] = (features_ref[...].astype(F32) * inv).astype(BF16)


def for_live(count_ref, slots, body):
    count = count_ref[0, 0]
    group = GROUP if slots % GROUP == 0 else 1

    def step(i, carry):
        for j in range(group):
            slot = i * group + j
            body(slot, slot < count)
        return carry

    lax.fori_loop(0, (count + group - 1) // group, step, 0)


def build_kernel(count_ref, edge_ref, bias_ref, blocks_ref, turned_ref, bias_out_ref):
    bias_out_ref[...] = bias_ref[...]
    slots, edges = edge_ref.shape[2], edge_ref.shape[3]
    node = lax.broadcasted_iota(jnp.int32, (BLOCK, edges), 0)

    def build(s, live):
        edge = edge_ref[0, 0, pl.ds(s, 1), :]
        row_hot = jnp.where(node == edge // BLOCK, 1.0, 0.0).astype(BF16)
        col_hot = jnp.where(node == edge % BLOCK, 1.0, 0.0).astype(BF16)
        counts = lax.dot_general(row_hot, col_hot, NT, preferred_element_type=F32)
        block = jnp.where(live, counts, 0.0).astype(BF16)
        blocks_ref[s] = block
        turned_ref[s] = block.T

    for_live(count_ref, slots, build)


def forward_kernel(rows, cols, pos_hold_ref, count_ref, blocks_ref, near_ref, next_ref, *refs):
    own_ref, *send, gathered, acc, pos_ref, sem = refs
    fetch = pltpu.make_async_copy(pos_hold_ref, pos_ref, sem)
    fetch.start()
    chips = rows // CORES
    row, col = lax.axis_index("row"), lax.axis_index("col")
    gathered[:chips] = near_ref[...]
    gathered[chips:] = next_ref[...]
    acc[...] = jnp.zeros_like(acc)
    fetch.wait()

    def add(s, live):
        p = pos_ref[0, 0, s]
        u, v = p // rows, lax.rem(p, rows)
        k = offset_from(chips, row // CORES, v // CORES)
        src = (lax.rem(v, CORES) ^ lax.rem(row, CORES)) * chips + k
        dst = offset_to(cols, col, u)
        acc[dst] += jnp.dot(blocks_ref[s], gathered[src], preferred_element_type=F32)

    for_live(count_ref, blocks_ref.shape[0], add)
    own_ref[...] = acc[0]
    for k, ref in enumerate(send, 1):
        ref[...] = acc[k].astype(BF16)


def pack_bias(total, rows):
    head = total.astype(BF16)
    tail = (total - head.astype(F32)).astype(BF16)
    index = lax.broadcasted_iota(jnp.int32, (rows, total.shape[1]), 0)
    both = jnp.where(index == 0, head.astype(F32), jnp.where(index == 1, tail.astype(F32), 0.0))
    return both.astype(BF16)


def add_bias(packed):
    return jnp.sum(packed.astype(F32), axis=0, keepdims=True)


def pointwise_kernel(cols, weight_ref, bias_ref, cot_ref, inv_ref, *refs):
    own_ref, *parts = refs[:cols]
    out_ref, hidden_ref, keep_ref, bias_keep_ref, send_ref = refs[cols:]
    width = out_ref.shape[1]
    half = width // CORES
    core = lax.rem(lax.axis_index("row"), CORES)
    inv = inv_ref[...]
    total = own_ref[...]
    for ref in parts:
        total = total + ref[...].astype(F32)
    agg = (total * inv).astype(BF16)
    weight = weight_ref[...]
    preact = jnp.dot(agg, weight, preferred_element_type=F32) + bias_ref[...]
    sig = jax.nn.sigmoid(preact)
    out_ref[...] = (preact * sig).astype(BF16)
    grad_pre = (cot_ref[...].astype(F32) * sig * (1.0 + preact * (1.0 - sig))).astype(BF16)
    hidden = lax.dot_general(grad_pre, weight, NT, preferred_element_type=F32)
    hidden_ref[...] = (hidden * inv).astype(BF16)
    term = lax.dot_general(agg, grad_pre, TN, preferred_element_type=F32)
    low, high = term[:half], term[half:]
    first = core == 0
    keep_ref[...] = jnp.where(first, low, high)
    send_ref[:half] = jnp.where(first, high, low).astype(BF16)
    bias_sum = jnp.sum(grad_pre.astype(F32), axis=0, keepdims=True)
    bias_keep_ref[...] = bias_sum
    send_ref[half:] = pack_bias(bias_sum, EXTRA)


def pair_sum_kernel(keep_ref, bias_keep_ref, got_ref, out_ref):
    half = keep_ref.shape[0]
    out_ref[:half] = (keep_ref[...] + got_ref[:half].astype(F32)).astype(BF16)
    out_ref[half:] = pack_bias(bias_keep_ref[...] + add_bias(got_ref[half:]), EXTRA)


def total_of(n, me, refs, stage):
    for k, ref in enumerate(refs):
        owner = me ^ k if is_power(n) else lax.rem(me - k + n, n)
        stage[owner] = ref[...]
    half = stage.shape[1] - EXTRA
    grads, bias = stage[0, :half].astype(F32), add_bias(stage[0, half:])
    for i in range(1, n):
        grads = grads + stage[i, :half].astype(F32)
        bias = bias + add_bias(stage[i, half:])
    return grads, bias


def chip_sum_kernel(*refs):
    *parts, out_ref, stage = refs
    chip = lax.axis_index("row") // CORES
    grads, bias = total_of(len(parts), chip, parts, stage)
    half = grads.shape[0]
    out_ref[:half] = grads.astype(BF16)
    out_ref[half:] = pack_bias(bias, EXTRA)


def col_sum_kernel(*refs):
    *parts, half_ref, bias_ref, stage = refs
    half_ref[...], bias_ref[...] = total_of(len(parts), lax.axis_index("col"), parts, stage)


def collect_kernel(*refs):
    *parts, out_ref = refs
    for n, ref in enumerate(parts):
        out_ref[n] = ref[...]


def backward_kernel(rows, cols, pos_hold_ref, count_ref, turned_ref, *refs):
    parts = refs[:cols]
    keep_ref, send_ref, hidden, acc, pos_ref, sem = refs[cols:]
    fetch = pltpu.make_async_copy(pos_hold_ref, pos_ref, sem)
    fetch.start()
    chips = rows // CORES
    row, col = lax.axis_index("row"), lax.axis_index("col")
    for k, ref in enumerate(parts):
        hidden[k] = ref[...]
    acc[...] = jnp.zeros_like(acc)
    fetch.wait()

    def add(s, live):
        p = pos_ref[0, 0, s]
        u, v = p // rows, lax.rem(p, rows)
        src = offset_from(cols, col, u)
        k = offset_to(chips, row // CORES, v // CORES)
        dst = (lax.rem(v, CORES) ^ lax.rem(row, CORES)) * chips + k
        acc[dst] += jnp.dot(turned_ref[s], hidden[src], preferred_element_type=F32)

    for_live(count_ref, turned_ref.shape[0], add)
    keep_ref[...] = acc[:chips]
    send_ref[...] = acc[chips:].astype(BF16)


def merge_kernel(keep_ref, got_ref, own_ref, *send):
    own_ref[...] = keep_ref[0] + got_ref[0].astype(F32)
    for k, ref in enumerate(send, 1):
        ref[...] = (keep_ref[k] + got_ref[k].astype(F32)).astype(BF16)


def owned_sum_kernel(inv_ref, own_ref, *refs):
    *parts, out_ref = refs
    total = own_ref[...]
    for ref in parts:
        total = total + ref[...].astype(F32)
    out_ref[...] = (total * inv_ref[...]).astype(BF16)


def finish_kernel(norm, out_ref, x_ref, mine_ref, theirs_ref, bias_ref, *refs):
    output_ref, grad_x_ref, grad_w_ref, grad_b_ref = refs
    output_ref[...] = out_ref[...]
    grad_x_ref[...] = x_ref[...]
    half = mine_ref.shape[0]
    first = lax.rem(lax.axis_index("row"), CORES) == 0
    mine, theirs = mine_ref[...] * norm, theirs_ref[...] * norm
    grad_w_ref[:half] = jnp.where(first, mine, theirs)
    grad_w_ref[half:] = jnp.where(first, theirs, mine)
    grad_b_ref[...] = bias_ref[...] * norm


def call(kernel, specs, outs, scratch=(), flops=1_000_000):
    shapes = [jax.ShapeDtypeStruct(shape, dtype) for shape, dtype in outs]
    single = len(shapes) == 1
    return pl.pallas_call(
        kernel,
        out_shape=shapes[0] if single else tuple(shapes),
        in_specs=specs,
        out_specs=VMEM if single else tuple(VMEM for _ in shapes),
        scratch_shapes=scratch,
        compiler_params=pltpu.CompilerParams(vmem_limit_bytes=40 * 1024 * 1024),
        cost_estimate=pl.CostEstimate(flops=flops, bytes_accessed=1_000_000, transcendentals=0),
    )


def per_device(features, degree, weight, bias_vector, cotangent, block_pos, edge_pos, block_count):
    owned, width = features.shape
    rows, cols = lax.axis_size("row"), lax.axis_size("col")
    chips = rows // CORES
    slots = block_pos.shape[2]
    half = width // CORES
    piece = (owned, width)
    grads_shape = (half + EXTRA, width)
    degree = degree.reshape(1, owned)
    bias_vector = bias_vector.reshape(1, width)

    scaled, inv = call(scale_kernel, [VMEM, VMEM], [(piece, BF16), (piece, F32)])(features, degree)
    near = [to_chip(scaled, rows, k) for k in range(1, chips)]
    blocks, turned, bias_vector = call(
        build_kernel,
        [SMEM, VMEM, VMEM],
        [((slots, BLOCK, BLOCK), BF16)] * 2 + [((1, width), F32)],
        flops=LONG,
    )(block_count, edge_pos, bias_vector)
    blocks, *near = lax.optimization_barrier((blocks, *near))
    near = call(collect_kernel, [VMEM] * chips, [((chips,) + piece, BF16)])(scaled, *near)

    fetched = [pltpu.SMEM(block_pos.shape, jnp.int32), pltpu.SemaphoreType.DMA]
    own, *send = call(
        functools.partial(forward_kernel, rows, cols),
        [VMEM, SMEM, VMEM, VMEM, VMEM],
        [(piece, F32)] + [(piece, BF16)] * (cols - 1),
        [pltpu.VMEM((rows,) + piece, BF16), pltpu.VMEM((cols,) + piece, F32), *fetched],
    )(block_pos, block_count, blocks, near, to_core(near, rows))
    order = list(range(2, cols)) + [1]
    parts = [to_col(send[k - 1], cols, k) for k in order]

    out_piece, hidden, keep, bias_keep, half_send = call(
        functools.partial(pointwise_kernel, cols),
        [VMEM] * (4 + cols),
        [(piece, BF16), (piece, BF16), ((half, width), F32), ((1, width), F32), (grads_shape, BF16)],
    )(weight, bias_vector, cotangent, inv, own, *parts)

    hidden_parts = {k: to_col(hidden, cols, k) for k in order}
    grads = call(pair_sum_kernel, [VMEM] * 3, [(grads_shape, BF16)])(
        keep, bias_keep, to_core(half_send, rows)
    )
    across = range(chips - 1, 0, -1)
    grad_parts = {k: to_chip(grads, rows, k) for k in across}
    grads = call(
        chip_sum_kernel,
        [VMEM] * chips,
        [(grads_shape, BF16)],
        [pltpu.VMEM((chips,) + grads_shape, BF16)],
    )(grads, *(grad_parts[k] for k in range(1, chips)))

    col_keep, col_send = call(
        functools.partial(backward_kernel, rows, cols),
        [VMEM, SMEM, VMEM] + [VMEM] * cols,
        [((chips,) + piece, F32), ((chips,) + piece, BF16)],
        [pltpu.VMEM((cols,) + piece, BF16), pltpu.VMEM((rows,) + piece, F32), *fetched],
        flops=LONG,
    )(block_pos, block_count, turned, hidden, *(hidden_parts[k] for k in range(1, cols)))
    col_send, grads = lax.optimization_barrier((col_send, grads))
    grad_parts = {k: to_col(grads, cols, k) for k in order}
    own_x, *send_x = call(
        merge_kernel, [VMEM] * 2, [(piece, F32)] + [(piece, BF16)] * (chips - 1)
    )(col_keep, to_core(col_send, rows))
    parts_x = [to_chip(send_x[k - 1], rows, k) for k in across]

    mine, bias_sum = call(
        col_sum_kernel,
        [VMEM] * cols,
        [((half, width), F32), ((1, width), F32)],
        [pltpu.VMEM((cols,) + grads_shape, BF16)],
    )(grads, *(grad_parts[k] for k in range(1, cols)))
    theirs = to_core(mine, rows)
    x_piece = call(owned_sum_kernel, [VMEM] * (1 + chips), [(piece, BF16)], flops=LONG)(
        inv, own_x, *parts_x
    )
    norm = float((owned * rows * cols) ** -0.5)
    output, grad_x, grad_w, grad_b = call(
        functools.partial(finish_kernel, norm),
        [VMEM] * 5,
        [(piece, BF16), (piece, BF16), ((width, width), F32), ((1, width), F32)],
    )(out_piece, x_piece, mine, theirs, bias_sum)
    return (output, grad_x, grad_w, grad_b.reshape(width))


def solution(mesh):
    placed = (
        P(("row", "col"), None),
        P(("row", "col")),
        P(),
        P(),
        P(("row", "col"), None),
        P("row", "col", None),
        P("row", "col", None, None),
        P("row", "col"),
    )
    return jax.shard_map(
        per_device,
        mesh=mesh,
        in_specs=placed,
        out_specs=(P(("row", "col"), None), P(("row", "col"), None), P(), P()),
        check_vma=False,
    )
```

```python
import functools

import jax
import jax.numpy as jnp
from jax import lax
from jax.experimental import pallas as pl
from jax.experimental.pallas import tpu as pltpu
from jax.sharding import PartitionSpec as P

BLOCK = 128
CORES = 2
EXTRA = 16
LONG = 4_000_000_000
GROUP = 8
VMEM = pl.BlockSpec(memory_space=pltpu.VMEM)
SMEM = pl.BlockSpec(memory_space=pltpu.SMEM)
NT = (((1,), (1,)), ((), ()))
TN = (((0,), (0,)), ((), ()))
BF16 = jnp.bfloat16
F32 = jnp.float32


def is_power(n):
    return n & (n - 1) == 0


def target(n, i, k):
    return i ^ k if is_power(n) else (i + k) % n


def offset_to(n, me, other):
    return me ^ other if is_power(n) else lax.rem(other - me + n, n)


def offset_from(n, me, other):
    return me ^ other if is_power(n) else lax.rem(me - other + n, n)


def to_core(x, rows):
    return lax.ppermute(x, "row", [(i, i ^ 1) for i in range(rows)])


def to_chip(x, rows, k):
    chips = rows // CORES
    pairs = [
        (a * CORES + b, target(chips, a, k) * CORES + b)
        for a in range(chips)
        for b in range(CORES)
    ]
    return lax.ppermute(x, "row", pairs)


def to_col(x, cols, k):
    return lax.ppermute(x, "col", [(i, target(cols, i, k)) for i in range(cols)])


def spread_inv(degree_ref, width):
    inv = lax.rsqrt(degree_ref[...].astype(F32))
    owned = inv.shape[1]
    tall = jnp.broadcast_to(inv, (BLOCK, owned)).T
    return jnp.concatenate([tall] * (width // BLOCK), axis=1)


def scale_kernel(features_ref, degree_ref, out_ref, inv_ref):
    inv = spread_inv(degree_ref, features_ref.shape[1])
    inv_ref[...] = inv
    out_ref[...] = (features_ref[...].astype(F32) * inv).astype(BF16)


def group_of(slots):
    return GROUP if slots % GROUP == 0 else 1


def for_live(count, slots, body):
    group = group_of(slots)
    for start in range(0, slots, group):

        @pl.when(start < count)
        def _():
            for slot in range(start, start + group):
                body(slot)


def build_kernel(count_ref, edge_ref, bias_ref, blocks_ref, turned_ref, bias_out_ref):
    bias_out_ref[...] = bias_ref[...]
    slots, edges = edge_ref.shape[2], edge_ref.shape[3]
    node = lax.broadcasted_iota(jnp.int32, (BLOCK, edges), 0)

    count = count_ref[0, 0]
    group = group_of(slots)

    def build(s):
        edge = edge_ref[0, 0, pl.ds(s, 1), :]
        row_hot = jnp.where(node == edge // BLOCK, 1.0, 0.0).astype(BF16)
        col_hot = jnp.where(node == edge % BLOCK, 1.0, 0.0).astype(BF16)
        counts = lax.dot_general(row_hot, col_hot, NT, preferred_element_type=F32)
        block = jnp.where(s < count, counts, 0.0).astype(BF16)
        blocks_ref[s] = block
        turned_ref[s] = block.T

    def step(i, carry):
        for j in range(group):
            build(i * group + j)
        return carry

    lax.fori_loop(0, (count + group - 1) // group, step, 0)


def forward_kernel(rows, cols, pos_ref, count_ref, blocks_ref, near_ref, next_ref, *refs):
    own_ref, *send, gathered, acc = refs
    chips = rows // CORES
    row, col = lax.axis_index("row"), lax.axis_index("col")
    gathered[:chips] = near_ref[...]
    gathered[chips:] = next_ref[...]
    acc[...] = jnp.zeros_like(acc)
    positions = pos_ref[0]

    def add(s):
        p = positions[0, s]
        u, v = p // rows, lax.rem(p, rows)
        k = offset_from(chips, row // CORES, v // CORES)
        src = (lax.rem(v, CORES) ^ lax.rem(row, CORES)) * chips + k
        dst = offset_to(cols, col, u)
        acc[dst] += jnp.dot(blocks_ref[s], gathered[src], preferred_element_type=F32)

    for_live(count_ref[0, 0], blocks_ref.shape[0], add)
    own_ref[...] = acc[0]
    for k, ref in enumerate(send, 1):
        ref[...] = acc[k].astype(BF16)


def pack_bias(total, rows):
    head = total.astype(BF16)
    tail = (total - head.astype(F32)).astype(BF16)
    index = lax.broadcasted_iota(jnp.int32, (rows, total.shape[1]), 0)
    both = jnp.where(index == 0, head.astype(F32), jnp.where(index == 1, tail.astype(F32), 0.0))
    return both.astype(BF16)


def add_bias(packed):
    return jnp.sum(packed.astype(F32), axis=0, keepdims=True)


def pointwise_kernel(cols, weight_ref, bias_ref, cot_ref, inv_ref, *refs):
    own_ref, *parts = refs[:cols]
    out_ref, hidden_ref, keep_ref, bias_keep_ref, send_ref = refs[cols:]
    width = out_ref.shape[1]
    half = width // CORES
    core = lax.rem(lax.axis_index("row"), CORES)
    inv = inv_ref[...]
    total = own_ref[...]
    for ref in parts:
        total = total + ref[...].astype(F32)
    agg = (total * inv).astype(BF16)
    weight = weight_ref[...]
    preact = jnp.dot(agg, weight, preferred_element_type=F32) + bias_ref[...]
    sig = jax.nn.sigmoid(preact)
    out_ref[...] = (preact * sig).astype(BF16)
    grad_pre = (cot_ref[...].astype(F32) * sig * (1.0 + preact * (1.0 - sig))).astype(BF16)
    hidden = lax.dot_general(grad_pre, weight, NT, preferred_element_type=F32)
    hidden_ref[...] = (hidden * inv).astype(BF16)
    term = lax.dot_general(agg, grad_pre, TN, preferred_element_type=F32)
    low, high = term[:half], term[half:]
    first = core == 0
    keep_ref[...] = jnp.where(first, low, high)
    send_ref[:half] = jnp.where(first, high, low).astype(BF16)
    bias_sum = jnp.sum(grad_pre.astype(F32), axis=0, keepdims=True)
    bias_keep_ref[...] = bias_sum
    send_ref[half:] = pack_bias(bias_sum, EXTRA)


def pair_sum_kernel(keep_ref, bias_keep_ref, got_ref, out_ref):
    half = keep_ref.shape[0]
    out_ref[:half] = (keep_ref[...] + got_ref[:half].astype(F32)).astype(BF16)
    out_ref[half:] = pack_bias(bias_keep_ref[...] + add_bias(got_ref[half:]), EXTRA)


def total_of(n, me, refs, stage):
    for k, ref in enumerate(refs):
        owner = me ^ k if is_power(n) else lax.rem(me - k + n, n)
        stage[owner] = ref[...]
    half = stage.shape[1] - EXTRA
    grads, bias = stage[0, :half].astype(F32), add_bias(stage[0, half:])
    for i in range(1, n):
        grads = grads + stage[i, :half].astype(F32)
        bias = bias + add_bias(stage[i, half:])
    return grads, bias


def chip_sum_kernel(*refs):
    *parts, out_ref, stage = refs
    chip = lax.axis_index("row") // CORES
    grads, bias = total_of(len(parts), chip, parts, stage)
    half = grads.shape[0]
    out_ref[:half] = grads.astype(BF16)
    out_ref[half:] = pack_bias(bias, EXTRA)


def col_sum_kernel(*refs):
    *parts, half_ref, bias_ref, stage = refs
    half_ref[...], bias_ref[...] = total_of(len(parts), lax.axis_index("col"), parts, stage)


def collect_kernel(*refs):
    *parts, out_ref = refs
    for n, ref in enumerate(parts):
        out_ref[n] = ref[...]


def backward_kernel(rows, cols, pos_ref, count_ref, turned_ref, *refs):
    parts = refs[:cols]
    keep_ref, send_ref, hidden, acc = refs[cols:]
    chips = rows // CORES
    row, col = lax.axis_index("row"), lax.axis_index("col")
    for k, ref in enumerate(parts):
        hidden[k] = ref[...]
    acc[...] = jnp.zeros_like(acc)
    positions = pos_ref[0]

    def add(s):
        p = positions[0, s]
        u, v = p // rows, lax.rem(p, rows)
        src = offset_from(cols, col, u)
        k = offset_to(chips, row // CORES, v // CORES)
        dst = (lax.rem(v, CORES) ^ lax.rem(row, CORES)) * chips + k
        acc[dst] += jnp.dot(turned_ref[s], hidden[src], preferred_element_type=F32)

    for_live(count_ref[0, 0], turned_ref.shape[0], add)
    keep_ref[...] = acc[:chips]
    send_ref[...] = acc[chips:].astype(BF16)


def merge_kernel(keep_ref, got_ref, own_ref, *send):
    own_ref[...] = keep_ref[0] + got_ref[0].astype(F32)
    for k, ref in enumerate(send, 1):
        ref[...] = (keep_ref[k] + got_ref[k].astype(F32)).astype(BF16)


def owned_sum_kernel(inv_ref, own_ref, *refs):
    *parts, out_ref = refs
    total = own_ref[...]
    for ref in parts:
        total = total + ref[...].astype(F32)
    out_ref[...] = (total * inv_ref[...]).astype(BF16)


def finish_kernel(norm, out_ref, x_ref, mine_ref, theirs_ref, bias_ref, *refs):
    output_ref, grad_x_ref, grad_w_ref, grad_b_ref = refs
    output_ref[...] = out_ref[...]
    grad_x_ref[...] = x_ref[...]
    half = mine_ref.shape[0]
    first = lax.rem(lax.axis_index("row"), CORES) == 0
    mine, theirs = mine_ref[...] * norm, theirs_ref[...] * norm
    grad_w_ref[:half] = jnp.where(first, mine, theirs)
    grad_w_ref[half:] = jnp.where(first, theirs, mine)
    grad_b_ref[...] = bias_ref[...] * norm


def call(kernel, specs, outs, scratch=(), flops=1_000_000):
    shapes = [jax.ShapeDtypeStruct(shape, dtype) for shape, dtype in outs]
    single = len(shapes) == 1
    return pl.pallas_call(
        kernel,
        out_shape=shapes[0] if single else tuple(shapes),
        in_specs=specs,
        out_specs=VMEM if single else tuple(VMEM for _ in shapes),
        scratch_shapes=scratch,
        compiler_params=pltpu.CompilerParams(vmem_limit_bytes=40 * 1024 * 1024),
        cost_estimate=pl.CostEstimate(flops=flops, bytes_accessed=1_000_000, transcendentals=0),
    )


def per_device(features, degree, weight, bias_vector, cotangent, block_pos, edge_pos, block_count):
    owned, width = features.shape
    rows, cols = lax.axis_size("row"), lax.axis_size("col")
    chips = rows // CORES
    slots = block_pos.shape[2]
    half = width // CORES
    piece = (owned, width)
    grads_shape = (half + EXTRA, width)
    degree = degree.reshape(1, owned)
    bias_vector = bias_vector.reshape(1, width)

    scaled, inv = call(scale_kernel, [VMEM, VMEM], [(piece, BF16), (piece, F32)])(features, degree)
    near = [to_chip(scaled, rows, k) for k in range(1, chips)]
    blocks, turned, bias_vector = call(
        build_kernel,
        [SMEM, VMEM, VMEM],
        [((slots, BLOCK, BLOCK), BF16)] * 2 + [((1, width), F32)],
        flops=LONG,
    )(block_count, edge_pos, bias_vector)
    blocks, *near = lax.optimization_barrier((blocks, *near))
    near = call(collect_kernel, [VMEM] * chips, [((chips,) + piece, BF16)])(scaled, *near)

    own, *send = call(
        functools.partial(forward_kernel, rows, cols),
        [VMEM, SMEM, VMEM, VMEM, VMEM],
        [(piece, F32)] + [(piece, BF16)] * (cols - 1),
        [pltpu.VMEM((rows,) + piece, BF16), pltpu.VMEM((cols,) + piece, F32)],
    )(block_pos, block_count, blocks, near, to_core(near, rows))
    order = list(range(2, cols)) + [1]
    parts = [to_col(send[k - 1], cols, k) for k in order]

    out_piece, hidden, keep, bias_keep, half_send = call(
        functools.partial(pointwise_kernel, cols),
        [VMEM] * (4 + cols),
        [(piece, BF16), (piece, BF16), ((half, width), F32), ((1, width), F32), (grads_shape, BF16)],
    )(weight, bias_vector, cotangent, inv, own, *parts)

    hidden_parts = {k: to_col(hidden, cols, k) for k in order}
    grads = call(pair_sum_kernel, [VMEM] * 3, [(grads_shape, BF16)])(
        keep, bias_keep, to_core(half_send, rows)
    )
    across = range(chips - 1, 0, -1)
    grad_parts = {k: to_chip(grads, rows, k) for k in across}
    grads = call(
        chip_sum_kernel,
        [VMEM] * chips,
        [(grads_shape, BF16)],
        [pltpu.VMEM((chips,) + grads_shape, BF16)],
    )(grads, *(grad_parts[k] for k in range(1, chips)))

    col_keep, col_send = call(
        functools.partial(backward_kernel, rows, cols),
        [VMEM, SMEM, VMEM] + [VMEM] * cols,
        [((chips,) + piece, F32), ((chips,) + piece, BF16)],
        [pltpu.VMEM((cols,) + piece, BF16), pltpu.VMEM((rows,) + piece, F32)],
        flops=LONG,
    )(block_pos, block_count, turned, hidden, *(hidden_parts[k] for k in range(1, cols)))
    col_send, grads = lax.optimization_barrier((col_send, grads))
    grad_parts = {k: to_col(grads, cols, k) for k in order}
    own_x, *send_x = call(
        merge_kernel, [VMEM] * 2, [(piece, F32)] + [(piece, BF16)] * (chips - 1)
    )(col_keep, to_core(col_send, rows))
    parts_x = [to_chip(send_x[k - 1], rows, k) for k in across]

    mine, bias_sum = call(
        col_sum_kernel,
        [VMEM] * cols,
        [((half, width), F32), ((1, width), F32)],
        [pltpu.VMEM((cols,) + grads_shape, BF16)],
    )(grads, *(grad_parts[k] for k in range(1, cols)))
    theirs = to_core(mine, rows)
    x_piece = call(owned_sum_kernel, [VMEM] * (1 + chips), [(piece, BF16)], flops=LONG)(
        inv, own_x, *parts_x
    )
    norm = float((owned * rows * cols) ** -0.5)
    output, grad_x, grad_w, grad_b = call(
        functools.partial(finish_kernel, norm),
        [VMEM] * 5,
        [(piece, BF16), (piece, BF16), ((width, width), F32), ((1, width), F32)],
    )(out_piece, x_piece, mine, theirs, bias_sum)
    return (output, grad_x, grad_w, grad_b.reshape(width))


def solution(mesh):
    placed = (
        P(("row", "col"), None),
        P(("row", "col")),
        P(),
        P(),
        P(("row", "col"), None),
        P("row", "col", None),
        P("row", "col", None, None),
        P("row", "col"),
    )
    return jax.shard_map(
        per_device,
        mesh=mesh,
        in_specs=placed,
        out_specs=(P(("row", "col"), None), P(("row", "col"), None), P(), P()),
        check_vma=False,
    )
```

```python
import functools

import jax
import jax.numpy as jnp
from jax import lax
from jax.experimental import pallas as pl
from jax.experimental.pallas import tpu as pltpu
from jax.sharding import PartitionSpec as P

BLOCK = 128
CORES = 2
EXTRA = 16
LONG = 4_000_000_000
GROUP = 8
VMEM = pl.BlockSpec(memory_space=pltpu.VMEM)
SMEM = pl.BlockSpec(memory_space=pltpu.SMEM)
NT = (((1,), (1,)), ((), ()))
TN = (((0,), (0,)), ((), ()))
BF16 = jnp.bfloat16
F32 = jnp.float32


def is_power(n):
    return n & (n - 1) == 0


def target(n, i, k):
    return i ^ k if is_power(n) else (i + k) % n


def offset_to(n, me, other):
    return me ^ other if is_power(n) else lax.rem(other - me + n, n)


def offset_from(n, me, other):
    return me ^ other if is_power(n) else lax.rem(me - other + n, n)


def to_core(x, rows):
    return lax.ppermute(x, "row", [(i, i ^ 1) for i in range(rows)])


def to_chip(x, rows, k):
    chips = rows // CORES
    pairs = [
        (a * CORES + b, target(chips, a, k) * CORES + b)
        for a in range(chips)
        for b in range(CORES)
    ]
    return lax.ppermute(x, "row", pairs)


def to_col(x, cols, k):
    return lax.ppermute(x, "col", [(i, target(cols, i, k)) for i in range(cols)])


def spread_inv(degree_ref, width):
    inv = lax.rsqrt(degree_ref[...].astype(F32))
    owned = inv.shape[1]
    tall = jnp.broadcast_to(inv, (BLOCK, owned)).T
    return jnp.concatenate([tall] * (width // BLOCK), axis=1)


def scale_kernel(features_ref, degree_ref, out_ref, inv_ref):
    inv = spread_inv(degree_ref, features_ref.shape[1])
    inv_ref[...] = inv
    out_ref[...] = (features_ref[...].astype(F32) * inv).astype(BF16)


def group_of(slots):
    return GROUP if slots % GROUP == 0 else 1


def for_live(count, slots, body):
    group = group_of(slots)
    for start in range(0, slots, group):

        @pl.when(start < count)
        def _():
            for slot in range(start, start + group):
                body(slot)


def build_kernel(count_ref, edge_ref, bias_ref, blocks_ref, turned_ref, bias_out_ref):
    bias_out_ref[...] = bias_ref[...]
    slots, edges = edge_ref.shape[2], edge_ref.shape[3]
    node = lax.broadcasted_iota(jnp.int32, (BLOCK, edges), 0)

    count = count_ref[0, 0]
    group = group_of(slots)

    def build(s):
        edge = edge_ref[0, 0, pl.ds(s, 1), :]
        row_hot = jnp.where(node == edge // BLOCK, 1.0, 0.0).astype(BF16)
        col_hot = jnp.where(node == edge % BLOCK, 1.0, 0.0).astype(BF16)
        counts = lax.dot_general(row_hot, col_hot, NT, preferred_element_type=F32)
        block = jnp.where(s < count, counts, 0.0).astype(BF16)
        blocks_ref[s] = block
        turned_ref[s] = block.T

    def step(i, carry):
        for j in range(group):
            build(i * group + j)
        return carry

    lax.fori_loop(0, (count + group - 1) // group, step, 0)


def forward_kernel(rows, cols, pos_ref, count_ref, blocks_ref, near_ref, next_ref, *refs):
    own_ref, *send, gathered, acc = refs
    chips = rows // CORES
    row, col = lax.axis_index("row"), lax.axis_index("col")
    gathered[:chips] = near_ref[...]
    gathered[chips:] = next_ref[...]
    acc[...] = jnp.zeros_like(acc)
    positions = pos_ref[0]

    def add(s):
        p = positions[0, s]
        u, v = p // rows, lax.rem(p, rows)
        k = offset_from(chips, row // CORES, v // CORES)
        src = (lax.rem(v, CORES) ^ lax.rem(row, CORES)) * chips + k
        dst = offset_to(cols, col, u)
        acc[dst] += jnp.dot(blocks_ref[s], gathered[src], preferred_element_type=F32)

    for_live(count_ref[0, 0], blocks_ref.shape[0], add)
    own_ref[...] = acc[0]
    for k, ref in enumerate(send, 1):
        ref[...] = acc[k].astype(BF16)


def pack_bias(total, rows):
    head = total.astype(BF16)
    tail = (total - head.astype(F32)).astype(BF16)
    index = lax.broadcasted_iota(jnp.int32, (rows, total.shape[1]), 0)
    both = jnp.where(index == 0, head.astype(F32), jnp.where(index == 1, tail.astype(F32), 0.0))
    return both.astype(BF16)


def add_bias(packed):
    return jnp.sum(packed.astype(F32), axis=0, keepdims=True)


def pointwise_kernel(cols, weight_ref, bias_ref, cot_ref, inv_ref, *refs):
    own_ref, *parts = refs[:cols]
    out_ref, hidden_ref, keep_ref, bias_keep_ref, send_ref = refs[cols:]
    width = out_ref.shape[1]
    half = width // CORES
    core = lax.rem(lax.axis_index("row"), CORES)
    inv = inv_ref[...]
    total = own_ref[...]
    for ref in parts:
        total = total + ref[...].astype(F32)
    agg = (total * inv).astype(BF16)
    weight = weight_ref[...]
    preact = jnp.dot(agg, weight, preferred_element_type=F32) + bias_ref[...]
    sig = jax.nn.sigmoid(preact)
    out_ref[...] = (preact * sig).astype(BF16)
    grad_pre = (cot_ref[...].astype(F32) * sig * (1.0 + preact * (1.0 - sig))).astype(BF16)
    hidden = lax.dot_general(grad_pre, weight, NT, preferred_element_type=F32)
    hidden_ref[...] = (hidden * inv).astype(BF16)
    term = lax.dot_general(agg, grad_pre, TN, preferred_element_type=F32)
    low, high = term[:half], term[half:]
    first = core == 0
    keep_ref[...] = jnp.where(first, low, high)
    send_ref[:half] = jnp.where(first, high, low).astype(BF16)
    bias_sum = jnp.sum(grad_pre.astype(F32), axis=0, keepdims=True)
    bias_keep_ref[...] = bias_sum
    send_ref[half:] = pack_bias(bias_sum, EXTRA)


def pair_sum_kernel(keep_ref, bias_keep_ref, got_ref, out_ref):
    half = keep_ref.shape[0]
    out_ref[:half] = (keep_ref[...] + got_ref[:half].astype(F32)).astype(BF16)
    out_ref[half:] = pack_bias(bias_keep_ref[...] + add_bias(got_ref[half:]), EXTRA)


def total_of(n, me, refs, stage):
    for k, ref in enumerate(refs):
        owner = me ^ k if is_power(n) else lax.rem(me - k + n, n)
        stage[owner] = ref[...]
    half = stage.shape[1] - EXTRA
    grads, bias = stage[0, :half].astype(F32), add_bias(stage[0, half:])
    for i in range(1, n):
        grads = grads + stage[i, :half].astype(F32)
        bias = bias + add_bias(stage[i, half:])
    return grads, bias


def chip_sum_kernel(*refs):
    *parts, out_ref, stage = refs
    chip = lax.axis_index("row") // CORES
    grads, bias = total_of(len(parts), chip, parts, stage)
    half = grads.shape[0]
    out_ref[:half] = grads.astype(BF16)
    out_ref[half:] = pack_bias(bias, EXTRA)


def col_sum_kernel(norm, *refs):
    *parts, half_ref, bias_ref, stage = refs
    grads, bias = total_of(len(parts), lax.axis_index("col"), parts, stage)
    half_ref[...] = grads * norm
    bias_ref[...] = bias * norm


def collect_kernel(*refs):
    *parts, out_ref = refs
    for n, ref in enumerate(parts):
        out_ref[n] = ref[...]


def backward_kernel(rows, cols, pos_ref, count_ref, turned_ref, *refs):
    parts = refs[:cols]
    keep_ref, send_ref, hidden, acc = refs[cols:]
    chips = rows // CORES
    row, col = lax.axis_index("row"), lax.axis_index("col")
    for k, ref in enumerate(parts):
        hidden[k] = ref[...]
    acc[...] = jnp.zeros_like(acc)
    positions = pos_ref[0]

    def add(s):
        p = positions[0, s]
        u, v = p // rows, lax.rem(p, rows)
        src = offset_from(cols, col, u)
        k = offset_to(chips, row // CORES, v // CORES)
        dst = (lax.rem(v, CORES) ^ lax.rem(row, CORES)) * chips + k
        acc[dst] += jnp.dot(turned_ref[s], hidden[src], preferred_element_type=F32)

    for_live(count_ref[0, 0], turned_ref.shape[0], add)
    keep_ref[...] = acc[:chips]
    send_ref[...] = acc[chips:].astype(BF16)


def merge_kernel(keep_ref, got_ref, own_ref, *send):
    own_ref[...] = keep_ref[0] + got_ref[0].astype(F32)
    for k, ref in enumerate(send, 1):
        ref[...] = (keep_ref[k] + got_ref[k].astype(F32)).astype(BF16)


def owned_sum_kernel(inv_ref, own_ref, *refs):
    *parts, out_ref = refs
    total = own_ref[...]
    for ref in parts:
        total = total + ref[...].astype(F32)
    out_ref[...] = (total * inv_ref[...]).astype(BF16)


def finish_kernel(out_ref, x_ref, mine_ref, theirs_ref, bias_ref, *refs):
    output_ref, grad_x_ref, grad_w_ref, grad_b_ref, sems = refs
    half = mine_ref.shape[0]
    core = lax.rem(lax.axis_index("row"), CORES)
    moves = [
        (mine_ref, grad_w_ref.at[pl.ds(pl.multiple_of(core * half, half), half)]),
        (theirs_ref, grad_w_ref.at[pl.ds(pl.multiple_of((1 - core) * half, half), half)]),
        (out_ref, output_ref),
        (x_ref, grad_x_ref),
        (bias_ref, grad_b_ref),
    ]
    copies = [pltpu.make_async_copy(*move, sems.at[i]) for i, move in enumerate(moves)]
    for copy in copies:
        copy.start()
    for copy in copies:
        copy.wait()


def call(kernel, specs, outs, scratch=(), flops=1_000_000, place=VMEM):
    shapes = [jax.ShapeDtypeStruct(shape, dtype) for shape, dtype in outs]
    single = len(shapes) == 1
    return pl.pallas_call(
        kernel,
        out_shape=shapes[0] if single else tuple(shapes),
        in_specs=specs,
        out_specs=place if single else tuple(place for _ in shapes),
        scratch_shapes=scratch,
        compiler_params=pltpu.CompilerParams(vmem_limit_bytes=40 * 1024 * 1024),
        cost_estimate=pl.CostEstimate(flops=flops, bytes_accessed=1_000_000, transcendentals=0),
    )


def per_device(features, degree, weight, bias_vector, cotangent, block_pos, edge_pos, block_count):
    owned, width = features.shape
    rows, cols = lax.axis_size("row"), lax.axis_size("col")
    chips = rows // CORES
    slots = block_pos.shape[2]
    half = width // CORES
    piece = (owned, width)
    grads_shape = (half + EXTRA, width)
    degree = degree.reshape(1, owned)
    bias_vector = bias_vector.reshape(1, width)

    scaled, inv = call(scale_kernel, [VMEM, VMEM], [(piece, BF16), (piece, F32)])(features, degree)
    near = [to_chip(scaled, rows, k) for k in range(1, chips)]
    blocks, turned, bias_vector = call(
        build_kernel,
        [SMEM, VMEM, VMEM],
        [((slots, BLOCK, BLOCK), BF16)] * 2 + [((1, width), F32)],
        flops=LONG,
    )(block_count, edge_pos, bias_vector)
    blocks, *near = lax.optimization_barrier((blocks, *near))
    near = call(collect_kernel, [VMEM] * chips, [((chips,) + piece, BF16)])(scaled, *near)

    own, *send = call(
        functools.partial(forward_kernel, rows, cols),
        [VMEM, SMEM, VMEM, VMEM, VMEM],
        [(piece, F32)] + [(piece, BF16)] * (cols - 1),
        [pltpu.VMEM((rows,) + piece, BF16), pltpu.VMEM((cols,) + piece, F32)],
    )(block_pos, block_count, blocks, near, to_core(near, rows))
    order = list(range(2, cols)) + [1]
    parts = [to_col(send[k - 1], cols, k) for k in order]

    out_piece, hidden, keep, bias_keep, half_send = call(
        functools.partial(pointwise_kernel, cols),
        [VMEM] * (4 + cols),
        [(piece, BF16), (piece, BF16), ((half, width), F32), ((1, width), F32), (grads_shape, BF16)],
    )(weight, bias_vector, cotangent, inv, own, *parts)

    hidden_parts = {k: to_col(hidden, cols, k) for k in order}
    grads = call(pair_sum_kernel, [VMEM] * 3, [(grads_shape, BF16)])(
        keep, bias_keep, to_core(half_send, rows)
    )
    across = range(chips - 1, 0, -1)
    grad_parts = {k: to_chip(grads, rows, k) for k in across}
    grads = call(
        chip_sum_kernel,
        [VMEM] * chips,
        [(grads_shape, BF16)],
        [pltpu.VMEM((chips,) + grads_shape, BF16)],
    )(grads, *(grad_parts[k] for k in range(1, chips)))

    col_keep, col_send = call(
        functools.partial(backward_kernel, rows, cols),
        [VMEM, SMEM, VMEM] + [VMEM] * cols,
        [((chips,) + piece, F32), ((chips,) + piece, BF16)],
        [pltpu.VMEM((cols,) + piece, BF16), pltpu.VMEM((rows,) + piece, F32)],
        flops=LONG,
    )(block_pos, block_count, turned, hidden, *(hidden_parts[k] for k in range(1, cols)))
    col_send, grads = lax.optimization_barrier((col_send, grads))
    grad_parts = {k: to_col(grads, cols, k) for k in order}
    own_x, *send_x = call(
        merge_kernel, [VMEM] * 2, [(piece, F32)] + [(piece, BF16)] * (chips - 1)
    )(col_keep, to_core(col_send, rows))
    parts_x = [to_chip(send_x[k - 1], rows, k) for k in across]

    norm = float((owned * rows * cols) ** -0.5)
    mine, bias_sum = call(
        functools.partial(col_sum_kernel, norm),
        [VMEM] * cols,
        [((half, width), F32), ((1, width), F32)],
        [pltpu.VMEM((cols,) + grads_shape, BF16)],
    )(grads, *(grad_parts[k] for k in range(1, cols)))
    theirs = to_core(mine, rows)
    x_piece = call(owned_sum_kernel, [VMEM] * (1 + chips), [(piece, BF16)], flops=LONG)(
        inv, own_x, *parts_x
    )
    output, grad_x, grad_w, grad_b = call(
        finish_kernel,
        [VMEM] * 5,
        [(piece, BF16), (piece, BF16), ((width, width), F32), ((1, width), F32)],
        [pltpu.SemaphoreType.DMA((5,))],
        place=pl.BlockSpec(memory_space=pl.ANY),
    )(out_piece, x_piece, mine, theirs, bias_sum)
    return (output, grad_x, grad_w, grad_b.reshape(width))


def solution(mesh):
    placed = (
        P(("row", "col"), None),
        P(("row", "col")),
        P(),
        P(),
        P(("row", "col"), None),
        P("row", "col", None),
        P("row", "col", None, None),
        P("row", "col"),
    )
    return jax.shard_map(
        per_device,
        mesh=mesh,
        in_specs=placed,
        out_specs=(P(("row", "col"), None), P(("row", "col"), None), P(), P()),
        check_vma=False,
    )
```

```python
import functools

import jax
import jax.numpy as jnp
from jax import lax
from jax.experimental import pallas as pl
from jax.experimental.pallas import tpu as pltpu
from jax.sharding import PartitionSpec as P

BLOCK = 128
CORES = 2
EXTRA = 16
LONG = 4_000_000_000
GROUP = 8
VMEM = pl.BlockSpec(memory_space=pltpu.VMEM)
SMEM = pl.BlockSpec(memory_space=pltpu.SMEM)
NT = (((1,), (1,)), ((), ()))
TN = (((0,), (0,)), ((), ()))
BF16 = jnp.bfloat16
F32 = jnp.float32


def is_power(n):
    return n & (n - 1) == 0


def target(n, i, k):
    return i ^ k if is_power(n) else (i + k) % n


def offset_to(n, me, other):
    return me ^ other if is_power(n) else lax.rem(other - me + n, n)


def offset_from(n, me, other):
    return me ^ other if is_power(n) else lax.rem(me - other + n, n)


def col_order(cols):
    return list(range(2, cols)) + [1]


def to_core(x, rows):
    return lax.ppermute(x, "row", [(i, i ^ 1) for i in range(rows)])


def to_chip(x, rows, k):
    chips = rows // CORES
    pairs = [
        (a * CORES + b, target(chips, a, k) * CORES + b)
        for a in range(chips)
        for b in range(CORES)
    ]
    return lax.ppermute(x, "row", pairs)


def to_col(x, cols, k):
    return lax.ppermute(x, "col", [(i, target(cols, i, k)) for i in range(cols)])


def spread_inv(degree_ref, width):
    inv = lax.rsqrt(degree_ref[...].astype(F32))
    owned = inv.shape[1]
    tall = jnp.broadcast_to(inv, (BLOCK, owned)).T
    return jnp.concatenate([tall] * (width // BLOCK), axis=1)


def scale_kernel(features_ref, degree_ref, out_ref, inv_ref):
    inv = spread_inv(degree_ref, features_ref.shape[1])
    inv_ref[...] = inv
    out_ref[...] = (features_ref[...].astype(F32) * inv).astype(BF16)


def group_of(slots):
    return GROUP if slots % GROUP == 0 else 1


def for_live(count, slots, body):
    group = group_of(slots)
    for start in range(0, slots, group):

        @pl.when(start < count)
        def _():
            for slot in range(start, start + group):
                body(slot)


def build_kernel(count_ref, edge_ref, bias_ref, blocks_ref, turned_ref, bias_out_ref):
    bias_out_ref[...] = bias_ref[...]
    slots, edges = edge_ref.shape[2], edge_ref.shape[3]
    node = lax.broadcasted_iota(jnp.int32, (BLOCK, edges), 0)

    count = count_ref[0, 0]
    group = group_of(slots)

    def build(s):
        edge = edge_ref[0, 0, pl.ds(s, 1), :]
        row_hot = jnp.where(node == edge // BLOCK, 1.0, 0.0).astype(BF16)
        col_hot = jnp.where(node == edge % BLOCK, 1.0, 0.0).astype(BF16)
        counts = lax.dot_general(row_hot, col_hot, NT, preferred_element_type=F32)
        block = jnp.where(s < count, counts, 0.0).astype(BF16)
        blocks_ref[s] = block
        turned_ref[s] = block.T

    def step(i, carry):
        for j in range(group):
            build(i * group + j)
        return carry

    lax.fori_loop(0, (count + group - 1) // group, step, 0)


def forward_kernel(rows, cols, pos_ref, count_ref, blocks_ref, near_ref, next_ref, *refs):
    own_ref, *send, gathered, acc = refs
    chips = rows // CORES
    row, col = lax.axis_index("row"), lax.axis_index("col")
    gathered[:chips] = near_ref[...]
    gathered[chips:] = next_ref[...]
    acc[...] = jnp.zeros_like(acc)
    positions = pos_ref[0]

    def add(s):
        p = positions[0, s]
        u, v = p // rows, lax.rem(p, rows)
        k = offset_from(chips, row // CORES, v // CORES)
        src = (lax.rem(v, CORES) ^ lax.rem(row, CORES)) * chips + k
        dst = offset_to(cols, col, u)
        acc[dst] += jnp.dot(blocks_ref[s], gathered[src], preferred_element_type=F32)

    for_live(count_ref[0, 0], blocks_ref.shape[0], add)
    own_ref[...] = acc[0]
    for k, ref in enumerate(send, 1):
        ref[...] = acc[k].astype(BF16)


def pack_bias(total, rows):
    head = total.astype(BF16)
    tail = (total - head.astype(F32)).astype(BF16)
    index = lax.broadcasted_iota(jnp.int32, (rows, total.shape[1]), 0)
    both = jnp.where(index == 0, head.astype(F32), jnp.where(index == 1, tail.astype(F32), 0.0))
    return both.astype(BF16)


def add_bias(packed):
    return jnp.sum(packed.astype(F32), axis=0, keepdims=True)


def pointwise_kernel(cols, weight_ref, bias_ref, cot_ref, inv_ref, *refs):
    own_ref, *parts = refs[:cols]
    out_ref, hidden_ref, keep_ref, bias_keep_ref, send_ref = refs[cols:]
    width = out_ref.shape[1]
    half = width // CORES
    core = lax.rem(lax.axis_index("row"), CORES)
    inv = inv_ref[...]
    total = own_ref[...]
    for ref in parts:
        total = total + ref[...].astype(F32)
    agg = (total * inv).astype(BF16)
    weight = weight_ref[...]
    preact = jnp.dot(agg, weight, preferred_element_type=F32) + bias_ref[...]
    sig = jax.nn.sigmoid(preact)
    out_ref[...] = (preact * sig).astype(BF16)
    grad_pre = (cot_ref[...].astype(F32) * sig * (1.0 + preact * (1.0 - sig))).astype(BF16)
    hidden = lax.dot_general(grad_pre, weight, NT, preferred_element_type=F32)
    hidden_ref[...] = (hidden * inv).astype(BF16)
    term = lax.dot_general(agg, grad_pre, TN, preferred_element_type=F32)
    low, high = term[:half], term[half:]
    first = core == 0
    keep_ref[...] = jnp.where(first, low, high)
    send_ref[:half] = jnp.where(first, high, low).astype(BF16)
    bias_sum = jnp.sum(grad_pre.astype(F32), axis=0, keepdims=True)
    bias_keep_ref[...] = bias_sum
    send_ref[half:] = pack_bias(bias_sum, EXTRA)


def pair_sum_kernel(keep_ref, bias_keep_ref, got_ref, out_ref):
    half = keep_ref.shape[0]
    out_ref[:half] = (keep_ref[...] + got_ref[:half].astype(F32)).astype(BF16)
    out_ref[half:] = pack_bias(bias_keep_ref[...] + add_bias(got_ref[half:]), EXTRA)


def total_of(n, me, offsets, refs, stage):
    for k, ref in zip(offsets, refs):
        owner = me ^ k if is_power(n) else lax.rem(me - k + n, n)
        stage[owner] = ref[...]
    half = stage.shape[1] - EXTRA
    grads, bias = stage[0, :half].astype(F32), add_bias(stage[0, half:])
    for i in range(1, n):
        grads = grads + stage[i, :half].astype(F32)
        bias = bias + add_bias(stage[i, half:])
    return grads, bias


def chip_sum_kernel(*refs):
    *parts, out_ref, stage = refs
    chip = lax.axis_index("row") // CORES
    grads, bias = total_of(len(parts), chip, range(len(parts)), parts, stage)
    half = grads.shape[0]
    out_ref[:half] = grads.astype(BF16)
    out_ref[half:] = pack_bias(bias, EXTRA)


def col_sum_kernel(norm, *refs):
    *parts, half_ref, bias_ref, stage = refs
    cols = len(parts)
    grads, bias = total_of(cols, lax.axis_index("col"), [0] + col_order(cols), parts, stage)
    half_ref[...] = grads * norm
    bias_ref[...] = bias * norm


def collect_kernel(*refs):
    *parts, out_ref = refs
    for n, ref in enumerate(parts):
        out_ref[n] = ref[...]


def backward_kernel(rows, cols, pos_ref, count_ref, turned_ref, *refs):
    parts = refs[:cols]
    keep_ref, send_ref, hidden, acc = refs[cols:]
    chips = rows // CORES
    row, col = lax.axis_index("row"), lax.axis_index("col")
    for k, ref in zip([0] + col_order(cols), parts):
        hidden[k] = ref[...]
    acc[...] = jnp.zeros_like(acc)
    positions = pos_ref[0]

    def add(s):
        p = positions[0, s]
        u, v = p // rows, lax.rem(p, rows)
        src = offset_from(cols, col, u)
        k = offset_to(chips, row // CORES, v // CORES)
        dst = (lax.rem(v, CORES) ^ lax.rem(row, CORES)) * chips + k
        acc[dst] += jnp.dot(turned_ref[s], hidden[src], preferred_element_type=F32)

    for_live(count_ref[0, 0], turned_ref.shape[0], add)
    keep_ref[...] = acc[:chips]
    send_ref[...] = acc[chips:].astype(BF16)


def merge_kernel(keep_ref, got_ref, own_ref, *send):
    own_ref[...] = keep_ref[0] + got_ref[0].astype(F32)
    for k, ref in enumerate(send, 1):
        ref[...] = (keep_ref[k] + got_ref[k].astype(F32)).astype(BF16)


def owned_sum_kernel(inv_ref, own_ref, *refs):
    *parts, out_ref = refs
    total = own_ref[...]
    for ref in parts:
        total = total + ref[...].astype(F32)
    out_ref[...] = (total * inv_ref[...]).astype(BF16)


def finish_kernel(out_ref, x_ref, mine_ref, theirs_ref, bias_ref, *refs):
    output_ref, grad_x_ref, grad_w_ref, grad_b_ref, sems = refs
    half = mine_ref.shape[0]
    core = lax.rem(lax.axis_index("row"), CORES)
    moves = [
        (mine_ref, grad_w_ref.at[pl.ds(pl.multiple_of(core * half, half), half)]),
        (theirs_ref, grad_w_ref.at[pl.ds(pl.multiple_of((1 - core) * half, half), half)]),
        (out_ref, output_ref),
        (x_ref, grad_x_ref),
        (bias_ref, grad_b_ref),
    ]
    copies = [pltpu.make_async_copy(*move, sems.at[i]) for i, move in enumerate(moves)]
    for copy in copies:
        copy.start()
    for copy in copies:
        copy.wait()


def call(kernel, specs, outs, scratch=(), flops=1_000_000, place=VMEM):
    shapes = [jax.ShapeDtypeStruct(shape, dtype) for shape, dtype in outs]
    single = len(shapes) == 1
    return pl.pallas_call(
        kernel,
        out_shape=shapes[0] if single else tuple(shapes),
        in_specs=specs,
        out_specs=place if single else tuple(place for _ in shapes),
        scratch_shapes=scratch,
        compiler_params=pltpu.CompilerParams(vmem_limit_bytes=40 * 1024 * 1024),
        cost_estimate=pl.CostEstimate(flops=flops, bytes_accessed=1_000_000, transcendentals=0),
    )


def per_device(features, degree, weight, bias_vector, cotangent, block_pos, edge_pos, block_count):
    owned, width = features.shape
    rows, cols = lax.axis_size("row"), lax.axis_size("col")
    chips = rows // CORES
    slots = block_pos.shape[2]
    half = width // CORES
    piece = (owned, width)
    grads_shape = (half + EXTRA, width)
    degree = degree.reshape(1, owned)
    bias_vector = bias_vector.reshape(1, width)

    scaled, inv = call(scale_kernel, [VMEM, VMEM], [(piece, BF16), (piece, F32)])(features, degree)
    near = [to_chip(scaled, rows, k) for k in range(1, chips)]
    blocks, turned, bias_vector = call(
        build_kernel,
        [SMEM, VMEM, VMEM],
        [((slots, BLOCK, BLOCK), BF16)] * 2 + [((1, width), F32)],
        flops=LONG,
    )(block_count, edge_pos, bias_vector)
    blocks, *near = lax.optimization_barrier((blocks, *near))
    near = call(collect_kernel, [VMEM] * chips, [((chips,) + piece, BF16)])(scaled, *near)

    own, *send = call(
        functools.partial(forward_kernel, rows, cols),
        [VMEM, SMEM, VMEM, VMEM, VMEM],
        [(piece, F32)] + [(piece, BF16)] * (cols - 1),
        [pltpu.VMEM((rows,) + piece, BF16), pltpu.VMEM((cols,) + piece, F32)],
    )(block_pos, block_count, blocks, near, to_core(near, rows))
    order = col_order(cols)
    parts = [to_col(send[k - 1], cols, k) for k in order]

    out_piece, hidden, keep, bias_keep, half_send = call(
        functools.partial(pointwise_kernel, cols),
        [VMEM] * (4 + cols),
        [(piece, BF16), (piece, BF16), ((half, width), F32), ((1, width), F32), (grads_shape, BF16)],
    )(weight, bias_vector, cotangent, inv, own, *parts)

    hidden_parts = [to_col(hidden, cols, k) for k in order]
    grads = call(pair_sum_kernel, [VMEM] * 3, [(grads_shape, BF16)])(
        keep, bias_keep, to_core(half_send, rows)
    )
    across = range(chips - 1, 0, -1)
    grad_parts = {k: to_chip(grads, rows, k) for k in across}
    grads = call(
        chip_sum_kernel,
        [VMEM] * chips,
        [(grads_shape, BF16)],
        [pltpu.VMEM((chips,) + grads_shape, BF16)],
    )(grads, *(grad_parts[k] for k in range(1, chips)))

    col_keep, col_send = call(
        functools.partial(backward_kernel, rows, cols),
        [VMEM, SMEM, VMEM] + [VMEM] * cols,
        [((chips,) + piece, F32), ((chips,) + piece, BF16)],
        [pltpu.VMEM((cols,) + piece, BF16), pltpu.VMEM((rows,) + piece, F32)],
        flops=LONG,
    )(block_pos, block_count, turned, hidden, *hidden_parts)
    col_send, grads = lax.optimization_barrier((col_send, grads))
    grad_parts = [to_col(grads, cols, k) for k in order]
    own_x, *send_x = call(
        merge_kernel, [VMEM] * 2, [(piece, F32)] + [(piece, BF16)] * (chips - 1)
    )(col_keep, to_core(col_send, rows))
    parts_x = [to_chip(send_x[k - 1], rows, k) for k in across]

    norm = float((owned * rows * cols) ** -0.5)
    mine, bias_sum = call(
        functools.partial(col_sum_kernel, norm),
        [VMEM] * cols,
        [((half, width), F32), ((1, width), F32)],
        [pltpu.VMEM((cols,) + grads_shape, BF16)],
    )(grads, *grad_parts)
    theirs = to_core(mine, rows)
    x_piece = call(owned_sum_kernel, [VMEM] * (1 + chips), [(piece, BF16)], flops=LONG)(
        inv, own_x, *parts_x
    )
    output, grad_x, grad_w, grad_b = call(
        finish_kernel,
        [VMEM] * 5,
        [(piece, BF16), (piece, BF16), ((width, width), F32), ((1, width), F32)],
        [pltpu.SemaphoreType.DMA((5,))],
        place=pl.BlockSpec(memory_space=pl.ANY),
    )(out_piece, x_piece, mine, theirs, bias_sum)
    return (output, grad_x, grad_w, grad_b.reshape(width))


def solution(mesh):
    placed = (
        P(("row", "col"), None),
        P(("row", "col")),
        P(),
        P(),
        P(("row", "col"), None),
        P("row", "col", None),
        P("row", "col", None, None),
        P("row", "col"),
    )
    return jax.shard_map(
        per_device,
        mesh=mesh,
        in_specs=placed,
        out_specs=(P(("row", "col"), None), P(("row", "col"), None), P(), P()),
        check_vma=False,
    )
```

```python
import functools

import jax
import jax.numpy as jnp
from jax import lax
from jax.experimental import pallas as pl
from jax.experimental.pallas import tpu as pltpu
from jax.sharding import PartitionSpec as P

BLOCK = 128
CORES = 2
EXTRA = 16
LONG = 4_000_000_000
GROUP = 8
VMEM = pl.BlockSpec(memory_space=pltpu.VMEM)
SMEM = pl.BlockSpec(memory_space=pltpu.SMEM)
NT = (((1,), (1,)), ((), ()))
TN = (((0,), (0,)), ((), ()))
BF16 = jnp.bfloat16
F32 = jnp.float32


def is_power(n):
    return n & (n - 1) == 0


def target(n, i, k):
    return i ^ k if is_power(n) else (i + k) % n


def offset_to(n, me, other):
    return me ^ other if is_power(n) else lax.rem(other - me + n, n)


def offset_from(n, me, other):
    return me ^ other if is_power(n) else lax.rem(me - other + n, n)


def col_order(cols):
    return list(range(2, cols)) + [1]


def to_core(x, rows):
    return lax.ppermute(x, "row", [(i, i ^ 1) for i in range(rows)])


def to_chip(x, rows, k):
    chips = rows // CORES
    pairs = [
        (a * CORES + b, target(chips, a, k) * CORES + b)
        for a in range(chips)
        for b in range(CORES)
    ]
    return lax.ppermute(x, "row", pairs)


def to_col(x, cols, k):
    return lax.ppermute(x, "col", [(i, target(cols, i, k)) for i in range(cols)])


def spread_inv(degree_ref, width):
    inv = lax.rsqrt(degree_ref[...].astype(F32))
    owned = inv.shape[1]
    tall = jnp.broadcast_to(inv, (BLOCK, owned)).T
    return jnp.concatenate([tall] * (width // BLOCK), axis=1)


def scale_kernel(features_ref, degree_ref, out_ref, inv_ref):
    inv = spread_inv(degree_ref, features_ref.shape[1])
    inv_ref[...] = inv
    out_ref[...] = (features_ref[...].astype(F32) * inv).astype(BF16)


def group_of(slots):
    return GROUP if slots % GROUP == 0 else 1


def for_live(count, slots, body):
    group = group_of(slots)
    for start in range(0, slots, group):

        @pl.when(start < count)
        def _():
            for slot in range(start, start + group):
                body(slot)


def build_kernel(count_ref, edge_ref, bias_ref, blocks_ref, turned_ref, bias_out_ref):
    bias_out_ref[...] = bias_ref[...]
    slots, edges = edge_ref.shape[2], edge_ref.shape[3]
    node = lax.broadcasted_iota(jnp.int32, (BLOCK, edges), 0)

    count = count_ref[0, 0]
    group = group_of(slots)

    def build(s):
        edge = edge_ref[0, 0, pl.ds(s, 1), :]
        row_hot = jnp.where(node == edge // BLOCK, 1.0, 0.0).astype(BF16)
        col_hot = jnp.where(node == edge % BLOCK, 1.0, 0.0).astype(BF16)
        counts = lax.dot_general(row_hot, col_hot, NT, preferred_element_type=F32)
        block = jnp.where(s < count, counts, 0.0).astype(BF16)
        blocks_ref[s] = block
        turned_ref[s] = block.T

    def step(i, carry):
        for j in range(group):
            build(i * group + j)
        return carry

    lax.fori_loop(0, (count + group - 1) // group, step, 0)


def forward_kernel(rows, cols, pos_ref, count_ref, blocks_ref, near_ref, next_ref, *refs):
    own_ref, *send, gathered, acc = refs
    chips = rows // CORES
    row, col = lax.axis_index("row"), lax.axis_index("col")
    gathered[:chips] = near_ref[...]
    gathered[chips:] = next_ref[...]
    acc[...] = jnp.zeros_like(acc)
    positions = pos_ref[0]

    def add(s):
        p = positions[0, s]
        u, v = p // rows, lax.rem(p, rows)
        k = offset_from(chips, row // CORES, v // CORES)
        src = (lax.rem(v, CORES) ^ lax.rem(row, CORES)) * chips + k
        dst = offset_to(cols, col, u)
        acc[dst] += jnp.dot(blocks_ref[s], gathered[src], preferred_element_type=F32)

    for_live(count_ref[0, 0], blocks_ref.shape[0], add)
    own_ref[...] = acc[0]
    for k, ref in enumerate(send, 1):
        ref[...] = acc[k].astype(BF16)


def pack_bias(total, rows):
    head = total.astype(BF16)
    tail = (total - head.astype(F32)).astype(BF16)
    index = lax.broadcasted_iota(jnp.int32, (rows, total.shape[1]), 0)
    both = jnp.where(index == 0, head.astype(F32), jnp.where(index == 1, tail.astype(F32), 0.0))
    return both.astype(BF16)


def add_bias(packed):
    return jnp.sum(packed.astype(F32), axis=0, keepdims=True)


def pointwise_kernel(cols, weight_ref, bias_ref, cot_ref, inv_ref, *refs):
    own_ref, *parts = refs[:cols]
    out_ref, hidden_ref, keep_ref, bias_keep_ref, send_ref = refs[cols:]
    width = out_ref.shape[1]
    half = width // CORES
    core = lax.rem(lax.axis_index("row"), CORES)
    inv = inv_ref[...]
    total = own_ref[...]
    for ref in parts:
        total = total + ref[...].astype(F32)
    agg = (total * inv).astype(BF16)
    weight = weight_ref[...]
    preact = jnp.dot(agg, weight, preferred_element_type=F32) + bias_ref[...]
    sig = jax.nn.sigmoid(preact)
    out_ref[...] = (preact * sig).astype(BF16)
    grad_pre = (cot_ref[...].astype(F32) * sig * (1.0 + preact * (1.0 - sig))).astype(BF16)
    hidden = lax.dot_general(grad_pre, weight, NT, preferred_element_type=F32)
    hidden_ref[...] = (hidden * inv).astype(BF16)
    term = lax.dot_general(agg, grad_pre, TN, preferred_element_type=F32)
    low, high = term[:half], term[half:]
    first = core == 0
    keep_ref[...] = jnp.where(first, low, high)
    send_ref[:half] = jnp.where(first, high, low).astype(BF16)
    bias_sum = jnp.sum(grad_pre.astype(F32), axis=0, keepdims=True)
    bias_keep_ref[...] = bias_sum
    send_ref[half:] = pack_bias(bias_sum, EXTRA)


def pair_sum_kernel(keep_ref, bias_keep_ref, got_ref, out_ref):
    half = keep_ref.shape[0]
    out_ref[:half] = (keep_ref[...] + got_ref[:half].astype(F32)).astype(BF16)
    out_ref[half:] = pack_bias(bias_keep_ref[...] + add_bias(got_ref[half:]), EXTRA)


def total_of(n, me, offsets, refs, stage):
    for k, ref in zip(offsets, refs):
        owner = me ^ k if is_power(n) else lax.rem(me - k + n, n)
        stage[owner] = ref[...]
    half = stage.shape[1] - EXTRA
    grads, bias = stage[0, :half].astype(F32), add_bias(stage[0, half:])
    for i in range(1, n):
        grads = grads + stage[i, :half].astype(F32)
        bias = bias + add_bias(stage[i, half:])
    return grads, bias


def chip_sum_kernel(*refs):
    *parts, out_ref, stage = refs
    chip = lax.axis_index("row") // CORES
    grads, bias = total_of(len(parts), chip, range(len(parts)), parts, stage)
    half = grads.shape[0]
    out_ref[:half] = grads.astype(BF16)
    out_ref[half:] = pack_bias(bias, EXTRA)


def col_sum_kernel(norm, *refs):
    *parts, half_ref, bias_ref, stage = refs
    cols = len(parts)
    grads, bias = total_of(cols, lax.axis_index("col"), [0] + col_order(cols)[::-1], parts, stage)
    half_ref[...] = grads * norm
    bias_ref[...] = bias * norm


def collect_kernel(*refs):
    *parts, out_ref = refs
    for n, ref in enumerate(parts):
        out_ref[n] = ref[...]


def backward_kernel(rows, cols, pos_ref, count_ref, turned_ref, *refs):
    parts = refs[:cols]
    keep_ref, send_ref, hidden, acc = refs[cols:]
    chips = rows // CORES
    row, col = lax.axis_index("row"), lax.axis_index("col")
    for k, ref in zip([0] + col_order(cols)[::-1], parts):
        hidden[k] = ref[...]
    acc[...] = jnp.zeros_like(acc)
    positions = pos_ref[0]

    def add(s):
        p = positions[0, s]
        u, v = p // rows, lax.rem(p, rows)
        src = offset_from(cols, col, u)
        k = offset_to(chips, row // CORES, v // CORES)
        dst = (lax.rem(v, CORES) ^ lax.rem(row, CORES)) * chips + k
        acc[dst] += jnp.dot(turned_ref[s], hidden[src], preferred_element_type=F32)

    for_live(count_ref[0, 0], turned_ref.shape[0], add)
    keep_ref[...] = acc[:chips]
    send_ref[...] = acc[chips:].astype(BF16)


def merge_kernel(keep_ref, got_ref, own_ref, *send):
    own_ref[...] = keep_ref[0] + got_ref[0].astype(F32)
    for k, ref in enumerate(send, 1):
        ref[...] = (keep_ref[k] + got_ref[k].astype(F32)).astype(BF16)


def owned_sum_kernel(inv_ref, own_ref, *refs):
    *parts, out_ref = refs
    total = own_ref[...]
    for ref in parts:
        total = total + ref[...].astype(F32)
    out_ref[...] = (total * inv_ref[...]).astype(BF16)


def finish_kernel(out_ref, x_ref, mine_ref, theirs_ref, bias_ref, *refs):
    output_ref, grad_x_ref, grad_w_ref, grad_b_ref, sems = refs
    half = mine_ref.shape[0]
    core = lax.rem(lax.axis_index("row"), CORES)
    moves = [
        (mine_ref, grad_w_ref.at[pl.ds(pl.multiple_of(core * half, half), half)]),
        (theirs_ref, grad_w_ref.at[pl.ds(pl.multiple_of((1 - core) * half, half), half)]),
        (out_ref, output_ref),
        (x_ref, grad_x_ref),
        (bias_ref, grad_b_ref),
    ]
    copies = [pltpu.make_async_copy(*move, sems.at[i]) for i, move in enumerate(moves)]
    for copy in copies:
        copy.start()
    for copy in copies:
        copy.wait()


def call(kernel, specs, outs, scratch=(), flops=1_000_000, place=VMEM):
    shapes = [jax.ShapeDtypeStruct(shape, dtype) for shape, dtype in outs]
    single = len(shapes) == 1
    return pl.pallas_call(
        kernel,
        out_shape=shapes[0] if single else tuple(shapes),
        in_specs=specs,
        out_specs=place if single else tuple(place for _ in shapes),
        scratch_shapes=scratch,
        compiler_params=pltpu.CompilerParams(vmem_limit_bytes=40 * 1024 * 1024),
        cost_estimate=pl.CostEstimate(flops=flops, bytes_accessed=1_000_000, transcendentals=0),
    )


def per_device(features, degree, weight, bias_vector, cotangent, block_pos, edge_pos, block_count):
    owned, width = features.shape
    rows, cols = lax.axis_size("row"), lax.axis_size("col")
    chips = rows // CORES
    slots = block_pos.shape[2]
    half = width // CORES
    piece = (owned, width)
    grads_shape = (half + EXTRA, width)
    degree = degree.reshape(1, owned)
    bias_vector = bias_vector.reshape(1, width)

    scaled, inv = call(scale_kernel, [VMEM, VMEM], [(piece, BF16), (piece, F32)])(features, degree)
    near = [to_chip(scaled, rows, k) for k in range(1, chips)]
    blocks, turned, bias_vector = call(
        build_kernel,
        [SMEM, VMEM, VMEM],
        [((slots, BLOCK, BLOCK), BF16)] * 2 + [((1, width), F32)],
        flops=LONG,
    )(block_count, edge_pos, bias_vector)
    blocks, *near = lax.optimization_barrier((blocks, *near))
    near = call(collect_kernel, [VMEM] * chips, [((chips,) + piece, BF16)])(scaled, *near)

    own, *send = call(
        functools.partial(forward_kernel, rows, cols),
        [VMEM, SMEM, VMEM, VMEM, VMEM],
        [(piece, F32)] + [(piece, BF16)] * (cols - 1),
        [pltpu.VMEM((rows,) + piece, BF16), pltpu.VMEM((cols,) + piece, F32)],
    )(block_pos, block_count, blocks, near, to_core(near, rows))
    order = col_order(cols)
    parts = [to_col(send[k - 1], cols, k) for k in order]

    out_piece, hidden, keep, bias_keep, half_send = call(
        functools.partial(pointwise_kernel, cols),
        [VMEM] * (4 + cols),
        [(piece, BF16), (piece, BF16), ((half, width), F32), ((1, width), F32), (grads_shape, BF16)],
    )(weight, bias_vector, cotangent, inv, own, *parts)

    hidden_parts = [to_col(hidden, cols, k) for k in order[::-1]]
    grads = call(pair_sum_kernel, [VMEM] * 3, [(grads_shape, BF16)])(
        keep, bias_keep, to_core(half_send, rows)
    )
    across = range(chips - 1, 0, -1)
    grad_parts = {k: to_chip(grads, rows, k) for k in across}
    grads = call(
        chip_sum_kernel,
        [VMEM] * chips,
        [(grads_shape, BF16)],
        [pltpu.VMEM((chips,) + grads_shape, BF16)],
    )(grads, *(grad_parts[k] for k in range(1, chips)))

    col_keep, col_send = call(
        functools.partial(backward_kernel, rows, cols),
        [VMEM, SMEM, VMEM] + [VMEM] * cols,
        [((chips,) + piece, F32), ((chips,) + piece, BF16)],
        [pltpu.VMEM((cols,) + piece, BF16), pltpu.VMEM((rows,) + piece, F32)],
        flops=LONG,
    )(block_pos, block_count, turned, hidden, *hidden_parts)
    col_send, grads = lax.optimization_barrier((col_send, grads))
    grad_parts = [to_col(grads, cols, k) for k in order[::-1]]
    own_x, *send_x = call(
        merge_kernel, [VMEM] * 2, [(piece, F32)] + [(piece, BF16)] * (chips - 1)
    )(col_keep, to_core(col_send, rows))
    parts_x = [to_chip(send_x[k - 1], rows, k) for k in across]

    norm = float((owned * rows * cols) ** -0.5)
    mine, bias_sum = call(
        functools.partial(col_sum_kernel, norm),
        [VMEM] * cols,
        [((half, width), F32), ((1, width), F32)],
        [pltpu.VMEM((cols,) + grads_shape, BF16)],
    )(grads, *grad_parts)
    theirs = to_core(mine, rows)
    x_piece = call(owned_sum_kernel, [VMEM] * (1 + chips), [(piece, BF16)], flops=LONG)(
        inv, own_x, *parts_x
    )
    output, grad_x, grad_w, grad_b = call(
        finish_kernel,
        [VMEM] * 5,
        [(piece, BF16), (piece, BF16), ((width, width), F32), ((1, width), F32)],
        [pltpu.SemaphoreType.DMA((5,))],
        place=pl.BlockSpec(memory_space=pl.ANY),
    )(out_piece, x_piece, mine, theirs, bias_sum)
    return (output, grad_x, grad_w, grad_b.reshape(width))


def solution(mesh):
    placed = (
        P(("row", "col"), None),
        P(("row", "col")),
        P(),
        P(),
        P(("row", "col"), None),
        P("row", "col", None),
        P("row", "col", None, None),
        P("row", "col"),
    )
    return jax.shard_map(
        per_device,
        mesh=mesh,
        in_specs=placed,
        out_specs=(P(("row", "col"), None), P(("row", "col"), None), P(), P()),
        check_vma=False,
    )
```

```python
import functools

import jax
import jax.numpy as jnp
from jax import lax
from jax.experimental import pallas as pl
from jax.experimental.pallas import tpu as pltpu
from jax.sharding import PartitionSpec as P

BLOCK = 128
CORES = 2
EXTRA = 16
LONG = 4_000_000_000
GROUP = 8
VMEM = pl.BlockSpec(memory_space=pltpu.VMEM)
SMEM = pl.BlockSpec(memory_space=pltpu.SMEM)
NT = (((1,), (1,)), ((), ()))
TN = (((0,), (0,)), ((), ()))
BF16 = jnp.bfloat16
F32 = jnp.float32


def is_power(n):
    return n & (n - 1) == 0


def target(n, i, k):
    return i ^ k if is_power(n) else (i + k) % n


def offset_to(n, me, other):
    return me ^ other if is_power(n) else lax.rem(other - me + n, n)


def offset_from(n, me, other):
    return me ^ other if is_power(n) else lax.rem(me - other + n, n)


def to_core(x, rows):
    return lax.ppermute(x, "row", [(i, i ^ 1) for i in range(rows)])


def to_chip(x, rows, k):
    chips = rows // CORES
    pairs = [
        (a * CORES + b, target(chips, a, k) * CORES + b)
        for a in range(chips)
        for b in range(CORES)
    ]
    return lax.ppermute(x, "row", pairs)


def to_col(x, cols, k):
    return lax.ppermute(x, "col", [(i, target(cols, i, k)) for i in range(cols)])


def spread_inv(degree_ref, width):
    inv = lax.rsqrt(degree_ref[...].astype(F32))
    owned = inv.shape[1]
    tall = jnp.broadcast_to(inv, (BLOCK, owned)).T
    return jnp.concatenate([tall] * (width // BLOCK), axis=1)


def scale_kernel(features_ref, degree_ref, out_ref, inv_ref):
    inv = spread_inv(degree_ref, features_ref.shape[1])
    inv_ref[...] = inv
    out_ref[...] = (features_ref[...].astype(F32) * inv).astype(BF16)


def group_of(slots):
    return GROUP if slots % GROUP == 0 else 1


def for_live(count, slots, body):
    group = group_of(slots)
    for start in range(0, slots, group):

        @pl.when(start < count)
        def _():
            for slot in range(start, start + group):
                body(slot)


def build_kernel(count_ref, edge_ref, bias_ref, blocks_ref, turned_ref, bias_out_ref):
    bias_out_ref[...] = bias_ref[...]
    slots, edges = edge_ref.shape[2], edge_ref.shape[3]
    node = lax.broadcasted_iota(jnp.int32, (BLOCK, edges), 0)

    count = count_ref[0, 0]
    group = group_of(slots)

    def build(s):
        edge = edge_ref[0, 0, pl.ds(s, 1), :]
        row_hot = jnp.where(node == edge // BLOCK, 1.0, 0.0).astype(BF16)
        col_hot = jnp.where(node == edge % BLOCK, 1.0, 0.0).astype(BF16)
        counts = lax.dot_general(row_hot, col_hot, NT, preferred_element_type=F32)
        block = jnp.where(s < count, counts, 0.0).astype(BF16)
        blocks_ref[s] = block
        turned_ref[s] = block.T

    def step(i, carry):
        for j in range(group):
            build(i * group + j)
        return carry

    lax.fori_loop(0, (count + group - 1) // group, step, 0)


def forward_kernel(rows, cols, pos_ref, count_ref, blocks_ref, near_ref, next_ref, *refs):
    own_ref, *send, gathered, acc = refs
    chips = rows // CORES
    row, col = lax.axis_index("row"), lax.axis_index("col")
    gathered[:chips] = near_ref[...]
    gathered[chips:] = next_ref[...]
    acc[...] = jnp.zeros_like(acc)
    positions = pos_ref[0]

    def add(s):
        p = positions[0, s]
        u, v = p // rows, lax.rem(p, rows)
        k = offset_from(chips, row // CORES, v // CORES)
        src = (lax.rem(v, CORES) ^ lax.rem(row, CORES)) * chips + k
        dst = offset_to(cols, col, u)
        acc[dst] += jnp.dot(blocks_ref[s], gathered[src], preferred_element_type=F32)

    for_live(count_ref[0, 0], blocks_ref.shape[0], add)
    own_ref[...] = acc[0]
    for k, ref in enumerate(send, 1):
        ref[...] = acc[k].astype(BF16)


def pack_bias(total, rows):
    head = total.astype(BF16)
    tail = (total - head.astype(F32)).astype(BF16)
    index = lax.broadcasted_iota(jnp.int32, (rows, total.shape[1]), 0)
    both = jnp.where(index == 0, head.astype(F32), jnp.where(index == 1, tail.astype(F32), 0.0))
    return both.astype(BF16)


def add_bias(packed):
    return jnp.sum(packed.astype(F32), axis=0, keepdims=True)


def pointwise_kernel(cols, weight_ref, bias_ref, cot_ref, inv_ref, *refs):
    own_ref, *parts = refs[:cols]
    out_ref, hidden_ref, keep_ref, bias_keep_ref, send_ref = refs[cols:]
    width = out_ref.shape[1]
    half = width // CORES
    core = lax.rem(lax.axis_index("row"), CORES)
    inv = inv_ref[...]
    total = own_ref[...]
    for ref in parts:
        total = total + ref[...].astype(F32)
    agg = (total * inv).astype(BF16)
    weight = weight_ref[...]
    preact = jnp.dot(agg, weight, preferred_element_type=F32) + bias_ref[...]
    sig = jax.nn.sigmoid(preact)
    out_ref[...] = (preact * sig).astype(BF16)
    grad_pre = (cot_ref[...].astype(F32) * sig * (1.0 + preact * (1.0 - sig))).astype(BF16)
    hidden = lax.dot_general(grad_pre, weight, NT, preferred_element_type=F32)
    hidden_ref[...] = (hidden * inv).astype(BF16)
    term = lax.dot_general(agg, grad_pre, TN, preferred_element_type=F32)
    low, high = term[:half], term[half:]
    first = core == 0
    keep_ref[...] = jnp.where(first, low, high)
    send_ref[:half] = jnp.where(first, high, low).astype(BF16)
    bias_sum = jnp.sum(grad_pre.astype(F32), axis=0, keepdims=True)
    bias_keep_ref[...] = bias_sum
    send_ref[half:] = pack_bias(bias_sum, EXTRA)


def pair_sum_kernel(keep_ref, bias_keep_ref, got_ref, out_ref):
    half = keep_ref.shape[0]
    out_ref[:half] = (keep_ref[...] + got_ref[:half].astype(F32)).astype(BF16)
    out_ref[half:] = pack_bias(bias_keep_ref[...] + add_bias(got_ref[half:]), EXTRA)


def total_of(n, me, refs, stage):
    for k, ref in enumerate(refs):
        owner = me ^ k if is_power(n) else lax.rem(me - k + n, n)
        stage[owner] = ref[...]
    half = stage.shape[1] - EXTRA
    grads, bias = stage[0, :half].astype(F32), add_bias(stage[0, half:])
    for i in range(1, n):
        grads = grads + stage[i, :half].astype(F32)
        bias = bias + add_bias(stage[i, half:])
    return grads, bias


def chip_sum_kernel(*refs):
    *parts, out_ref, stage = refs
    chip = lax.axis_index("row") // CORES
    grads, bias = total_of(len(parts), chip, parts, stage)
    half = grads.shape[0]
    out_ref[:half] = grads.astype(BF16)
    out_ref[half:] = pack_bias(bias, EXTRA)


def col_sum_kernel(norm, *refs):
    *parts, half_ref, bias_ref, stage = refs
    grads, bias = total_of(len(parts), lax.axis_index("col"), parts, stage)
    half_ref[...] = grads * norm
    bias_ref[...] = bias * norm


def collect_kernel(*refs):
    *parts, out_ref = refs
    for n, ref in enumerate(parts):
        out_ref[n] = ref[...]


def backward_kernel(rows, cols, pos_ref, count_ref, turned_ref, *refs):
    own_ref, next_ref, far_ref, keep_ref, send_ref, hidden, acc = refs
    chips = rows // CORES
    row, col = lax.axis_index("row"), lax.axis_index("col")
    hidden[0] = own_ref[...]
    hidden[1] = next_ref[...]
    hidden[2:] = far_ref[...]
    acc[...] = jnp.zeros_like(acc)
    positions = pos_ref[0]

    def add(s):
        p = positions[0, s]
        u, v = p // rows, lax.rem(p, rows)
        src = offset_from(cols, col, u)
        k = offset_to(chips, row // CORES, v // CORES)
        dst = (lax.rem(v, CORES) ^ lax.rem(row, CORES)) * chips + k
        acc[dst] += jnp.dot(turned_ref[s], hidden[src], preferred_element_type=F32)

    for_live(count_ref[0, 0], turned_ref.shape[0], add)
    keep_ref[...] = acc[:chips]
    send_ref[...] = acc[chips:].astype(BF16)


def merge_kernel(keep_ref, got_ref, own_ref, *send):
    own_ref[...] = keep_ref[0] + got_ref[0].astype(F32)
    for k, ref in enumerate(send, 1):
        ref[...] = (keep_ref[k] + got_ref[k].astype(F32)).astype(BF16)


def owned_sum_kernel(inv_ref, own_ref, *refs):
    *parts, out_ref = refs
    total = own_ref[...]
    for ref in parts:
        total = total + ref[...].astype(F32)
    out_ref[...] = (total * inv_ref[...]).astype(BF16)


def finish_kernel(out_ref, x_ref, mine_ref, theirs_ref, bias_ref, *refs):
    output_ref, grad_x_ref, grad_w_ref, grad_b_ref, sems = refs
    half = mine_ref.shape[0]
    core = lax.rem(lax.axis_index("row"), CORES)
    moves = [
        (mine_ref, grad_w_ref.at[pl.ds(pl.multiple_of(core * half, half), half)]),
        (theirs_ref, grad_w_ref.at[pl.ds(pl.multiple_of((1 - core) * half, half), half)]),
        (out_ref, output_ref),
        (x_ref, grad_x_ref),
        (bias_ref, grad_b_ref),
    ]
    copies = [pltpu.make_async_copy(*move, sems.at[i]) for i, move in enumerate(moves)]
    for copy in copies:
        copy.start()
    for copy in copies:
        copy.wait()


def call(kernel, specs, outs, scratch=(), flops=1_000_000, place=VMEM):
    shapes = [jax.ShapeDtypeStruct(shape, dtype) for shape, dtype in outs]
    single = len(shapes) == 1
    return pl.pallas_call(
        kernel,
        out_shape=shapes[0] if single else tuple(shapes),
        in_specs=specs,
        out_specs=place if single else tuple(place for _ in shapes),
        scratch_shapes=scratch,
        compiler_params=pltpu.CompilerParams(vmem_limit_bytes=40 * 1024 * 1024),
        cost_estimate=pl.CostEstimate(flops=flops, bytes_accessed=1_000_000, transcendentals=0),
    )


def per_device(features, degree, weight, bias_vector, cotangent, block_pos, edge_pos, block_count):
    owned, width = features.shape
    rows, cols = lax.axis_size("row"), lax.axis_size("col")
    chips = rows // CORES
    slots = block_pos.shape[2]
    half = width // CORES
    piece = (owned, width)
    grads_shape = (half + EXTRA, width)
    degree = degree.reshape(1, owned)
    bias_vector = bias_vector.reshape(1, width)

    scaled, inv = call(scale_kernel, [VMEM, VMEM], [(piece, BF16), (piece, F32)])(features, degree)
    near = [to_chip(scaled, rows, k) for k in range(1, chips)]
    blocks, turned, bias_vector = call(
        build_kernel,
        [SMEM, VMEM, VMEM],
        [((slots, BLOCK, BLOCK), BF16)] * 2 + [((1, width), F32)],
        flops=LONG,
    )(block_count, edge_pos, bias_vector)
    blocks, *near = lax.optimization_barrier((blocks, *near))
    near = call(collect_kernel, [VMEM] * chips, [((chips,) + piece, BF16)])(scaled, *near)

    own, *send = call(
        functools.partial(forward_kernel, rows, cols),
        [VMEM, SMEM, VMEM, VMEM, VMEM],
        [(piece, F32)] + [(piece, BF16)] * (cols - 1),
        [pltpu.VMEM((rows,) + piece, BF16), pltpu.VMEM((cols,) + piece, F32)],
    )(block_pos, block_count, blocks, near, to_core(near, rows))
    order = list(range(2, cols)) + [1]
    parts = [to_col(send[k - 1], cols, k) for k in order]

    out_piece, hidden, keep, bias_keep, half_send = call(
        functools.partial(pointwise_kernel, cols),
        [VMEM] * (4 + cols),
        [(piece, BF16), (piece, BF16), ((half, width), F32), ((1, width), F32), (grads_shape, BF16)],
    )(weight, bias_vector, cotangent, inv, own, *parts)

    far = [to_col(hidden, cols, k) for k in range(2, cols)]
    grads = call(pair_sum_kernel, [VMEM] * 3, [(grads_shape, BF16)])(
        keep, bias_keep, to_core(half_send, rows)
    )
    nearby, grads = lax.optimization_barrier((hidden, grads))
    next_to = to_col(nearby, cols, 1)
    far = call(collect_kernel, [VMEM] * len(far), [((cols - 2,) + piece, BF16)], flops=LONG)(*far)
    across = range(chips - 1, 0, -1)
    grad_parts = {k: to_chip(grads, rows, k) for k in across}
    grads, far = lax.optimization_barrier((grads, far))
    grads = call(
        chip_sum_kernel,
        [VMEM] * chips,
        [(grads_shape, BF16)],
        [pltpu.VMEM((chips,) + grads_shape, BF16)],
    )(grads, *(grad_parts[k] for k in range(1, chips)))
    next_to, grads = lax.optimization_barrier((next_to, grads))

    col_keep, col_send = call(
        functools.partial(backward_kernel, rows, cols),
        [VMEM, SMEM, VMEM] + [VMEM] * 3,
        [((chips,) + piece, F32), ((chips,) + piece, BF16)],
        [pltpu.VMEM((cols,) + piece, BF16), pltpu.VMEM((rows,) + piece, F32)],
        flops=LONG,
    )(block_pos, block_count, turned, hidden, next_to, far)
    grad_parts = {k: to_col(grads, cols, k) for k in order}
    own_x, *send_x = call(
        merge_kernel, [VMEM] * 2, [(piece, F32)] + [(piece, BF16)] * (chips - 1)
    )(col_keep, to_core(col_send, rows))
    parts_x = [to_chip(send_x[k - 1], rows, k) for k in across]

    norm = float((owned * rows * cols) ** -0.5)
    mine, bias_sum = call(
        functools.partial(col_sum_kernel, norm),
        [VMEM] * cols,
        [((half, width), F32), ((1, width), F32)],
        [pltpu.VMEM((cols,) + grads_shape, BF16)],
    )(grads, *(grad_parts[k] for k in range(1, cols)))
    theirs = to_core(mine, rows)
    x_piece = call(owned_sum_kernel, [VMEM] * (1 + chips), [(piece, BF16)], flops=LONG)(
        inv, own_x, *parts_x
    )
    output, grad_x, grad_w, grad_b = call(
        finish_kernel,
        [VMEM] * 5,
        [(piece, BF16), (piece, BF16), ((width, width), F32), ((1, width), F32)],
        [pltpu.SemaphoreType.DMA((5,))],
        place=pl.BlockSpec(memory_space=pl.ANY),
    )(out_piece, x_piece, mine, theirs, bias_sum)
    return (output, grad_x, grad_w, grad_b.reshape(width))


def solution(mesh):
    placed = (
        P(("row", "col"), None),
        P(("row", "col")),
        P(),
        P(),
        P(("row", "col"), None),
        P("row", "col", None),
        P("row", "col", None, None),
        P("row", "col"),
    )
    return jax.shard_map(
        per_device,
        mesh=mesh,
        in_specs=placed,
        out_specs=(P(("row", "col"), None), P(("row", "col"), None), P(), P()),
        check_vma=False,
    )
```

```python
import functools

import jax
import jax.numpy as jnp
from jax import lax
from jax.experimental import pallas as pl
from jax.experimental.pallas import tpu as pltpu
from jax.sharding import PartitionSpec as P

BLOCK = 128
CORES = 2
EXTRA = 16
LONG = 4_000_000_000
GROUP = 8
VMEM = pl.BlockSpec(memory_space=pltpu.VMEM)
SMEM = pl.BlockSpec(memory_space=pltpu.SMEM)
NT = (((1,), (1,)), ((), ()))
TN = (((0,), (0,)), ((), ()))
BF16 = jnp.bfloat16
F32 = jnp.float32


def is_power(n):
    return n & (n - 1) == 0


def target(n, i, k):
    return i ^ k if is_power(n) else (i + k) % n


def offset_to(n, me, other):
    return me ^ other if is_power(n) else lax.rem(other - me + n, n)


def offset_from(n, me, other):
    return me ^ other if is_power(n) else lax.rem(me - other + n, n)


def to_core(x, rows):
    return lax.ppermute(x, "row", [(i, i ^ 1) for i in range(rows)])


def to_chip(x, rows, k):
    chips = rows // CORES
    pairs = [
        (a * CORES + b, target(chips, a, k) * CORES + b)
        for a in range(chips)
        for b in range(CORES)
    ]
    return lax.ppermute(x, "row", pairs)


def to_col(x, cols, k):
    return lax.ppermute(x, "col", [(i, target(cols, i, k)) for i in range(cols)])


def spread_inv(degree_ref, width):
    inv = lax.rsqrt(degree_ref[...].astype(F32))
    owned = inv.shape[1]
    tall = jnp.broadcast_to(inv, (BLOCK, owned)).T
    return jnp.concatenate([tall] * (width // BLOCK), axis=1)


def scale_kernel(features_hbm, degree_hbm, out_ref, inv_ref, features_ref, degree_ref, sems):
    copies = [
        pltpu.make_async_copy(degree_hbm, degree_ref, sems.at[0]),
        pltpu.make_async_copy(features_hbm, features_ref, sems.at[1]),
    ]
    for copy in copies:
        copy.start()
    copies[0].wait()
    inv = spread_inv(degree_ref, features_ref.shape[1])
    inv_ref[...] = inv
    copies[1].wait()
    out_ref[...] = (features_ref[...].astype(F32) * inv).astype(BF16)


def group_of(slots):
    return GROUP if slots % GROUP == 0 else 1


def for_live(count, slots, body):
    group = group_of(slots)
    for start in range(0, slots, group):

        @pl.when(start < count)
        def _():
            for slot in range(start, start + group):
                body(slot)


def build_kernel(count_ref, edge_ref, bias_ref, blocks_ref, turned_ref, bias_out_ref):
    bias_out_ref[...] = bias_ref[...]
    slots, edges = edge_ref.shape[2], edge_ref.shape[3]
    node = lax.broadcasted_iota(jnp.int32, (BLOCK, edges), 0)

    count = count_ref[0, 0]
    group = group_of(slots)

    def build(s):
        edge = edge_ref[0, 0, pl.ds(s, 1), :]
        row_hot = jnp.where(node == edge // BLOCK, 1.0, 0.0).astype(BF16)
        col_hot = jnp.where(node == edge % BLOCK, 1.0, 0.0).astype(BF16)
        counts = lax.dot_general(row_hot, col_hot, NT, preferred_element_type=F32)
        block = jnp.where(s < count, counts, 0.0).astype(BF16)
        blocks_ref[s] = block
        turned_ref[s] = block.T

    def step(i, carry):
        for j in range(group):
            build(i * group + j)
        return carry

    lax.fori_loop(0, (count + group - 1) // group, step, 0)


def forward_kernel(rows, cols, pos_ref, count_ref, blocks_ref, near_ref, next_ref, *refs):
    own_ref, *send, gathered, acc = refs
    chips = rows // CORES
    row, col = lax.axis_index("row"), lax.axis_index("col")
    gathered[:chips] = near_ref[...]
    gathered[chips:] = next_ref[...]
    acc[...] = jnp.zeros_like(acc)
    positions = pos_ref[0]

    def add(s):
        p = positions[0, s]
        u, v = p // rows, lax.rem(p, rows)
        k = offset_from(chips, row // CORES, v // CORES)
        src = (lax.rem(v, CORES) ^ lax.rem(row, CORES)) * chips + k
        dst = offset_to(cols, col, u)
        acc[dst] += jnp.dot(blocks_ref[s], gathered[src], preferred_element_type=F32)

    for_live(count_ref[0, 0], blocks_ref.shape[0], add)
    own_ref[...] = acc[0]
    for k, ref in enumerate(send, 1):
        ref[...] = acc[k].astype(BF16)


def pack_bias(total, rows):
    head = total.astype(BF16)
    tail = (total - head.astype(F32)).astype(BF16)
    index = lax.broadcasted_iota(jnp.int32, (rows, total.shape[1]), 0)
    both = jnp.where(index == 0, head.astype(F32), jnp.where(index == 1, tail.astype(F32), 0.0))
    return both.astype(BF16)


def add_bias(packed):
    return jnp.sum(packed.astype(F32), axis=0, keepdims=True)


def pointwise_kernel(cols, weight_ref, bias_ref, cot_ref, inv_ref, *refs):
    own_ref, *parts = refs[:cols]
    out_ref, hidden_ref, keep_ref, bias_keep_ref, send_ref = refs[cols:]
    width = out_ref.shape[1]
    half = width // CORES
    core = lax.rem(lax.axis_index("row"), CORES)
    inv = inv_ref[...]
    total = own_ref[...]
    for ref in parts:
        total = total + ref[...].astype(F32)
    agg = (total * inv).astype(BF16)
    weight = weight_ref[...]
    preact = jnp.dot(agg, weight, preferred_element_type=F32) + bias_ref[...]
    sig = jax.nn.sigmoid(preact)
    out_ref[...] = (preact * sig).astype(BF16)
    grad_pre = (cot_ref[...].astype(F32) * sig * (1.0 + preact * (1.0 - sig))).astype(BF16)
    hidden = lax.dot_general(grad_pre, weight, NT, preferred_element_type=F32)
    hidden_ref[...] = (hidden * inv).astype(BF16)
    term = lax.dot_general(agg, grad_pre, TN, preferred_element_type=F32)
    low, high = term[:half], term[half:]
    first = core == 0
    keep_ref[...] = jnp.where(first, low, high)
    send_ref[:half] = jnp.where(first, high, low).astype(BF16)
    bias_sum = jnp.sum(grad_pre.astype(F32), axis=0, keepdims=True)
    bias_keep_ref[...] = bias_sum
    send_ref[half:] = pack_bias(bias_sum, EXTRA)


def pair_sum_kernel(keep_ref, bias_keep_ref, got_ref, out_ref):
    half = keep_ref.shape[0]
    out_ref[:half] = (keep_ref[...] + got_ref[:half].astype(F32)).astype(BF16)
    out_ref[half:] = pack_bias(bias_keep_ref[...] + add_bias(got_ref[half:]), EXTRA)


def total_of(n, me, refs, stage):
    for k, ref in enumerate(refs):
        owner = me ^ k if is_power(n) else lax.rem(me - k + n, n)
        stage[owner] = ref[...]
    half = stage.shape[1] - EXTRA
    grads, bias = stage[0, :half].astype(F32), add_bias(stage[0, half:])
    for i in range(1, n):
        grads = grads + stage[i, :half].astype(F32)
        bias = bias + add_bias(stage[i, half:])
    return grads, bias


def chip_sum_kernel(*refs):
    *parts, out_ref, stage = refs
    chip = lax.axis_index("row") // CORES
    grads, bias = total_of(len(parts), chip, parts, stage)
    half = grads.shape[0]
    out_ref[:half] = grads.astype(BF16)
    out_ref[half:] = pack_bias(bias, EXTRA)


def col_sum_kernel(norm, *refs):
    *parts, half_ref, bias_ref, stage = refs
    grads, bias = total_of(len(parts), lax.axis_index("col"), parts, stage)
    half_ref[...] = grads * norm
    bias_ref[...] = bias * norm


def collect_kernel(*refs):
    *parts, out_ref = refs
    for n, ref in enumerate(parts):
        out_ref[n] = ref[...]


def backward_kernel(rows, cols, pos_ref, count_ref, turned_ref, *refs):
    parts = refs[:cols]
    keep_ref, send_ref, hidden, acc = refs[cols:]
    chips = rows // CORES
    row, col = lax.axis_index("row"), lax.axis_index("col")
    for k, ref in enumerate(parts):
        hidden[k] = ref[...]
    acc[...] = jnp.zeros_like(acc)
    positions = pos_ref[0]

    def add(s):
        p = positions[0, s]
        u, v = p // rows, lax.rem(p, rows)
        src = offset_from(cols, col, u)
        k = offset_to(chips, row // CORES, v // CORES)
        dst = (lax.rem(v, CORES) ^ lax.rem(row, CORES)) * chips + k
        acc[dst] += jnp.dot(turned_ref[s], hidden[src], preferred_element_type=F32)

    for_live(count_ref[0, 0], turned_ref.shape[0], add)
    keep_ref[...] = acc[:chips]
    send_ref[...] = acc[chips:].astype(BF16)


def merge_kernel(keep_ref, got_ref, own_ref, *send):
    own_ref[...] = keep_ref[0] + got_ref[0].astype(F32)
    for k, ref in enumerate(send, 1):
        ref[...] = (keep_ref[k] + got_ref[k].astype(F32)).astype(BF16)


def owned_sum_kernel(inv_ref, own_ref, *refs):
    *parts, out_ref = refs
    total = own_ref[...]
    for ref in parts:
        total = total + ref[...].astype(F32)
    out_ref[...] = (total * inv_ref[...]).astype(BF16)


def finish_kernel(out_ref, x_ref, mine_ref, theirs_ref, bias_ref, *refs):
    output_ref, grad_x_ref, grad_w_ref, grad_b_ref, sems = refs
    half = mine_ref.shape[0]
    core = lax.rem(lax.axis_index("row"), CORES)
    moves = [
        (mine_ref, grad_w_ref.at[pl.ds(pl.multiple_of(core * half, half), half)]),
        (theirs_ref, grad_w_ref.at[pl.ds(pl.multiple_of((1 - core) * half, half), half)]),
        (out_ref, output_ref),
        (x_ref, grad_x_ref),
        (bias_ref, grad_b_ref),
    ]
    copies = [pltpu.make_async_copy(*move, sems.at[i]) for i, move in enumerate(moves)]
    for copy in copies:
        copy.start()
    for copy in copies:
        copy.wait()


def call(kernel, specs, outs, scratch=(), flops=1_000_000, place=VMEM):
    shapes = [jax.ShapeDtypeStruct(shape, dtype) for shape, dtype in outs]
    single = len(shapes) == 1
    return pl.pallas_call(
        kernel,
        out_shape=shapes[0] if single else tuple(shapes),
        in_specs=specs,
        out_specs=place if single else tuple(place for _ in shapes),
        scratch_shapes=scratch,
        compiler_params=pltpu.CompilerParams(vmem_limit_bytes=40 * 1024 * 1024),
        cost_estimate=pl.CostEstimate(flops=flops, bytes_accessed=1_000_000, transcendentals=0),
    )


def per_device(features, degree, weight, bias_vector, cotangent, block_pos, edge_pos, block_count):
    owned, width = features.shape
    rows, cols = lax.axis_size("row"), lax.axis_size("col")
    chips = rows // CORES
    slots = block_pos.shape[2]
    half = width // CORES
    piece = (owned, width)
    grads_shape = (half + EXTRA, width)
    degree = degree.reshape(1, owned)
    bias_vector = bias_vector.reshape(1, width)

    features, degree = (
        pltpu.with_memory_space_constraint(x, pltpu.HBM) for x in (features, degree)
    )
    scaled, inv = call(
        scale_kernel,
        [pl.BlockSpec(memory_space=pltpu.HBM)] * 2,
        [(piece, BF16), (piece, F32)],
        [pltpu.VMEM(piece, BF16), pltpu.VMEM((1, owned), jnp.int32), pltpu.SemaphoreType.DMA((2,))],
    )(features, degree)
    near = [to_chip(scaled, rows, k) for k in range(1, chips)]
    blocks, turned, bias_vector = call(
        build_kernel,
        [SMEM, VMEM, VMEM],
        [((slots, BLOCK, BLOCK), BF16)] * 2 + [((1, width), F32)],
        flops=LONG,
    )(block_count, edge_pos, bias_vector)
    blocks, *near = lax.optimization_barrier((blocks, *near))
    near = call(collect_kernel, [VMEM] * chips, [((chips,) + piece, BF16)])(scaled, *near)

    own, *send = call(
        functools.partial(forward_kernel, rows, cols),
        [VMEM, SMEM, VMEM, VMEM, VMEM],
        [(piece, F32)] + [(piece, BF16)] * (cols - 1),
        [pltpu.VMEM((rows,) + piece, BF16), pltpu.VMEM((cols,) + piece, F32)],
    )(block_pos, block_count, blocks, near, to_core(near, rows))
    order = list(range(2, cols)) + [1]
    parts = [to_col(send[k - 1], cols, k) for k in order]

    out_piece, hidden, keep, bias_keep, half_send = call(
        functools.partial(pointwise_kernel, cols),
        [VMEM] * (4 + cols),
        [(piece, BF16), (piece, BF16), ((half, width), F32), ((1, width), F32), (grads_shape, BF16)],
    )(weight, bias_vector, cotangent, inv, own, *parts)

    hidden_parts = {k: to_col(hidden, cols, k) for k in order}
    grads = call(pair_sum_kernel, [VMEM] * 3, [(grads_shape, BF16)])(
        keep, bias_keep, to_core(half_send, rows)
    )
    across = range(chips - 1, 0, -1)
    grad_parts = {k: to_chip(grads, rows, k) for k in across}
    grads = call(
        chip_sum_kernel,
        [VMEM] * chips,
        [(grads_shape, BF16)],
        [pltpu.VMEM((chips,) + grads_shape, BF16)],
    )(grads, *(grad_parts[k] for k in range(1, chips)))

    col_keep, col_send = call(
        functools.partial(backward_kernel, rows, cols),
        [VMEM, SMEM, VMEM] + [VMEM] * cols,
        [((chips,) + piece, F32), ((chips,) + piece, BF16)],
        [pltpu.VMEM((cols,) + piece, BF16), pltpu.VMEM((rows,) + piece, F32)],
        flops=LONG,
    )(block_pos, block_count, turned, hidden, *(hidden_parts[k] for k in range(1, cols)))
    col_send, grads = lax.optimization_barrier((col_send, grads))
    grad_parts = {k: to_col(grads, cols, k) for k in order}
    own_x, *send_x = call(
        merge_kernel, [VMEM] * 2, [(piece, F32)] + [(piece, BF16)] * (chips - 1)
    )(col_keep, to_core(col_send, rows))
    parts_x = [to_chip(send_x[k - 1], rows, k) for k in across]

    norm = float((owned * rows * cols) ** -0.5)
    mine, bias_sum = call(
        functools.partial(col_sum_kernel, norm),
        [VMEM] * cols,
        [((half, width), F32), ((1, width), F32)],
        [pltpu.VMEM((cols,) + grads_shape, BF16)],
    )(grads, *(grad_parts[k] for k in range(1, cols)))
    theirs = to_core(mine, rows)
    x_piece = call(owned_sum_kernel, [VMEM] * (1 + chips), [(piece, BF16)], flops=LONG)(
        inv, own_x, *parts_x
    )
    output, grad_x, grad_w, grad_b = call(
        finish_kernel,
        [VMEM] * 5,
        [(piece, BF16), (piece, BF16), ((width, width), F32), ((1, width), F32)],
        [pltpu.SemaphoreType.DMA((5,))],
        place=pl.BlockSpec(memory_space=pl.ANY),
    )(out_piece, x_piece, mine, theirs, bias_sum)
    return (output, grad_x, grad_w, grad_b.reshape(width))


def solution(mesh):
    placed = (
        P(("row", "col"), None),
        P(("row", "col")),
        P(),
        P(),
        P(("row", "col"), None),
        P("row", "col", None),
        P("row", "col", None, None),
        P("row", "col"),
    )
    return jax.shard_map(
        per_device,
        mesh=mesh,
        in_specs=placed,
        out_specs=(P(("row", "col"), None), P(("row", "col"), None), P(), P()),
        check_vma=False,
    )
```

```python
import functools

import jax
import jax.numpy as jnp
from jax import lax
from jax.experimental import pallas as pl
from jax.experimental.pallas import tpu as pltpu
from jax.sharding import PartitionSpec as P

BLOCK = 128
CORES = 2
EXTRA = 16
LONG = 4_000_000_000
SHORT = 1_000_000_000
GROUP = 8
VMEM = pl.BlockSpec(memory_space=pltpu.VMEM)
SMEM = pl.BlockSpec(memory_space=pltpu.SMEM)
NT = (((1,), (1,)), ((), ()))
TN = (((0,), (0,)), ((), ()))
BF16 = jnp.bfloat16
F32 = jnp.float32


def is_power(n):
    return n & (n - 1) == 0


def target(n, i, k):
    return i ^ k if is_power(n) else (i + k) % n


def offset_to(n, me, other):
    return me ^ other if is_power(n) else lax.rem(other - me + n, n)


def offset_from(n, me, other):
    return me ^ other if is_power(n) else lax.rem(me - other + n, n)


def to_core(x, rows):
    return lax.ppermute(x, "row", [(i, i ^ 1) for i in range(rows)])


def to_chip(x, rows, k):
    chips = rows // CORES
    pairs = [
        (a * CORES + b, target(chips, a, k) * CORES + b)
        for a in range(chips)
        for b in range(CORES)
    ]
    return lax.ppermute(x, "row", pairs)


def to_col(x, cols, k):
    return lax.ppermute(x, "col", [(i, target(cols, i, k)) for i in range(cols)])


def spread_inv(degree_ref, width):
    inv = lax.rsqrt(degree_ref[...].astype(F32))
    owned = inv.shape[1]
    tall = jnp.broadcast_to(inv, (BLOCK, owned)).T
    return jnp.concatenate([tall] * (width // BLOCK), axis=1)


def scale_kernel(features_hbm, degree_hbm, out_ref, inv_ref, features_ref, degree_ref, sems):
    copies = [
        pltpu.make_async_copy(degree_hbm, degree_ref, sems.at[0]),
        pltpu.make_async_copy(features_hbm, features_ref, sems.at[1]),
    ]
    for copy in copies:
        copy.start()
    copies[0].wait()
    inv = spread_inv(degree_ref, features_ref.shape[1])
    inv_ref[...] = inv
    copies[1].wait()
    out_ref[...] = (features_ref[...].astype(F32) * inv).astype(BF16)


def group_of(slots):
    return GROUP if slots % GROUP == 0 else 1


def for_live(count, slots, body):
    group = group_of(slots)
    for start in range(0, slots, group):

        @pl.when(start < count)
        def _():
            for slot in range(start, start + group):
                body(slot)


def build_kernel(count_ref, edge_ref, bias_ref, blocks_ref, turned_ref, bias_out_ref):
    bias_out_ref[...] = bias_ref[...]
    slots, edges = edge_ref.shape[2], edge_ref.shape[3]
    node = lax.broadcasted_iota(jnp.int32, (BLOCK, edges), 0)

    count = count_ref[0, 0]
    group = group_of(slots)

    def build(s):
        edge = edge_ref[0, 0, pl.ds(s, 1), :]
        row_hot = jnp.where(node == edge // BLOCK, 1.0, 0.0).astype(BF16)
        col_hot = jnp.where(node == edge % BLOCK, 1.0, 0.0).astype(BF16)
        counts = lax.dot_general(row_hot, col_hot, NT, preferred_element_type=F32)
        block = jnp.where(s < count, counts, 0.0).astype(BF16)
        blocks_ref[s] = block
        turned_ref[s] = block.T

    def step(i, carry):
        for j in range(group):
            build(i * group + j)
        return carry

    lax.fori_loop(0, (count + group - 1) // group, step, 0)


def forward_kernel(rows, cols, pos_ref, count_ref, blocks_ref, near_ref, next_ref, *refs):
    own_ref, *send, gathered, acc = refs
    chips = rows // CORES
    row, col = lax.axis_index("row"), lax.axis_index("col")
    gathered[:chips] = near_ref[...]
    gathered[chips:] = next_ref[...]
    acc[...] = jnp.zeros_like(acc)
    positions = pos_ref[0]

    def add(s):
        p = positions[0, s]
        u, v = p // rows, lax.rem(p, rows)
        k = offset_from(chips, row // CORES, v // CORES)
        src = (lax.rem(v, CORES) ^ lax.rem(row, CORES)) * chips + k
        dst = offset_to(cols, col, u)
        acc[dst] += jnp.dot(blocks_ref[s], gathered[src], preferred_element_type=F32)

    for_live(count_ref[0, 0], blocks_ref.shape[0], add)
    own_ref[...] = acc[0]
    for k, ref in enumerate(send, 1):
        ref[...] = acc[k].astype(BF16)


def pack_bias(total, rows):
    head = total.astype(BF16)
    tail = (total - head.astype(F32)).astype(BF16)
    index = lax.broadcasted_iota(jnp.int32, (rows, total.shape[1]), 0)
    both = jnp.where(index == 0, head.astype(F32), jnp.where(index == 1, tail.astype(F32), 0.0))
    return both.astype(BF16)


def add_bias(packed):
    return jnp.sum(packed.astype(F32), axis=0, keepdims=True)


def pointwise_kernel(cols, weight_ref, bias_ref, cot_ref, inv_ref, *refs):
    own_ref, *parts = refs[:cols]
    out_ref, hidden_ref, keep_ref, send_ref = refs[cols:]
    owned = out_ref.shape[0]
    width = out_ref.shape[1]
    half = width // CORES
    core = lax.rem(lax.axis_index("row"), CORES)
    inv = inv_ref[...]
    total = own_ref[...]
    for ref in parts:
        total = total + ref[...].astype(F32)
    agg = (total * inv).astype(BF16)
    weight = weight_ref[...]
    preact = jnp.dot(agg, weight, preferred_element_type=F32) + bias_ref[...]
    sig = jax.nn.sigmoid(preact)
    out_ref[...] = (preact * sig).astype(BF16)
    grad_pre = (cot_ref[...].astype(F32) * sig * (1.0 + preact * (1.0 - sig))).astype(BF16)
    hidden = lax.dot_general(grad_pre, weight, NT, preferred_element_type=F32)
    hidden_ref[:owned] = (hidden * inv).astype(BF16)
    term = lax.dot_general(agg, grad_pre, TN, preferred_element_type=F32)
    low, high = term[:half], term[half:]
    first = core == 0
    keep_ref[...] = jnp.where(first, low, high)
    send_ref[...] = jnp.where(first, high, low).astype(BF16)
    bias_sum = jnp.sum(grad_pre.astype(F32), axis=0, keepdims=True)
    hidden_ref[owned:] = pack_bias(bias_sum, EXTRA)


def pair_sum_kernel(keep_ref, got_ref, out_ref):
    out_ref[...] = (keep_ref[...] + got_ref[...].astype(F32)).astype(BF16)


def owner_of(n, me, k):
    return me ^ k if is_power(n) else lax.rem(me - k + n, n)


def total_of(n, me, pieces, stage):
    for k, piece in enumerate(pieces):
        stage[owner_of(n, me, k)] = piece
    total = stage[0].astype(F32)
    for i in range(1, n):
        total = total + stage[i].astype(F32)
    return total


def chip_sum_kernel(*refs):
    *parts, out_ref, stage = refs
    chip = lax.axis_index("row") // CORES
    out_ref[...] = total_of(len(parts), chip, [ref[...] for ref in parts], stage).astype(BF16)


def col_sum_kernel(norm, *refs):
    *parts, half_ref, stage = refs
    total = total_of(len(parts), lax.axis_index("col"), [ref[...] for ref in parts], stage)
    half_ref[...] = total * norm


def collect_kernel(*refs):
    *parts, out_ref = refs
    for n, ref in enumerate(parts):
        out_ref[n] = ref[...]


def backward_kernel(rows, cols, pos_ref, count_ref, turned_ref, *refs):
    parts = refs[:cols]
    keep_ref, bias_ref, send_ref, hidden, acc, stage = refs[cols:]
    owned = acc.shape[1]
    chips = rows // CORES
    row, col = lax.axis_index("row"), lax.axis_index("col")
    for k, ref in enumerate(parts):
        hidden[k] = ref[:owned]
    acc[...] = jnp.zeros_like(acc)
    positions = pos_ref[0]

    def add(s):
        p = positions[0, s]
        u, v = p // rows, lax.rem(p, rows)
        src = offset_from(cols, col, u)
        k = offset_to(chips, row // CORES, v // CORES)
        dst = (lax.rem(v, CORES) ^ lax.rem(row, CORES)) * chips + k
        acc[dst] += jnp.dot(turned_ref[s], hidden[src], preferred_element_type=F32)

    for_live(count_ref[0, 0], turned_ref.shape[0], add)
    keep_ref[...] = acc[:chips]
    for k in range(chips):
        send_ref[k * owned : (k + 1) * owned] = acc[chips + k].astype(BF16)
    bias = total_of(cols, col, [ref[owned:] for ref in parts], stage)
    packed = pack_bias(jnp.sum(bias, axis=0, keepdims=True), EXTRA)
    bias_ref[...] = packed
    send_ref[chips * owned :] = packed


def merge_kernel(keep_ref, bias_ref, got_ref, own_ref, pair_ref, *send):
    chips, owned = keep_ref.shape[:2]
    packed = pack_bias(add_bias(bias_ref[...]) + add_bias(got_ref[chips * owned :]), EXTRA)
    pair_ref[...] = packed
    own_ref[...] = keep_ref[0] + got_ref[:owned].astype(F32)
    for k, ref in enumerate(send, 1):
        part = got_ref[k * owned : (k + 1) * owned].astype(F32)
        ref[:owned] = (keep_ref[k] + part).astype(BF16)
        ref[owned:] = packed


def owned_sum_kernel(norm, offsets, inv_ref, own_ref, pair_ref, *refs):
    *parts, out_ref, grad_b_ref, stage = refs
    owned = own_ref.shape[0]
    chips = len(parts) + 1
    total = own_ref[...]
    biases = {0: pair_ref[...]}
    for k, ref in zip(offsets, parts):
        total = total + ref[:owned].astype(F32)
        biases[k] = ref[owned:]
    out_ref[...] = (total * inv_ref[...]).astype(BF16)
    chip = lax.axis_index("row") // CORES
    bias = total_of(chips, chip, [biases[k] for k in range(chips)], stage)
    grad_b_ref[...] = jnp.sum(bias, axis=0, keepdims=True) * norm


def finish_kernel(out_ref, x_ref, mine_ref, theirs_ref, bias_ref, *refs):
    output_ref, grad_x_ref, grad_w_ref, grad_b_ref, sems = refs
    half = mine_ref.shape[0]
    core = lax.rem(lax.axis_index("row"), CORES)
    moves = [
        (mine_ref, grad_w_ref.at[pl.ds(pl.multiple_of(core * half, half), half)]),
        (theirs_ref, grad_w_ref.at[pl.ds(pl.multiple_of((1 - core) * half, half), half)]),
        (out_ref, output_ref),
        (x_ref, grad_x_ref),
        (bias_ref, grad_b_ref),
    ]
    copies = [pltpu.make_async_copy(*move, sems.at[i]) for i, move in enumerate(moves)]
    for copy in copies:
        copy.start()
    for copy in copies:
        copy.wait()


def call(kernel, specs, outs, scratch=(), flops=1_000_000, place=VMEM):
    shapes = [jax.ShapeDtypeStruct(shape, dtype) for shape, dtype in outs]
    single = len(shapes) == 1
    return pl.pallas_call(
        kernel,
        out_shape=shapes[0] if single else tuple(shapes),
        in_specs=specs,
        out_specs=place if single else tuple(place for _ in shapes),
        scratch_shapes=scratch,
        compiler_params=pltpu.CompilerParams(vmem_limit_bytes=40 * 1024 * 1024),
        cost_estimate=pl.CostEstimate(flops=flops, bytes_accessed=1_000_000, transcendentals=0),
    )


def per_device(features, degree, weight, bias_vector, cotangent, block_pos, edge_pos, block_count):
    owned, width = features.shape
    rows, cols = lax.axis_size("row"), lax.axis_size("col")
    chips = rows // CORES
    slots = block_pos.shape[2]
    half = width // CORES
    piece = (owned, width)
    grads_shape = (half, width)
    bias_shape = (EXTRA, width)
    norm = float((owned * rows * cols) ** -0.5)
    degree = degree.reshape(1, owned)
    bias_vector = bias_vector.reshape(1, width)

    features, degree = (
        pltpu.with_memory_space_constraint(x, pltpu.HBM) for x in (features, degree)
    )
    scaled, inv = call(
        scale_kernel,
        [pl.BlockSpec(memory_space=pltpu.HBM)] * 2,
        [(piece, BF16), (piece, F32)],
        [pltpu.VMEM(piece, BF16), pltpu.VMEM((1, owned), jnp.int32), pltpu.SemaphoreType.DMA((2,))],
    )(features, degree)
    near = [to_chip(scaled, rows, k) for k in range(1, chips)]
    blocks, turned, bias_vector = call(
        build_kernel,
        [SMEM, VMEM, VMEM],
        [((slots, BLOCK, BLOCK), BF16)] * 2 + [((1, width), F32)],
        flops=LONG,
    )(block_count, edge_pos, bias_vector)
    blocks, *near = lax.optimization_barrier((blocks, *near))
    near = call(collect_kernel, [VMEM] * chips, [((chips,) + piece, BF16)])(scaled, *near)

    own, *send = call(
        functools.partial(forward_kernel, rows, cols),
        [VMEM, SMEM, VMEM, VMEM, VMEM],
        [(piece, F32)] + [(piece, BF16)] * (cols - 1),
        [pltpu.VMEM((rows,) + piece, BF16), pltpu.VMEM((cols,) + piece, F32)],
    )(block_pos, block_count, blocks, near, to_core(near, rows))
    order = list(range(2, cols)) + [1]
    parts = [to_col(send[k - 1], cols, k) for k in order]

    out_piece, hidden, keep, half_send = call(
        functools.partial(pointwise_kernel, cols),
        [VMEM] * (4 + cols),
        [(piece, BF16), ((owned + EXTRA, width), BF16), (grads_shape, F32), (grads_shape, BF16)],
    )(weight, bias_vector, cotangent, inv, own, *parts)
    hidden_parts = {k: to_col(hidden, cols, k) for k in order}
    grads = call(pair_sum_kernel, [VMEM] * 2, [(grads_shape, BF16)])(
        keep, to_core(half_send, rows)
    )
    across = range(chips - 1, 0, -1)
    grad_parts = {k: to_chip(grads, rows, k) for k in across}
    grads = call(
        chip_sum_kernel,
        [VMEM] * chips,
        [(grads_shape, BF16)],
        [pltpu.VMEM((chips,) + grads_shape, BF16)],
    )(grads, *(grad_parts[k] for k in range(1, chips)))

    col_keep, bias, col_send = call(
        functools.partial(backward_kernel, rows, cols),
        [VMEM, SMEM, VMEM] + [VMEM] * cols,
        [((chips,) + piece, F32), (bias_shape, BF16), ((chips * owned + EXTRA, width), BF16)],
        [
            pltpu.VMEM((cols,) + piece, BF16),
            pltpu.VMEM((rows,) + piece, F32),
            pltpu.VMEM((cols,) + bias_shape, BF16),
        ],
        flops=LONG,
    )(block_pos, block_count, turned, hidden, *(hidden_parts[k] for k in range(1, cols)))
    col_send, grads = lax.optimization_barrier((col_send, grads))
    grad_parts = {k: to_col(grads, cols, k) for k in order}
    own_x, bias, *send_x = call(
        merge_kernel,
        [VMEM] * 3,
        [(piece, F32), (bias_shape, BF16)] + [((owned + EXTRA, width), BF16)] * (chips - 1),
    )(col_keep, bias, to_core(col_send, rows))
    parts_x = [to_chip(send_x[k - 1], rows, k) for k in across]

    mine = call(
        functools.partial(col_sum_kernel, norm),
        [VMEM] * cols,
        [(grads_shape, F32)],
        [pltpu.VMEM((cols,) + grads_shape, BF16)],
    )(grads, *(grad_parts[k] for k in range(1, cols)))
    theirs = to_core(mine, rows)
    x_piece, bias_sum = call(
        functools.partial(owned_sum_kernel, norm, list(across)),
        [VMEM] * (2 + chips),
        [(piece, BF16), ((1, width), F32)],
        [pltpu.VMEM((chips,) + bias_shape, BF16)],
        flops=SHORT,
    )(inv, own_x, bias, *parts_x)
    output, grad_x, grad_w, grad_b = call(
        finish_kernel,
        [VMEM] * 5,
        [(piece, BF16), (piece, BF16), ((width, width), F32), ((1, width), F32)],
        [pltpu.SemaphoreType.DMA((5,))],
        place=pl.BlockSpec(memory_space=pl.ANY),
    )(out_piece, x_piece, mine, theirs, bias_sum)
    return (output, grad_x, grad_w, grad_b.reshape(width))


def solution(mesh):
    placed = (
        P(("row", "col"), None),
        P(("row", "col")),
        P(),
        P(),
        P(("row", "col"), None),
        P("row", "col", None),
        P("row", "col", None, None),
        P("row", "col"),
    )
    return jax.shard_map(
        per_device,
        mesh=mesh,
        in_specs=placed,
        out_specs=(P(("row", "col"), None), P(("row", "col"), None), P(), P()),
        check_vma=False,
    )
```

```python
import functools

import jax
import jax.numpy as jnp
from jax import lax
from jax.experimental import pallas as pl
from jax.experimental.pallas import tpu as pltpu
from jax.sharding import PartitionSpec as P

BLOCK = 128
CORES = 2
EXTRA = 16
LONG = 4_000_000_000
SHORT = 1_000_000_000
GROUP = 8
VMEM = pl.BlockSpec(memory_space=pltpu.VMEM)
SMEM = pl.BlockSpec(memory_space=pltpu.SMEM)
NT = (((1,), (1,)), ((), ()))
TN = (((0,), (0,)), ((), ()))
BF16 = jnp.bfloat16
F32 = jnp.float32


def is_power(n):
    return n & (n - 1) == 0


def target(n, i, k):
    return i ^ k if is_power(n) else (i + k) % n


def offset_to(n, me, other):
    return me ^ other if is_power(n) else lax.rem(other - me + n, n)


def offset_from(n, me, other):
    return me ^ other if is_power(n) else lax.rem(me - other + n, n)


def to_core(x, rows):
    return lax.ppermute(x, "row", [(i, i ^ 1) for i in range(rows)])


def to_chip(x, rows, k):
    chips = rows // CORES
    pairs = [
        (a * CORES + b, target(chips, a, k) * CORES + b)
        for a in range(chips)
        for b in range(CORES)
    ]
    return lax.ppermute(x, "row", pairs)


def to_col(x, cols, k):
    return lax.ppermute(x, "col", [(i, target(cols, i, k)) for i in range(cols)])


def spread_inv(degree_ref, width):
    inv = lax.rsqrt(degree_ref[...].astype(F32))
    owned = inv.shape[1]
    tall = jnp.broadcast_to(inv, (BLOCK, owned)).T
    return jnp.concatenate([tall] * (width // BLOCK), axis=1)


def scale_kernel(features_hbm, degree_hbm, out_ref, inv_ref, features_ref, degree_ref, sems):
    copies = [
        pltpu.make_async_copy(degree_hbm, degree_ref, sems.at[0]),
        pltpu.make_async_copy(features_hbm, features_ref, sems.at[1]),
    ]
    for copy in copies:
        copy.start()
    copies[0].wait()
    inv = spread_inv(degree_ref, features_ref.shape[1])
    inv_ref[...] = inv
    copies[1].wait()
    out_ref[...] = (features_ref[...].astype(F32) * inv).astype(BF16)


def group_of(slots):
    return GROUP if slots % GROUP == 0 else 1


def for_live(count, slots, body):
    group = group_of(slots)
    for start in range(0, slots, group):

        @pl.when(start < count)
        def _():
            for slot in range(start, start + group):
                body(slot)


def build_kernel(count_ref, edge_ref, bias_ref, blocks_ref, turned_ref, bias_out_ref):
    bias_out_ref[...] = bias_ref[...]
    slots, edges = edge_ref.shape[2], edge_ref.shape[3]
    node = lax.broadcasted_iota(jnp.int32, (BLOCK, edges), 0)

    count = count_ref[0, 0]
    group = group_of(slots)

    def build(s):
        edge = edge_ref[0, 0, pl.ds(s, 1), :]
        row_hot = jnp.where(node == edge // BLOCK, 1.0, 0.0).astype(BF16)
        col_hot = jnp.where(node == edge % BLOCK, 1.0, 0.0).astype(BF16)
        counts = lax.dot_general(row_hot, col_hot, NT, preferred_element_type=F32)
        block = jnp.where(s < count, counts, 0.0).astype(BF16)
        blocks_ref[s] = block
        turned_ref[s] = block.T

    def step(i, carry):
        for j in range(group):
            build(i * group + j)
        return carry

    lax.fori_loop(0, (count + group - 1) // group, step, 0)


def forward_kernel(rows, cols, pos_ref, count_ref, blocks_ref, near_ref, next_ref, *refs):
    own_ref, *send, gathered, acc = refs
    chips = rows // CORES
    row, col = lax.axis_index("row"), lax.axis_index("col")
    gathered[:chips] = near_ref[...]
    gathered[chips:] = next_ref[...]
    acc[...] = jnp.zeros_like(acc)
    positions = pos_ref[0]

    def add(s):
        p = positions[0, s]
        u, v = p // rows, lax.rem(p, rows)
        k = offset_from(chips, row // CORES, v // CORES)
        src = (lax.rem(v, CORES) ^ lax.rem(row, CORES)) * chips + k
        dst = offset_to(cols, col, u)
        acc[dst] += jnp.dot(blocks_ref[s], gathered[src], preferred_element_type=F32)

    for_live(count_ref[0, 0], blocks_ref.shape[0], add)
    own_ref[...] = acc[0]
    for k, ref in enumerate(send, 1):
        ref[...] = acc[k].astype(BF16)


def pack_bias(total, rows):
    head = total.astype(BF16)
    tail = (total - head.astype(F32)).astype(BF16)
    index = lax.broadcasted_iota(jnp.int32, (rows, total.shape[1]), 0)
    both = jnp.where(index == 0, head.astype(F32), jnp.where(index == 1, tail.astype(F32), 0.0))
    return both.astype(BF16)


def add_bias(packed):
    return jnp.sum(packed.astype(F32), axis=0, keepdims=True)


def pointwise_kernel(cols, weight_ref, bias_ref, cot_ref, inv_ref, *refs):
    own_ref, *parts = refs[:cols]
    out_ref, hidden_ref, keep_ref, send_ref = refs[cols:]
    owned = out_ref.shape[0]
    width = out_ref.shape[1]
    half = width // CORES
    core = lax.rem(lax.axis_index("row"), CORES)
    inv = inv_ref[...]
    total = own_ref[...]
    for ref in parts:
        total = total + ref[...].astype(F32)
    agg = (total * inv).astype(BF16)
    weight = weight_ref[...]
    preact = jnp.dot(agg, weight, preferred_element_type=F32) + bias_ref[...]
    sig = jax.nn.sigmoid(preact)
    out_ref[...] = (preact * sig).astype(BF16)
    grad_pre = (cot_ref[...].astype(F32) * sig * (1.0 + preact * (1.0 - sig))).astype(BF16)
    hidden = lax.dot_general(grad_pre, weight, NT, preferred_element_type=F32)
    hidden_ref[:owned] = (hidden * inv).astype(BF16)
    term = lax.dot_general(agg, grad_pre, TN, preferred_element_type=F32)
    low, high = term[:half], term[half:]
    first = core == 0
    keep_ref[...] = jnp.where(first, low, high)
    send_ref[...] = jnp.where(first, high, low).astype(BF16)
    bias_sum = jnp.sum(grad_pre.astype(F32), axis=0, keepdims=True)
    hidden_ref[owned:] = pack_bias(bias_sum, EXTRA)


def pair_sum_kernel(keep_ref, got_ref, out_ref):
    out_ref[...] = (keep_ref[...] + got_ref[...].astype(F32)).astype(BF16)


def owner_of(n, me, k):
    return me ^ k if is_power(n) else lax.rem(me - k + n, n)


def total_of(n, me, pieces, stage):
    for k, piece in enumerate(pieces):
        stage[owner_of(n, me, k)] = piece
    total = stage[0].astype(F32)
    for i in range(1, n):
        total = total + stage[i].astype(F32)
    return total


def chip_sum_kernel(*refs):
    *parts, out_ref, stage = refs
    chip = lax.axis_index("row") // CORES
    out_ref[...] = total_of(len(parts), chip, [ref[...] for ref in parts], stage).astype(BF16)


def col_sum_kernel(norm, *refs):
    *parts, half_ref, stage = refs
    total = total_of(len(parts), lax.axis_index("col"), [ref[...] for ref in parts], stage)
    half_ref[...] = total * norm


def collect_kernel(*refs):
    *parts, out_ref = refs
    for n, ref in enumerate(parts):
        out_ref[n] = ref[...]


def backward_kernel(rows, cols, pos_ref, count_ref, turned_ref, *refs):
    parts = refs[:cols]
    keep_ref, bias_ref, send_ref, hidden, acc, stage = refs[cols:]
    owned = acc.shape[1]
    chips = rows // CORES
    row, col = lax.axis_index("row"), lax.axis_index("col")
    for k, ref in enumerate(parts):
        hidden[k] = ref[:owned]
    acc[...] = jnp.zeros_like(acc)
    positions = pos_ref[0]

    def add(s):
        p = positions[0, s]
        u, v = p // rows, lax.rem(p, rows)
        src = offset_from(cols, col, u)
        k = offset_to(chips, row // CORES, v // CORES)
        dst = (lax.rem(v, CORES) ^ lax.rem(row, CORES)) * chips + k
        acc[dst] += jnp.dot(turned_ref[s], hidden[src], preferred_element_type=F32)

    for_live(count_ref[0, 0], turned_ref.shape[0], add)
    keep_ref[...] = acc[:chips]
    for k in range(chips):
        send_ref[k * owned : (k + 1) * owned] = acc[chips + k].astype(BF16)
    bias = total_of(cols, col, [ref[owned:] for ref in parts], stage)
    packed = pack_bias(jnp.sum(bias, axis=0, keepdims=True), EXTRA)
    bias_ref[...] = packed
    send_ref[chips * owned :] = packed


def merge_kernel(keep_ref, bias_ref, got_ref, own_ref, pair_ref, *send):
    chips, owned = keep_ref.shape[:2]
    packed = pack_bias(add_bias(bias_ref[...]) + add_bias(got_ref[chips * owned :]), EXTRA)
    pair_ref[...] = packed
    own_ref[...] = keep_ref[0] + got_ref[:owned].astype(F32)
    for k, ref in enumerate(send, 1):
        part = got_ref[k * owned : (k + 1) * owned].astype(F32)
        ref[:owned] = (keep_ref[k] + part).astype(BF16)
        ref[owned:] = packed


def owned_sum_kernel(norm, offsets, inv_ref, own_ref, pair_ref, *refs):
    *parts, out_ref, grad_b_ref, stage = refs
    owned = own_ref.shape[0]
    chips = len(parts) + 1
    total = own_ref[...]
    biases = {0: pair_ref[...]}
    for k, ref in zip(offsets, parts):
        total = total + ref[:owned].astype(F32)
        biases[k] = ref[owned:]
    out_ref[...] = (total * inv_ref[...]).astype(BF16)
    chip = lax.axis_index("row") // CORES
    bias = total_of(chips, chip, [biases[k] for k in range(chips)], stage)
    grad_b_ref[...] = jnp.sum(bias, axis=0, keepdims=True) * norm


def finish_kernel(out_ref, x_ref, mine_ref, theirs_ref, bias_ref, *refs):
    output_ref, grad_x_ref, grad_w_ref, grad_b_ref, sems = refs
    half = mine_ref.shape[0]
    core = lax.rem(lax.axis_index("row"), CORES)
    moves = [
        (mine_ref, grad_w_ref.at[pl.ds(pl.multiple_of(core * half, half), half)]),
        (theirs_ref, grad_w_ref.at[pl.ds(pl.multiple_of((1 - core) * half, half), half)]),
        (out_ref, output_ref),
        (x_ref, grad_x_ref),
        (bias_ref, grad_b_ref),
    ]
    copies = [pltpu.make_async_copy(*move, sems.at[i]) for i, move in enumerate(moves)]
    for copy in copies:
        copy.start()
    for copy in copies:
        copy.wait()


def call(kernel, specs, outs, scratch=(), flops=1_000_000, place=VMEM):
    shapes = [jax.ShapeDtypeStruct(shape, dtype) for shape, dtype in outs]
    single = len(shapes) == 1
    return pl.pallas_call(
        kernel,
        out_shape=shapes[0] if single else tuple(shapes),
        in_specs=specs,
        out_specs=place if single else tuple(place for _ in shapes),
        scratch_shapes=scratch,
        compiler_params=pltpu.CompilerParams(vmem_limit_bytes=40 * 1024 * 1024),
        cost_estimate=pl.CostEstimate(flops=flops, bytes_accessed=1_000_000, transcendentals=0),
    )


def per_device(features, degree, weight, bias_vector, cotangent, block_pos, edge_pos, block_count):
    owned, width = features.shape
    rows, cols = lax.axis_size("row"), lax.axis_size("col")
    chips = rows // CORES
    slots = block_pos.shape[2]
    half = width // CORES
    piece = (owned, width)
    grads_shape = (half, width)
    bias_shape = (EXTRA, width)
    norm = float((owned * rows * cols) ** -0.5)
    degree = degree.reshape(1, owned)
    bias_vector = bias_vector.reshape(1, width)

    features, degree = (
        pltpu.with_memory_space_constraint(x, pltpu.HBM) for x in (features, degree)
    )
    scaled, inv = call(
        scale_kernel,
        [pl.BlockSpec(memory_space=pltpu.HBM)] * 2,
        [(piece, BF16), (piece, F32)],
        [pltpu.VMEM(piece, BF16), pltpu.VMEM((1, owned), jnp.int32), pltpu.SemaphoreType.DMA((2,))],
    )(features, degree)
    near = [to_chip(scaled, rows, k) for k in range(1, chips)]
    blocks, turned, bias_vector = call(
        build_kernel,
        [SMEM, VMEM, VMEM],
        [((slots, BLOCK, BLOCK), BF16)] * 2 + [((1, width), F32)],
        flops=LONG,
    )(block_count, edge_pos, bias_vector)
    blocks, *near = lax.optimization_barrier((blocks, *near))
    near = call(collect_kernel, [VMEM] * chips, [((chips,) + piece, BF16)])(scaled, *near)

    own, *send = call(
        functools.partial(forward_kernel, rows, cols),
        [VMEM, SMEM, VMEM, VMEM, VMEM],
        [(piece, F32)] + [(piece, BF16)] * (cols - 1),
        [pltpu.VMEM((rows,) + piece, BF16), pltpu.VMEM((cols,) + piece, F32)],
    )(block_pos, block_count, blocks, near, to_core(near, rows))
    order = list(range(2, cols)) + [1]
    parts = [to_col(send[k - 1], cols, k) for k in order]

    out_piece, hidden, keep, half_send = call(
        functools.partial(pointwise_kernel, cols),
        [VMEM] * (4 + cols),
        [(piece, BF16), ((owned + EXTRA, width), BF16), (grads_shape, F32), (grads_shape, BF16)],
    )(weight, bias_vector, cotangent, inv, own, *parts)
    hidden_parts = {k: to_col(hidden, cols, k) for k in order}
    grads = call(pair_sum_kernel, [VMEM] * 2, [(grads_shape, BF16)], flops=LONG)(
        keep, to_core(half_send, rows)
    )
    across = range(chips - 1, 0, -1)
    grad_parts = {k: to_chip(grads, rows, k) for k in across}
    grads = call(
        chip_sum_kernel,
        [VMEM] * chips,
        [(grads_shape, BF16)],
        [pltpu.VMEM((chips,) + grads_shape, BF16)],
    )(grads, *(grad_parts[k] for k in range(1, chips)))

    col_keep, bias, col_send = call(
        functools.partial(backward_kernel, rows, cols),
        [VMEM, SMEM, VMEM] + [VMEM] * cols,
        [((chips,) + piece, F32), (bias_shape, BF16), ((chips * owned + EXTRA, width), BF16)],
        [
            pltpu.VMEM((cols,) + piece, BF16),
            pltpu.VMEM((rows,) + piece, F32),
            pltpu.VMEM((cols,) + bias_shape, BF16),
        ],
        flops=LONG,
    )(block_pos, block_count, turned, hidden, *(hidden_parts[k] for k in range(1, cols)))
    col_send, grads = lax.optimization_barrier((col_send, grads))
    grad_parts = {k: to_col(grads, cols, k) for k in order}
    own_x, bias, *send_x = call(
        merge_kernel,
        [VMEM] * 3,
        [(piece, F32), (bias_shape, BF16)] + [((owned + EXTRA, width), BF16)] * (chips - 1),
    )(col_keep, bias, to_core(col_send, rows))
    parts_x = [to_chip(send_x[k - 1], rows, k) for k in across]

    mine = call(
        functools.partial(col_sum_kernel, norm),
        [VMEM] * cols,
        [(grads_shape, F32)],
        [pltpu.VMEM((cols,) + grads_shape, BF16)],
    )(grads, *(grad_parts[k] for k in range(1, cols)))
    theirs = to_core(mine, rows)
    x_piece, bias_sum = call(
        functools.partial(owned_sum_kernel, norm, list(across)),
        [VMEM] * (2 + chips),
        [(piece, BF16), ((1, width), F32)],
        [pltpu.VMEM((chips,) + bias_shape, BF16)],
        flops=SHORT,
    )(inv, own_x, bias, *parts_x)
    output, grad_x, grad_w, grad_b = call(
        finish_kernel,
        [VMEM] * 5,
        [(piece, BF16), (piece, BF16), ((width, width), F32), ((1, width), F32)],
        [pltpu.SemaphoreType.DMA((5,))],
        place=pl.BlockSpec(memory_space=pl.ANY),
    )(out_piece, x_piece, mine, theirs, bias_sum)
    return (output, grad_x, grad_w, grad_b.reshape(width))


def solution(mesh):
    placed = (
        P(("row", "col"), None),
        P(("row", "col")),
        P(),
        P(),
        P(("row", "col"), None),
        P("row", "col", None),
        P("row", "col", None, None),
        P("row", "col"),
    )
    return jax.shard_map(
        per_device,
        mesh=mesh,
        in_specs=placed,
        out_specs=(P(("row", "col"), None), P(("row", "col"), None), P(), P()),
        check_vma=False,
    )
```

```python
import functools

import jax
import jax.numpy as jnp
from jax import lax
from jax.experimental import pallas as pl
from jax.experimental.pallas import tpu as pltpu
from jax.sharding import PartitionSpec as P

BLOCK = 128
CORES = 2
EXTRA = 16
LONG = 4_000_000_000
SHORT = 1_000_000_000
GROUP = 8
VMEM = pl.BlockSpec(memory_space=pltpu.VMEM)
SMEM = pl.BlockSpec(memory_space=pltpu.SMEM)
NT = (((1,), (1,)), ((), ()))
TN = (((0,), (0,)), ((), ()))
BF16 = jnp.bfloat16
F32 = jnp.float32


def is_power(n):
    return n & (n - 1) == 0


def target(n, i, k):
    return i ^ k if is_power(n) else (i + k) % n


def offset_to(n, me, other):
    return me ^ other if is_power(n) else lax.rem(other - me + n, n)


def offset_from(n, me, other):
    return me ^ other if is_power(n) else lax.rem(me - other + n, n)


def to_core(x, rows):
    return lax.ppermute(x, "row", [(i, i ^ 1) for i in range(rows)])


def to_chip(x, rows, k):
    chips = rows // CORES
    pairs = [
        (a * CORES + b, target(chips, a, k) * CORES + b)
        for a in range(chips)
        for b in range(CORES)
    ]
    return lax.ppermute(x, "row", pairs)


def to_col(x, cols, k):
    return lax.ppermute(x, "col", [(i, target(cols, i, k)) for i in range(cols)])


def spread_inv(degree_ref, width):
    inv = lax.rsqrt(degree_ref[...].astype(F32))
    owned = inv.shape[1]
    tall = jnp.broadcast_to(inv, (BLOCK, owned)).T
    return jnp.concatenate([tall] * (width // BLOCK), axis=1)


def scale_kernel(features_hbm, degree_hbm, out_ref, inv_ref, features_ref, degree_ref, sems):
    copies = [
        pltpu.make_async_copy(degree_hbm, degree_ref, sems.at[0]),
        pltpu.make_async_copy(features_hbm, features_ref, sems.at[1]),
    ]
    for copy in copies:
        copy.start()
    copies[0].wait()
    inv = spread_inv(degree_ref, features_ref.shape[1])
    inv_ref[...] = inv
    copies[1].wait()
    out_ref[...] = (features_ref[...].astype(F32) * inv).astype(BF16)


def group_of(slots):
    return GROUP if slots % GROUP == 0 else 1


def for_live(count, slots, body):
    group = group_of(slots)
    for start in range(0, slots, group):

        @pl.when(start < count)
        def _():
            for slot in range(start, start + group):
                body(slot)


def build_kernel(count_ref, edge_ref, bias_ref, blocks_ref, turned_ref, bias_out_ref):
    bias_out_ref[...] = bias_ref[...]
    slots, edges = edge_ref.shape[2], edge_ref.shape[3]
    node = lax.broadcasted_iota(jnp.int32, (BLOCK, edges), 0)

    count = count_ref[0, 0]
    group = group_of(slots)

    def build(s):
        edge = edge_ref[0, 0, pl.ds(s, 1), :]
        row_hot = jnp.where(node == edge // BLOCK, 1.0, 0.0).astype(BF16)
        col_hot = jnp.where(node == edge % BLOCK, 1.0, 0.0).astype(BF16)
        counts = lax.dot_general(row_hot, col_hot, NT, preferred_element_type=F32)
        block = jnp.where(s < count, counts, 0.0).astype(BF16)
        blocks_ref[s] = block
        turned_ref[s] = block.T

    def step(i, carry):
        for j in range(group):
            build(i * group + j)
        return carry

    lax.fori_loop(0, (count + group - 1) // group, step, 0)


def forward_kernel(rows, cols, pos_ref, count_ref, blocks_ref, near_ref, next_ref, *refs):
    own_ref, *send, gathered, acc = refs
    chips = rows // CORES
    row, col = lax.axis_index("row"), lax.axis_index("col")
    gathered[:chips] = near_ref[...]
    gathered[chips:] = next_ref[...]
    acc[...] = jnp.zeros_like(acc)
    positions = pos_ref[0]

    def add(s):
        p = positions[0, s]
        u, v = p // rows, lax.rem(p, rows)
        k = offset_from(chips, row // CORES, v // CORES)
        src = (lax.rem(v, CORES) ^ lax.rem(row, CORES)) * chips + k
        dst = offset_to(cols, col, u)
        acc[dst] += jnp.dot(blocks_ref[s], gathered[src], preferred_element_type=F32)

    for_live(count_ref[0, 0], blocks_ref.shape[0], add)
    own_ref[...] = acc[0]
    for k, ref in enumerate(send, 1):
        ref[...] = acc[k].astype(BF16)


def pack_bias(total, rows):
    head = total.astype(BF16)
    tail = (total - head.astype(F32)).astype(BF16)
    index = lax.broadcasted_iota(jnp.int32, (rows, total.shape[1]), 0)
    both = jnp.where(index == 0, head.astype(F32), jnp.where(index == 1, tail.astype(F32), 0.0))
    return both.astype(BF16)


def add_bias(packed):
    return jnp.sum(packed.astype(F32), axis=0, keepdims=True)


def pointwise_kernel(cols, weight_ref, bias_ref, cot_ref, inv_ref, *refs):
    own_ref, *parts = refs[:cols]
    out_ref, hidden_ref, keep_ref, send_ref = refs[cols:]
    owned = out_ref.shape[0]
    width = out_ref.shape[1]
    half = width // CORES
    core = lax.rem(lax.axis_index("row"), CORES)
    inv = inv_ref[...]
    total = own_ref[...]
    for ref in parts:
        total = total + ref[...].astype(F32)
    agg = (total * inv).astype(BF16)
    weight = weight_ref[...]
    preact = jnp.dot(agg, weight, preferred_element_type=F32) + bias_ref[...]
    sig = jax.nn.sigmoid(preact)
    out_ref[...] = (preact * sig).astype(BF16)
    grad_pre = (cot_ref[...].astype(F32) * sig * (1.0 + preact * (1.0 - sig))).astype(BF16)
    hidden = lax.dot_general(grad_pre, weight, NT, preferred_element_type=F32)
    hidden_ref[:owned] = (hidden * inv).astype(BF16)
    term = lax.dot_general(agg, grad_pre, TN, preferred_element_type=F32)
    low, high = term[:half], term[half:]
    first = core == 0
    keep_ref[...] = jnp.where(first, low, high)
    send_ref[...] = jnp.where(first, high, low).astype(BF16)
    bias_sum = jnp.sum(grad_pre.astype(F32), axis=0, keepdims=True)
    hidden_ref[owned:] = pack_bias(bias_sum, EXTRA)


def pair_sum_kernel(keep_ref, got_ref, out_ref):
    out_ref[...] = (keep_ref[...] + got_ref[...].astype(F32)).astype(BF16)


def owner_of(n, me, k):
    return me ^ k if is_power(n) else lax.rem(me - k + n, n)


def total_of(n, me, pieces, stage):
    for k, piece in enumerate(pieces):
        stage[owner_of(n, me, k)] = piece
    total = stage[0].astype(F32)
    for i in range(1, n):
        total = total + stage[i].astype(F32)
    return total


def chip_sum_kernel(*refs):
    *parts, out_ref, stage = refs
    chip = lax.axis_index("row") // CORES
    out_ref[...] = total_of(len(parts), chip, [ref[...] for ref in parts], stage).astype(BF16)


def col_sum_kernel(norm, *refs):
    *parts, half_ref, stage = refs
    cols = len(parts)
    by_offset = dict(zip([0] + list(range(2, cols)) + [1], parts))
    pieces = [by_offset[k][...] for k in range(cols)]
    total = total_of(cols, lax.axis_index("col"), pieces, stage)
    half_ref[...] = total * norm


def collect_kernel(*refs):
    *parts, out_ref = refs
    for n, ref in enumerate(parts):
        out_ref[n] = ref[...]


def backward_kernel(rows, cols, pos_ref, count_ref, turned_ref, *refs):
    parts = refs[:cols]
    keep_ref, bias_ref, send_ref, hidden, acc, stage = refs[cols:]
    owned = acc.shape[1]
    chips = rows // CORES
    row, col = lax.axis_index("row"), lax.axis_index("col")
    for k, ref in enumerate(parts):
        hidden[k] = ref[:owned]
    acc[...] = jnp.zeros_like(acc)
    positions = pos_ref[0]

    def add(s):
        p = positions[0, s]
        u, v = p // rows, lax.rem(p, rows)
        src = offset_from(cols, col, u)
        k = offset_to(chips, row // CORES, v // CORES)
        dst = (lax.rem(v, CORES) ^ lax.rem(row, CORES)) * chips + k
        acc[dst] += jnp.dot(turned_ref[s], hidden[src], preferred_element_type=F32)

    for_live(count_ref[0, 0], turned_ref.shape[0], add)
    keep_ref[...] = acc[:chips]
    for k in range(chips):
        send_ref[k * owned : (k + 1) * owned] = acc[chips + k].astype(BF16)
    bias = total_of(cols, col, [ref[owned:] for ref in parts], stage)
    packed = pack_bias(jnp.sum(bias, axis=0, keepdims=True), EXTRA)
    bias_ref[...] = packed
    send_ref[chips * owned :] = packed


def merge_kernel(keep_ref, bias_ref, got_ref, own_ref, pair_ref, *send):
    chips, owned = keep_ref.shape[:2]
    packed = pack_bias(add_bias(bias_ref[...]) + add_bias(got_ref[chips * owned :]), EXTRA)
    pair_ref[...] = packed
    own_ref[...] = keep_ref[0] + got_ref[:owned].astype(F32)
    for k, ref in enumerate(send, 1):
        part = got_ref[k * owned : (k + 1) * owned].astype(F32)
        ref[:owned] = (keep_ref[k] + part).astype(BF16)
        ref[owned:] = packed


def owned_sum_kernel(norm, offsets, inv_ref, own_ref, pair_ref, *refs):
    *parts, out_ref, grad_b_ref, stage = refs
    owned = own_ref.shape[0]
    chips = len(parts) + 1
    total = own_ref[...]
    biases = {0: pair_ref[...]}
    for k, ref in zip(offsets, parts):
        total = total + ref[:owned].astype(F32)
        biases[k] = ref[owned:]
    out_ref[...] = (total * inv_ref[...]).astype(BF16)
    chip = lax.axis_index("row") // CORES
    bias = total_of(chips, chip, [biases[k] for k in range(chips)], stage)
    grad_b_ref[...] = jnp.sum(bias, axis=0, keepdims=True) * norm


def finish_kernel(out_ref, x_ref, mine_ref, theirs_ref, bias_ref, *refs):
    output_ref, grad_x_ref, grad_w_ref, grad_b_ref, sems = refs
    half = mine_ref.shape[0]
    core = lax.rem(lax.axis_index("row"), CORES)
    moves = [
        (mine_ref, grad_w_ref.at[pl.ds(pl.multiple_of(core * half, half), half)]),
        (theirs_ref, grad_w_ref.at[pl.ds(pl.multiple_of((1 - core) * half, half), half)]),
        (out_ref, output_ref),
        (x_ref, grad_x_ref),
        (bias_ref, grad_b_ref),
    ]
    copies = [pltpu.make_async_copy(*move, sems.at[i]) for i, move in enumerate(moves)]
    for copy in copies:
        copy.start()
    for copy in copies:
        copy.wait()


def call(kernel, specs, outs, scratch=(), flops=1_000_000, place=VMEM):
    shapes = [jax.ShapeDtypeStruct(shape, dtype) for shape, dtype in outs]
    single = len(shapes) == 1
    return pl.pallas_call(
        kernel,
        out_shape=shapes[0] if single else tuple(shapes),
        in_specs=specs,
        out_specs=place if single else tuple(place for _ in shapes),
        scratch_shapes=scratch,
        compiler_params=pltpu.CompilerParams(vmem_limit_bytes=40 * 1024 * 1024),
        cost_estimate=pl.CostEstimate(flops=flops, bytes_accessed=1_000_000, transcendentals=0),
    )


def per_device(features, degree, weight, bias_vector, cotangent, block_pos, edge_pos, block_count):
    owned, width = features.shape
    rows, cols = lax.axis_size("row"), lax.axis_size("col")
    chips = rows // CORES
    slots = block_pos.shape[2]
    half = width // CORES
    piece = (owned, width)
    grads_shape = (half, width)
    bias_shape = (EXTRA, width)
    norm = float((owned * rows * cols) ** -0.5)
    degree = degree.reshape(1, owned)
    bias_vector = bias_vector.reshape(1, width)

    features, degree = (
        pltpu.with_memory_space_constraint(x, pltpu.HBM) for x in (features, degree)
    )
    scaled, inv = call(
        scale_kernel,
        [pl.BlockSpec(memory_space=pltpu.HBM)] * 2,
        [(piece, BF16), (piece, F32)],
        [pltpu.VMEM(piece, BF16), pltpu.VMEM((1, owned), jnp.int32), pltpu.SemaphoreType.DMA((2,))],
    )(features, degree)
    near = [to_chip(scaled, rows, k) for k in range(1, chips)]
    blocks, turned, bias_vector = call(
        build_kernel,
        [SMEM, VMEM, VMEM],
        [((slots, BLOCK, BLOCK), BF16)] * 2 + [((1, width), F32)],
        flops=LONG,
    )(block_count, edge_pos, bias_vector)
    blocks, *near = lax.optimization_barrier((blocks, *near))
    near = call(collect_kernel, [VMEM] * chips, [((chips,) + piece, BF16)])(scaled, *near)

    own, *send = call(
        functools.partial(forward_kernel, rows, cols),
        [VMEM, SMEM, VMEM, VMEM, VMEM],
        [(piece, F32)] + [(piece, BF16)] * (cols - 1),
        [pltpu.VMEM((rows,) + piece, BF16), pltpu.VMEM((cols,) + piece, F32)],
    )(block_pos, block_count, blocks, near, to_core(near, rows))
    order = list(range(2, cols)) + [1]
    parts = [to_col(send[k - 1], cols, k) for k in order]

    out_piece, hidden, keep, half_send = call(
        functools.partial(pointwise_kernel, cols),
        [VMEM] * (4 + cols),
        [(piece, BF16), ((owned + EXTRA, width), BF16), (grads_shape, F32), (grads_shape, BF16)],
    )(weight, bias_vector, cotangent, inv, own, *parts)
    hidden_parts = {k: to_col(hidden, cols, k) for k in order}
    grads = call(pair_sum_kernel, [VMEM] * 2, [(grads_shape, BF16)], flops=LONG)(
        keep, to_core(half_send, rows)
    )
    across = range(chips - 1, 0, -1)
    grad_parts = {k: to_chip(grads, rows, k) for k in across}
    grads = call(
        chip_sum_kernel,
        [VMEM] * chips,
        [(grads_shape, BF16)],
        [pltpu.VMEM((chips,) + grads_shape, BF16)],
    )(grads, *(grad_parts[k] for k in range(1, chips)))

    col_keep, bias, col_send = call(
        functools.partial(backward_kernel, rows, cols),
        [VMEM, SMEM, VMEM] + [VMEM] * cols,
        [((chips,) + piece, F32), (bias_shape, BF16), ((chips * owned + EXTRA, width), BF16)],
        [
            pltpu.VMEM((cols,) + piece, BF16),
            pltpu.VMEM((rows,) + piece, F32),
            pltpu.VMEM((cols,) + bias_shape, BF16),
        ],
        flops=LONG,
    )(block_pos, block_count, turned, hidden, *(hidden_parts[k] for k in range(1, cols)))
    col_send, grads = lax.optimization_barrier((col_send, grads))
    grad_parts = {k: to_col(grads, cols, k) for k in order}
    own_x, bias, *send_x = call(
        merge_kernel,
        [VMEM] * 3,
        [(piece, F32), (bias_shape, BF16)] + [((owned + EXTRA, width), BF16)] * (chips - 1),
    )(col_keep, bias, to_core(col_send, rows))
    parts_x = [to_chip(send_x[k - 1], rows, k) for k in across]

    mine = call(
        functools.partial(col_sum_kernel, norm),
        [VMEM] * cols,
        [(grads_shape, F32)],
        [pltpu.VMEM((cols,) + grads_shape, BF16)],
    )(grads, *(grad_parts[k] for k in order))
    theirs = to_core(mine, rows)
    x_piece, bias_sum = call(
        functools.partial(owned_sum_kernel, norm, list(across)),
        [VMEM] * (2 + chips),
        [(piece, BF16), ((1, width), F32)],
        [pltpu.VMEM((chips,) + bias_shape, BF16)],
        flops=SHORT,
    )(inv, own_x, bias, *parts_x)
    output, grad_x, grad_w, grad_b = call(
        finish_kernel,
        [VMEM] * 5,
        [(piece, BF16), (piece, BF16), ((width, width), F32), ((1, width), F32)],
        [pltpu.SemaphoreType.DMA((5,))],
        place=pl.BlockSpec(memory_space=pl.ANY),
    )(out_piece, x_piece, mine, theirs, bias_sum)
    return (output, grad_x, grad_w, grad_b.reshape(width))


def solution(mesh):
    placed = (
        P(("row", "col"), None),
        P(("row", "col")),
        P(),
        P(),
        P(("row", "col"), None),
        P("row", "col", None),
        P("row", "col", None, None),
        P("row", "col"),
    )
    return jax.shard_map(
        per_device,
        mesh=mesh,
        in_specs=placed,
        out_specs=(P(("row", "col"), None), P(("row", "col"), None), P(), P()),
        check_vma=False,
    )
```
